512 devices in a mesh: lat: 16 (over x, z_lo), lon: 32 (over z_hi, y, core).
Axes of the slice: x: 4, y: 8, z: 8 (z_hi: 2, z_lo: 4; z = z_hi * 4 + z_lo), core: 2. Of those that a mesh axis runs over, the one named last changes fastest.
Arguments:
- frame_one: bfloat16 [256, 1024, 256], P('lat', 'lon'), may hold values from -6 to 6
- frame_two: bfloat16 [256, 1024, 256], P('lat', 'lon'), may hold values from -6 to 6
- enc_weight: bfloat16 [3, 3, 256, 256], replicated, may hold values from -0.125 to 0.125
- mask_weight: bfloat16 [256, 576], replicated, may hold values from -0.375 to 0.375
Outputs:
- up_flow: float32 [2, 2048, 8192], P(None, 'lat', 'lon')
The draws below stay inside these ranges and needn't reach their ends.
All inputs are finite; a program needn't handle non-finite values.
Results may differ from the reference program's by a relative error of at most 0.0011.
Values may be sent and summed in bfloat16 or wider, within the bound.
No kernel may reach another device: no remote copies, remote signals or barrier semaphores. Data moves between devices by JAX's collectives and lax.ppermute only.
A program may use at most 64 MiB of HBM per device.

```python
import math
import jax
import jax.numpy as jnp
from jax import lax

CHANNELS = 256
BLOCK_ROWS = 8
BLOCK_COLS = 16
UPSCALE = 8
MASK_COLS = 576
GRID_ROWS = 256
GRID_COLS = 1024


def level_of(rng, extent, cuts, low, largest):
    def one(axis_at, blocks):
        draws = jax.random.uniform(jax.random.fold_in(jax.random.fold_in(rng, 6), axis_at), (blocks,), jnp.float32, low / len(cuts), largest / len(cuts))
        return jnp.repeat(jnp.exp(draws), extent[axis_at] // blocks).reshape((-1,) + (1,) * (len(extent) - axis_at - 1))

    gain = one(*cuts[0])
    for cut in cuts[1:]:
        gain = gain * one(*cut)
    return gain


def scatter_about(own_key, extent, scale, reach, split=(), kind=jnp.bfloat16):
    result = jax.random.normal(own_key, extent, jnp.float32) * scale
    if len(split) > 0:
        result = level_of(own_key, extent, split, -0.22, 0.18) * result
    return jnp.clip(result, min=-reach, max=reach).astype(kind)


def setup_inputs(seed: int = 0) -> dict:
    streams_of = jax.random.split(jax.random.key(seed), 5)
    frame_one = scatter_about(streams_of[0], (GRID_ROWS, GRID_COLS, CHANNELS), 1.0, 6.0, ((0, 16), (1, 32)))
    frame_two = scatter_about(streams_of[1], (GRID_ROWS, GRID_COLS, CHANNELS), 1.0, 6.0, ((0, 16), (1, 32)))
    enc_weight = scatter_about(streams_of[2], (3, 3, CHANNELS, CHANNELS), (9 * CHANNELS) ** -0.5, 0.125)
    mask_weight = scatter_about(streams_of[3], (CHANNELS, MASK_COLS), CHANNELS ** -0.5, 0.375)
    return dict(frame_one=frame_one, frame_two=frame_two, enc_weight=enc_weight, mask_weight=mask_weight)


def encode_grid(source, weight):
    padded = jnp.pad(source, ((1, 1), (0, 0), (0, 0)))
    summed = jnp.zeros((GRID_ROWS, GRID_COLS, CHANNELS), jnp.float32)
    for row_off in range(3):
        for col_off in range(3):
            moved = jnp.roll(padded[row_off:row_off + GRID_ROWS], 1 - col_off, axis=1)
            summed = summed + jnp.dot(moved.reshape(GRID_ROWS * GRID_COLS, CHANNELS), weight[row_off, col_off], preferred_element_type=jnp.float32).reshape(GRID_ROWS, GRID_COLS, CHANNELS)
    return summed.astype(jnp.bfloat16)

def reference(frame_one, frame_two, enc_weight, mask_weight):
    enc_one = encode_grid(frame_one, enc_weight)
    enc_two = encode_grid(frame_two, enc_weight)
    padded_two = jnp.pad(enc_two, ((BLOCK_ROWS, BLOCK_ROWS), (0, 0), (0, 0)))
    block_size = BLOCK_ROWS * BLOCK_COLS
    column_blocks = GRID_COLS // BLOCK_COLS
    row_blocks = GRID_ROWS // BLOCK_ROWS
    key_row = (jnp.arange(block_size) // BLOCK_COLS).astype(jnp.float32)
    key_col = (jnp.arange(block_size) % BLOCK_COLS).astype(jnp.float32)
    scale = 1.0 / math.sqrt(CHANNELS)

    def block_row(index):
        query = lax.dynamic_slice_in_dim(enc_one, index * BLOCK_ROWS, BLOCK_ROWS, 0)
        query = query.reshape(BLOCK_ROWS, column_blocks, BLOCK_COLS, CHANNELS).transpose(1, 0, 2, 3)
        query = query.reshape(column_blocks, block_size, CHANNELS).astype(jnp.float32)
        window = lax.dynamic_slice_in_dim(padded_two, index * BLOCK_ROWS, 3 * BLOCK_ROWS, 0)
        window = window.reshape(3, BLOCK_ROWS, column_blocks, BLOCK_COLS, CHANNELS).transpose(0, 2, 1, 3, 4)
        window = window.reshape(3, column_blocks, block_size, CHANNELS).astype(jnp.float32)
        mass = jnp.zeros((column_blocks, block_size), jnp.float32)
        sum_y = jnp.zeros((column_blocks, block_size), jnp.float32)
        sum_x = jnp.zeros((column_blocks, block_size), jnp.float32)
        for row_off in range(3):
            target = index + row_off - 1
            inside = ((target >= 0) & (target < row_blocks)).astype(jnp.float32)
            for col_off in range(3):
                keyed = jnp.roll(window[row_off], 1 - col_off, axis=0)
                scores = jnp.einsum('jqc,jkc->jqk', query, keyed) * scale
                expo = jnp.exp(scores) * inside
                part = lax.optimization_barrier(jnp.sum(expo, axis=-1))
                mass = mass + part
                sum_y = sum_y + lax.optimization_barrier(jnp.sum(expo * key_row, axis=-1)) + BLOCK_ROWS * (row_off - 1) * part
                sum_x = sum_x + lax.optimization_barrier(jnp.sum(expo * key_col, axis=-1)) + BLOCK_COLS * (col_off - 1) * part
        flow_y = sum_y / mass - key_row
        flow_x = sum_x / mass - key_col
        stacked = jnp.stack([flow_y, flow_x]).reshape(2, column_blocks, BLOCK_ROWS, BLOCK_COLS)
        return stacked.transpose(0, 2, 1, 3).reshape(2, BLOCK_ROWS, GRID_COLS)
    rows_out = lax.map(block_row, jnp.arange(row_blocks, dtype=jnp.int32))
    flow = rows_out.transpose(1, 0, 2, 3).reshape(2, GRID_ROWS, GRID_COLS)
    logits = jnp.dot(enc_one.reshape(GRID_ROWS * GRID_COLS, CHANNELS), mask_weight, preferred_element_type=jnp.float32)
    logits = logits.reshape(GRID_ROWS, GRID_COLS, 9, UPSCALE * UPSCALE)
    expo = jnp.exp(logits)
    mix = expo / lax.optimization_barrier(jnp.sum(expo, axis=2, keepdims=True))
    padded_flow = jnp.pad(flow, ((0, 0), (1, 1), (0, 0)))
    upsampled = jnp.zeros((2, GRID_ROWS, GRID_COLS, UPSCALE * UPSCALE), jnp.float32)
    for row_off in range(3):
        for col_off in range(3):
            beside = jnp.roll(padded_flow[:, row_off:row_off + GRID_ROWS], 1 - col_off, axis=2) * UPSCALE
            upsampled = upsampled + mix[None, :, :, 3 * row_off + col_off, :] * beside[..., None]
    upsampled = upsampled.reshape(2, GRID_ROWS, GRID_COLS, UPSCALE, UPSCALE).transpose(0, 1, 3, 2, 4)
    return upsampled.reshape(2, GRID_ROWS * UPSCALE, GRID_COLS * UPSCALE)
```

```python
import functools
import math

import jax
import jax.numpy as jnp
from jax import lax
from jax.experimental import pallas as pl
from jax.experimental.pallas import tpu as pltpu
from jax.sharding import PartitionSpec as P

CH = 256
BR = 8
BC = 16
UP = 8
F32 = jnp.float32
BF16 = jnp.bfloat16
VMEM = pl.BlockSpec(memory_space=pltpu.VMEM)


def params(mib):
    return pltpu.CompilerParams(vmem_limit_bytes=mib * 1024 * 1024)


def pair_perm(size, first, wrap):
    out = []
    for i in range(first, size, 2):
        j = i + 1
        if j >= size:
            if not wrap:
                continue
            j -= size
        out += [(i, j), (j, i)]
    return out


def pack_kernel(rows, cols, f1, f2, ra, rb, m_in, m_x, ext, col):
    lat_odd = lax.axis_index("lat") % 2 == 1
    lon_odd = lax.axis_index("lon") % 2 == 1

    def halo(north, south):
        ext[0 : BR + 1] = north[0 : BR + 1]
        ext[BR + 1 : BR + 1 + rows] = f2[...]
        ext[BR + 1 + rows : 2 * BR + 2 + rows] = south[0 : BR + 1]
        ext[2 * BR + 2 + rows] = north[BR + 1]
        ext[2 * BR + 3 + rows : 2 * BR + 3 + 2 * rows] = f1[...]
        ext[2 * BR + 3 + 2 * rows] = south[BR + 1]

    @pl.when(lat_odd)
    def _():
        halo(rb, ra)

    @pl.when(jnp.logical_not(lat_odd))
    def _():
        halo(ra, rb)

    n2 = rows + 2 * BR + 2
    n1 = rows + 2
    slots2 = -(-n2 // BC)
    slots1 = -(-n1 // BC)

    def edge(msg, main, extra, one):
        msg[0:n2] = ext[0:n2, main : main + BC]
        lo = extra // BC * BC
        slab = ext[0:n2, lo : lo + BC].astype(F32)
        col[0:n2] = slab[:, extra - lo, :]
        msg[n2 : n2 + slots2] = col[0 : slots2 * BC].astype(BF16).reshape(slots2, BC, CH)
        lo = one // BC * BC
        slab = ext[n2 : n2 + n1, lo : lo + BC].astype(F32)
        col[0:n1] = slab[:, one - lo, :]
        msg[n2 + slots2 :] = col[0 : slots1 * BC].astype(BF16).reshape(slots1, BC, CH)

    def right(msg):
        edge(msg, cols - BC, cols - BC - 1, cols - 1)

    def left(msg):
        edge(msg, 0, BC, 0)

    @pl.when(lon_odd)
    def _():
        right(m_x)
        left(m_in)

    @pl.when(jnp.logical_not(lon_odd))
    def _():
        left(m_x)
        right(m_in)


def flow_kernel(rows, cols, f1, f2, ra, rb, c_in, c_x, w, flow, enc_one, s2, s1, x2, x1, e2):
    lat = lax.axis_index("lat")
    lat_odd = lat % 2 == 1
    lon_odd = lax.axis_index("lon") % 2 == 1
    n2 = rows + 2 * BR + 2
    n1 = rows + 2
    wide = cols + 2 * BC
    slots2 = -(-n2 // BC)
    slots1 = -(-n1 // BC)
    own = BR + BC

    def put_rows(north, south):
        s2[0 : BR + 1, own : own + cols] = north[0 : BR + 1].astype(F32)
        s2[BR + 1 + rows :, own : own + cols] = south[0 : BR + 1].astype(F32)
        s1[0, BR : BR + cols] = north[BR + 1].astype(F32)
        s1[n1 - 1, BR : BR + cols] = south[BR + 1].astype(F32)

    def put_cols(left, right):
        s2[:, BR : BR + BC] = left[0:n2].astype(F32)
        s2[:, own + cols : own + cols + BC] = right[0:n2].astype(F32)
        extra = left[n2 : n2 + slots2].astype(F32).reshape(slots2 * BC, CH)
        s2[:, BR - 1 : BR] = extra[0:n2][:, None, :]
        extra = right[n2 : n2 + slots2].astype(F32).reshape(slots2 * BC, CH)
        s2[:, BR + wide : BR + wide + 1] = extra[0:n2][:, None, :]
        one = left[n2 + slots2 :].astype(F32).reshape(slots1 * BC, CH)
        s1[:, BR - 1 : BR] = one[0:n1][:, None, :]
        one = right[n2 + slots2 :].astype(F32).reshape(slots1 * BC, CH)
        s1[:, BR + cols : BR + cols + 1] = one[0:n1][:, None, :]

    s2[BR + 1 : BR + 1 + rows, own : own + cols] = f2[...].astype(F32)
    s1[1 : 1 + rows, BR : BR + cols] = f1[...].astype(F32)

    @pl.when(lat_odd)
    def _():
        put_rows(rb, ra)

    @pl.when(jnp.logical_not(lat_odd))
    def _():
        put_rows(ra, rb)

    @pl.when(lon_odd)
    def _():
        put_cols(c_in, c_x)

    @pl.when(jnp.logical_not(lon_odd))
    def _():
        put_cols(c_x, c_in)

    for b in range(3):
        x2[b] = s2[:, BR - 1 + b : BR - 1 + b + wide].astype(BF16)
        x1[b] = s1[:, BR - 1 + b : BR - 1 + b + cols].astype(BF16)

    def conv(x, row, count, width):
        lhs = jnp.concatenate(
            [
                x[b, pl.ds(row + a, count)].reshape(count * width, CH)
                for a in range(3)
                for b in range(3)
            ],
            axis=1,
        )
        return jnp.dot(lhs, w[...], preferred_element_type=F32)

    half = BR // 2
    for g in range(rows // BR):
        enc_one[g * BR : g * BR + BR] = (
            conv(x1, g * BR, BR, cols).astype(BF16).reshape(BR, cols, CH)
        )
    for g in range((rows + 2 * BR) // half):
        e2[g * half : g * half + half] = (
            conv(x2, g * half, half, wide).astype(BF16).reshape(half, wide, CH)
        )

    bands = rows // BR
    queries = BR * cols
    lane = lax.broadcasted_iota(jnp.int32, (BR, queries), 1)
    sub = lax.broadcasted_iota(jnp.int32, (BR, queries), 0).astype(F32)
    q_col = lane % cols
    on_left = q_col < BC
    lefts = jnp.broadcast_to(on_left[None], (2, BR, queries))
    last = lax.axis_size("lat") - 1
    for g in range(bands):
        query = (enc_one[g * BR : g * BR + BR].reshape(queries, CH).astype(F32) * (1.0 / math.sqrt(CH))).astype(BF16)
        sums = [jnp.zeros((BR, queries), F32) for _ in range(6)]
        sum_y = jnp.zeros((BR, queries), F32)
        for kb in range(3):
            part = [jnp.zeros((BR, queries), F32) for _ in range(6)]
            part_y = jnp.zeros((BR, queries), F32)
            for kr in range(BR):
                keys = e2[(g + kb) * BR + kr]
                score = lax.dot_general(
                    keys, query, (((1,), (1,)), ((), ())), preferred_element_type=F32
                ).reshape(wide // BR, BR, queries)
                mid = jnp.exp(score[2:6])
                rim = jnp.exp(jnp.where(lefts, score[0:2], score[6:8]))
                pieces = [mid[0], mid[1], mid[2], mid[3], rim[0], rim[1]]
                total = (pieces[0] + pieces[1]) + (pieces[2] + pieces[3]) + (pieces[4] + pieces[5])
                part = [p + e for p, e in zip(part, pieces)]
                part_y = part_y + total * float((kb - 1) * BR + kr)
            if kb == 0 and g == 0:
                fits = lat > 0
            elif kb == 2 and g == bands - 1:
                fits = lat < last
            else:
                fits = None
            if fits is not None:
                part = [jnp.where(fits, p, 0.0) for p in part]
                part_y = jnp.where(fits, part_y, 0.0)
            sums = [s + p for s, p in zip(sums, part)]
            sum_y = sum_y + part_y
        mass = (sums[0] + sums[1]) + (sums[2] + sums[3]) + (sums[4] + sums[5])
        at_four = jnp.where(on_left, -2.0, 4.0)
        at_five = jnp.where(on_left, -1.0, 5.0)
        octs = sums[1] + 2.0 * sums[2] + 3.0 * sums[3] + at_four * sums[4] + at_five * sums[5]
        sum_x = octs * 8.0 + mass * sub
        mass = jnp.sum(mass, axis=0, keepdims=True)
        sum_x = jnp.sum(sum_x, axis=0, keepdims=True)
        sum_y = jnp.sum(sum_y, axis=0, keepdims=True)
        row = (lane // cols)[0:1].astype(F32)
        column = q_col[0:1].astype(F32)
        flow[0:1, g * queries : (g + 1) * queries] = sum_y / mass - row
        flow[1:2, g * queries : (g + 1) * queries] = sum_x / mass - column


def mix_kernel(cells, enc_one, wt, mix):
    feats = enc_one[...].reshape(cells, CH)
    step = 256
    for c0 in range(0, cells, step):
        for k in range(UP):
            wk = jnp.concatenate(
                [wt[n * 64 + k * UP : n * 64 + k * UP + UP] for n in range(9)], axis=0
            )
            logits = lax.dot_general(
                wk, feats[c0 : c0 + step], (((1,), (1,)), ((), ())), preferred_element_type=F32
            )
            expo = jnp.exp(logits).reshape(9, UP, step)
            total = jnp.sum(expo, axis=0)
            mix[:, k, :, c0 : c0 + step] = expo / total[None]


def up_kernel(rows, cols, mix, own, lat_a, lat_b, lon_in, lon_x, out, pad):
    lat_odd = lax.axis_index("lat") % 2 == 1
    lon_odd = lax.axis_index("lon") % 2 == 1
    cells = rows * cols
    width = cells + 2 * cols

    def place(slot, mine, a, b):
        def at(north, south):
            pad[slot, :, 0:cols] = north[:, cells - cols : cells]
            pad[slot, :, cols + cells : width] = south[:, 0:cols]

        pad[slot, :, cols : cols + cells] = mine[...]

        @pl.when(lat_odd)
        def _():
            at(b, a)

        @pl.when(jnp.logical_not(lat_odd))
        def _():
            at(a, b)

    place(0, own, lat_a, lat_b)

    @pl.when(lon_odd)
    def _():
        place(1, lon_in.at[0], lon_in.at[1], lon_in.at[2])
        place(2, lon_x.at[0], lon_x.at[1], lon_x.at[2])

    @pl.when(jnp.logical_not(lon_odd))
    def _():
        place(1, lon_x.at[0], lon_x.at[1], lon_x.at[2])
        place(2, lon_in.at[0], lon_in.at[1], lon_in.at[2])

    total_lanes = pad.shape[2]
    mid, left, right = pad[0] * UP, pad[1] * UP, pad[2] * UP
    column = lax.broadcasted_iota(jnp.int32, mid.shape, 1) % cols
    west = jnp.where(
        column == 0, pltpu.roll(left, total_lanes - (cols - 1), 1), pltpu.roll(mid, 1, 1)
    )
    east = jnp.where(
        column == cols - 1, pltpu.roll(right, cols - 1, 1), pltpu.roll(mid, total_lanes - 1, 1)
    )
    shifted = []
    for a in range(3):
        for field in (west, mid, east):
            moved = field if a == 0 else pltpu.roll(field, total_lanes - a * cols, 1)
            shifted.append(moved[:, 0:cells])
    src = lax.broadcasted_iota(jnp.int32, (UP * cols, UP * cols), 0)
    dst = lax.broadcasted_iota(jnp.int32, (UP * cols, UP * cols), 1)
    order = jnp.where((dst // UP == src % cols) & (dst % UP == src // cols), 1.0, 0.0).astype(BF16)
    tile = 128
    group = tile // cols
    lane = lax.broadcasted_iota(jnp.int32, (UP, tile), 1)
    bits = []
    span = 1
    while span < group:
        bits.append((span, (lane // (span * cols)) % 2 == 1))
        span *= 2
    for d in range(2):
        lanes_of = [[None] * (UP // group) for _ in range(rows)]
        for t in range(cells // tile):
            flows = [
                jnp.broadcast_to(s[d : d + 1, t * tile : (t + 1) * tile], (UP, tile))
                for s in shifted
            ]
            for u in range(UP // group):
                block = []
                for k in range(group):
                    acc = None
                    for n in range(9):
                        term = mix[n, u * group + k, :, t * tile : (t + 1) * tile] * flows[n]
                        acc = term if acc is None else acc + term
                    block.append(acc)
                for span, high in bits:
                    shift = span * cols
                    done = list(block)
                    for k in range(group):
                        if k & span:
                            continue
                        lo_v, hi_v = block[k], block[k | span]
                        done[k] = jnp.where(high, pltpu.roll(hi_v, shift, 1), lo_v)
                        done[k | span] = jnp.where(
                            high, hi_v, pltpu.roll(lo_v, tile - shift, 1)
                        )
                    block = done
                for k in range(group):
                    lanes_of[t * group + k][u] = block[k]
        value = jnp.concatenate([jnp.concatenate(v, axis=1) for v in lanes_of], axis=0)
        high_part = value.astype(BF16)
        low_part = (value - high_part.astype(F32)).astype(BF16)
        out[d] = jnp.dot(high_part, order, preferred_element_type=F32) + jnp.dot(
            low_part, order, preferred_element_type=F32
        )


def body(frame_one, frame_two, enc_weight, mask_weight):
    rows, cols = frame_one.shape[0], frame_one.shape[1]
    cells = rows * cols
    n2, n1 = rows + 2 * BR + 2, rows + 2
    slots = n2 + -(-n2 // BC) + -(-n1 // BC)
    wide = cols + 2 * BC
    lats, lons = lax.axis_size("lat"), lax.axis_size("lon")
    lat_odd = lax.axis_index("lat") % 2 == 1
    far_lat = pair_perm(lats, 1, False)
    near_lat = pair_perm(lats, 0, False)
    far_lon = pair_perm(lons, 1, True)
    near_lon = pair_perm(lons, 0, True)

    def edge_rows(bottom):
        two = lax.dynamic_slice_in_dim(frame_two, jnp.where(bottom, rows - BR - 1, 0), BR + 1, 0)
        one = lax.dynamic_slice_in_dim(frame_one, jnp.where(bottom, rows - 1, 0), 1, 0)
        return jnp.concatenate([two, one], axis=0)

    row_a = lax.ppermute(edge_rows(lat_odd), "lat", far_lat)
    row_b = lax.ppermute(edge_rows(jnp.logical_not(lat_odd)), "lat", near_lat)

    msg = jax.ShapeDtypeStruct((slots, BC, CH), BF16)
    m_in, m_x = pl.pallas_call(
        functools.partial(pack_kernel, rows, cols),
        out_shape=(msg, msg),
        in_specs=[VMEM] * 4,
        out_specs=(VMEM, VMEM),
        scratch_shapes=[
            pltpu.VMEM((n2 + n1, cols, CH), BF16),
            pltpu.VMEM((-(-n2 // BC) * BC, CH), F32),
        ],
        compiler_params=params(16),
        name="pack",
    )(frame_one, frame_two, row_a, row_b)
    col_x = lax.ppermute(m_x, "lon", far_lon)
    col_in = lax.ppermute(m_in, "lon", near_lon)

    flow, enc_one = pl.pallas_call(
        functools.partial(flow_kernel, rows, cols),
        out_shape=(
            jax.ShapeDtypeStruct((2, cells), F32),
            jax.ShapeDtypeStruct((rows, cols, CH), BF16),
        ),
        in_specs=[VMEM] * 7,
        out_specs=(VMEM, VMEM),
        scratch_shapes=[
            pltpu.VMEM((n2, wide + 2 * BR, CH), F32),
            pltpu.VMEM((n1, cols + 2 * BR, CH), F32),
            pltpu.VMEM((3, n2, wide, CH), BF16),
            pltpu.VMEM((3, n1, cols, CH), BF16),
            pltpu.VMEM((rows + 2 * BR, wide, CH), BF16),
        ],
        compiler_params=params(32),
        name="flow",
    )(frame_one, frame_two, row_a, row_b, col_in, col_x, enc_weight.reshape(9 * CH, CH))

    flow_a = lax.ppermute(flow, "lat", far_lat)
    flow_b = lax.ppermute(flow, "lat", near_lat)

    wt = mask_weight.reshape(CH, 9, UP, UP).transpose(1, 3, 2, 0).reshape(9 * UP * UP, CH)
    mix = pl.pallas_call(
        functools.partial(mix_kernel, cells),
        out_shape=jax.ShapeDtypeStruct((9, UP, UP, cells), F32),
        in_specs=[VMEM] * 2,
        out_specs=VMEM,
        compiler_params=params(16),
        cost_estimate=pl.CostEstimate(
            flops=2 * 576 * CH * cells, bytes_accessed=4 * 576 * cells, transcendentals=576 * cells
        ),
        name="mix",
    )(enc_one, wt)

    trio = jnp.stack([flow, flow_a, flow_b])
    lon_x = lax.ppermute(trio, "lon", far_lon)
    lon_in = lax.ppermute(trio, "lon", near_lon)
    lanes = -(-(cells + 2 * cols) // 128) * 128
    return pl.pallas_call(
        functools.partial(up_kernel, rows, cols),
        out_shape=jax.ShapeDtypeStruct((2, rows * UP, cols * UP), F32),
        in_specs=[VMEM] * 6,
        out_specs=VMEM,
        scratch_shapes=[pltpu.VMEM((3, 2, lanes), F32)],
        compiler_params=params(16),
        name="upsample",
    )(mix, flow, flow_a, flow_b, lon_in, lon_x)


def solution(mesh):
    in_specs = (P("lat", "lon", None), P("lat", "lon", None), P(), P())
    return jax.shard_map(
        body, mesh=mesh, in_specs=in_specs, out_specs=P(None, "lat", "lon"), check_vma=False
    )
```

```python
import functools
import math

import jax
import jax.numpy as jnp
from jax import lax
from jax.experimental import pallas as pl
from jax.experimental.pallas import tpu as pltpu
from jax.sharding import PartitionSpec as P

CH = 256
BR = 8
BC = 16
UP = 8
F32 = jnp.float32
BF16 = jnp.bfloat16
VMEM = pl.BlockSpec(memory_space=pltpu.VMEM)


def params(mib):
    return pltpu.CompilerParams(vmem_limit_bytes=mib * 1024 * 1024)


def pair_perm(size, first, wrap):
    out = []
    for i in range(first, size, 2):
        j = i + 1
        if j >= size:
            if not wrap:
                continue
            j -= size
        out += [(i, j), (j, i)]
    return out


def edge_kernel(rows, f1, f2, m_a, m_b, sems):
    odd = lax.axis_index("lat") % 2
    copies = []
    for k, (msg, low) in enumerate(((m_a, odd), (m_b, 1 - odd))):
        copies.append(
            pltpu.make_async_copy(
                f2.at[pl.ds(low * (rows - BR - 1), BR + 1)], msg.at[pl.ds(0, BR + 1)], sems.at[2 * k]
            )
        )
        copies.append(
            pltpu.make_async_copy(
                f1.at[pl.ds(low * (rows - 1), 1)], msg.at[pl.ds(BR + 1, 1)], sems.at[2 * k + 1]
            )
        )
    for copy in copies:
        copy.start()
    for copy in copies:
        copy.wait()


def pack_kernel(rows, cols, f1, f2, ra, rb, m_x, m_in, ends, ext, col):
    lat_odd = lax.axis_index("lat") % 2 == 1
    lon_odd = lax.axis_index("lon") % 2 == 1
    n2 = rows + 2 * BR + 2
    n1 = rows + 2
    slots2 = -(-n2 // BC)
    slots1 = -(-n1 // BC)

    def halo(north, south):
        ext[0 : BR + 1] = north[0 : BR + 1]
        ext[BR + 1 : BR + 1 + rows] = f2[...]
        ext[BR + 1 + rows : n2] = south[0 : BR + 1]
        ext[n2] = north[BR + 1]
        ext[n2 + 1 : n2 + 1 + rows] = f1[...]
        ext[n2 + 1 + rows] = south[BR + 1]

    @pl.when(lat_odd)
    def _():
        halo(rb, ra)

    @pl.when(jnp.logical_not(lat_odd))
    def _():
        halo(ra, rb)

    first = ext[0:n2, 0:BC].astype(F32)
    ends[0, 0:n2] = first[:, 0, :]
    final = ext[0:n2, cols - BC : cols].astype(F32)
    ends[1, 0:n2] = final[:, BC - 1, :]

    def edge(msg, main, extra, one):
        msg[0:n2] = ext[0:n2, main : main + BC]
        lo = extra // BC * BC
        slab = ext[0:n2, lo : lo + BC].astype(F32)
        col[0:n2] = slab[:, extra - lo, :]
        msg[n2 : n2 + slots2] = col[0 : slots2 * BC].astype(BF16).reshape(slots2, BC, CH)
        lo = one // BC * BC
        slab = ext[n2 : n2 + n1, lo : lo + BC].astype(F32)
        col[0:n1] = slab[:, one - lo, :]
        msg[n2 + slots2 :] = col[0 : slots1 * BC].astype(BF16).reshape(slots1, BC, CH)

    def right(msg):
        edge(msg, cols - BC, cols - BC - 1, cols - 1)

    def left(msg):
        edge(msg, 0, BC, 0)

    @pl.when(lon_odd)
    def _():
        right(m_x)
        left(m_in)

    @pl.when(jnp.logical_not(lon_odd))
    def _():
        left(m_x)
        right(m_in)


def conv(x, w, row, count, width):
    lhs = jnp.concatenate(
        [
            x[b, row + a : row + a + count].reshape(count * width, CH)
            for a in range(3)
            for b in range(3)
        ],
        axis=1,
    )
    return jnp.dot(lhs, w[...], preferred_element_type=F32)


def own_kernel(rows, cols, f1, f2, ra, rb, w, e2, e1, ends2, ends1, s2, s1, x2, x1):
    lat_odd = lax.axis_index("lat") % 2 == 1
    n2 = rows + 2 * BR + 2
    n1 = rows + 2

    def put_rows(north, south):
        s2[0 : BR + 1, BR : BR + cols] = north[0 : BR + 1].astype(F32)
        s2[BR + 1 + rows :, BR : BR + cols] = south[0 : BR + 1].astype(F32)
        s1[0, BR : BR + cols] = north[BR + 1].astype(F32)
        s1[n1 - 1, BR : BR + cols] = south[BR + 1].astype(F32)

    s2[BR + 1 : BR + 1 + rows, BR : BR + cols] = f2[...].astype(F32)
    s1[1 : 1 + rows, BR : BR + cols] = f1[...].astype(F32)

    @pl.when(lat_odd)
    def _():
        put_rows(rb, ra)

    @pl.when(jnp.logical_not(lat_odd))
    def _():
        put_rows(ra, rb)

    for s in (s2, s1):
        s[:, 0:BR] = jnp.zeros((s.shape[0], BR, CH), F32)
        s[:, BR + cols :] = jnp.zeros((s.shape[0], BR, CH), F32)
    for b in range(3):
        x2[b] = s2[:, BR - 1 + b : BR - 1 + b + cols].astype(BF16)
        x1[b] = s1[:, BR - 1 + b : BR - 1 + b + cols].astype(BF16)

    def run(x, out, ends, total):
        step = 2 * BR
        for r in range(0, total, step):
            acc = conv(x, w, r, step, cols).reshape(step, cols, CH)
            out[r : r + step] = acc.astype(BF16)
            ends[0, r : r + step] = acc[:, 0, :]
            ends[1, r : r + step] = acc[:, cols - 1, :]

    run(x1, e1, ends1, rows)
    run(x2, e2, ends2, rows + 2 * BR)


def flow_kernel(rows, cols, o2, o1, ends2, ends1, edges, c_x, c_in, w, flow, enc_one, ext, xs, e2):
    lat = lax.axis_index("lat")
    lon_odd = lax.axis_index("lon") % 2 == 1
    n2 = rows + 2 * BR + 2
    n1 = rows + 2
    wide = cols + 2 * BC
    tall = rows + 2 * BR
    slots2 = -(-n2 // BC)
    slots1 = -(-n1 // BC)
    place = lax.broadcasted_iota(jnp.int32, (1, BC, CH), 1)

    def beside(side, msg):
        extra = msg[n2 : n2 + slots2].astype(F32).reshape(slots2 * BC, CH)[0:n2][:, None, :]
        inner = edges[side, 0:n2][:, None, :]
        ext[:, BR : BR + BC] = msg[0:n2].astype(F32)
        ext[:, BR - 1 : BR] = inner if side else extra
        ext[:, BR + BC : BR + BC + 1] = extra if side else inner
        for b in range(3):
            xs[b] = ext[:, BR - 1 + b : BR - 1 + b + BC].astype(BF16)
        at = BC + cols if side else 0
        e2[:, at : at + BC] = conv(xs, w, 0, tall, BC).astype(BF16).reshape(tall, BC, CH)
        near = ext[:, BR : BR + 1] if side else ext[:, BR + BC - 1 : BR + BC]
        near = near[:, 0, :].astype(BF16)
        one = msg[n2 + slots2 :].reshape(slots1 * BC, CH)
        one = one.astype(F32)[0:n1].astype(BF16)
        taps = jnp.concatenate(
            [w[(3 * a + 2 * side) * CH : (3 * a + 2 * side + 1) * CH] for a in range(3)], axis=0
        )
        lhs = jnp.concatenate(
            [
                jnp.concatenate([near[a : a + tall], one[a : a + rows]], axis=0)
                for a in range(3)
            ],
            axis=1,
        )
        more = jnp.dot(lhs, taps, preferred_element_type=F32)
        hit = place == (BC - 1 if side else 0)
        lo = cols - BC if side else 0
        full = ends2[side] + more[0:tall]
        slab = jnp.where(hit, full[:, None, :], o2[:, lo : lo + BC].astype(F32))
        e2[:, BC + lo : 2 * BC + lo] = slab.astype(BF16)
        full = ends1[side] + more[tall : tall + rows]
        slab = jnp.where(hit, full[:, None, :], o1[:, lo : lo + BC].astype(F32))
        enc_one[:, lo : lo + BC] = slab.astype(BF16)

    @pl.when(lon_odd)
    def _():
        beside(0, c_in)
        beside(1, c_x)

    @pl.when(jnp.logical_not(lon_odd))
    def _():
        beside(0, c_x)
        beside(1, c_in)

    bands = rows // BR
    queries = BR * cols
    lane = lax.broadcasted_iota(jnp.int32, (BR, queries), 1)
    sub = lax.broadcasted_iota(jnp.int32, (BR, queries), 0).astype(F32)
    q_col = lane % cols
    on_left = q_col < BC
    last = lax.axis_size("lat") - 1
    for g in range(bands):
        query = enc_one[g * BR : g * BR + BR].reshape(queries, CH).astype(F32)
        query = (query * (1.0 / math.sqrt(CH))).astype(BF16)
        sums = None
        for kb in range(3):
            keys = e2[(g + kb) * BR : (g + kb + 1) * BR].reshape(BR * wide, CH)
            score = lax.dot_general(
                keys, query, (((1,), (1,)), ((), ())), preferred_element_type=F32
            ).reshape(BR, wide // BR, BR, queries)
            part = None
            part_y = None
            for kr in range(BR):
                line = score[kr]
                pieces = [jnp.exp(line[2 + i]) for i in range(4)]
                pieces += [jnp.exp(jnp.where(on_left, line[i], line[6 + i])) for i in range(2)]
                total = (pieces[0] + pieces[1]) + (pieces[2] + pieces[3]) + (pieces[4] + pieces[5])
                scaled = total * float((kb - 1) * BR + kr)
                part = pieces if part is None else [p + e for p, e in zip(part, pieces)]
                part_y = scaled if part_y is None else part_y + scaled
            part = part + [part_y]
            if kb == 0 and g == 0:
                part = [jnp.where(lat > 0, p, 0.0) for p in part]
            elif kb == 2 and g == bands - 1:
                part = [jnp.where(lat < last, p, 0.0) for p in part]
            sums = part if sums is None else [s + p for s, p in zip(sums, part)]
        mass = (sums[0] + sums[1]) + (sums[2] + sums[3]) + (sums[4] + sums[5])
        at_four = jnp.where(on_left, -2.0, 4.0)
        at_five = jnp.where(on_left, -1.0, 5.0)
        octs = sums[1] + 2.0 * sums[2] + 3.0 * sums[3] + at_four * sums[4] + at_five * sums[5]
        sum_x = octs * 8.0 + mass * sub
        mass = jnp.sum(mass, axis=0, keepdims=True)
        sum_x = jnp.sum(sum_x, axis=0, keepdims=True)
        sum_y = jnp.sum(sums[6], axis=0, keepdims=True)
        row = (lane // cols)[0:1].astype(F32)
        column = q_col[0:1].astype(F32)
        flow[0:1, g * queries : (g + 1) * queries] = sum_y / mass - row
        flow[1:2, g * queries : (g + 1) * queries] = sum_x / mass - column


def mix_kernel(cells, enc_one, wt, mix):
    feats = enc_one[...].reshape(cells, CH)
    step = 256
    for c0 in range(0, cells, step):
        for k in range(UP):
            wk = jnp.concatenate(
                [wt[n * 64 + k * UP : n * 64 + k * UP + UP] for n in range(9)], axis=0
            )
            logits = lax.dot_general(
                wk, feats[c0 : c0 + step], (((1,), (1,)), ((), ())), preferred_element_type=F32
            )
            expo = jnp.exp(logits).reshape(9, UP, step)
            total = jnp.sum(expo, axis=0)
            mix[:, k, :, c0 : c0 + step] = expo / total[None]


def up_kernel(rows, cols, mix, own, lat_a, lat_b, lon_x, lon_in, out, pad):
    lat_odd = lax.axis_index("lat") % 2 == 1
    lon_odd = lax.axis_index("lon") % 2 == 1
    cells = rows * cols
    width = cells + 2 * cols

    def place(slot, mine, a, b):
        def at(north, south):
            pad[slot, :, 0:cols] = north[:, cells - cols : cells]
            pad[slot, :, cols + cells : width] = south[:, 0:cols]

        pad[slot, :, cols : cols + cells] = mine[...]

        @pl.when(lat_odd)
        def _():
            at(b, a)

        @pl.when(jnp.logical_not(lat_odd))
        def _():
            at(a, b)

    place(0, own, lat_a, lat_b)

    @pl.when(lon_odd)
    def _():
        place(1, lon_in.at[0], lon_in.at[1], lon_in.at[2])
        place(2, lon_x.at[0], lon_x.at[1], lon_x.at[2])

    @pl.when(jnp.logical_not(lon_odd))
    def _():
        place(1, lon_x.at[0], lon_x.at[1], lon_x.at[2])
        place(2, lon_in.at[0], lon_in.at[1], lon_in.at[2])

    total_lanes = pad.shape[2]
    mid, left, right = pad[0] * UP, pad[1] * UP, pad[2] * UP
    column = lax.broadcasted_iota(jnp.int32, mid.shape, 1) % cols
    west = jnp.where(
        column == 0, pltpu.roll(left, total_lanes - (cols - 1), 1), pltpu.roll(mid, 1, 1)
    )
    east = jnp.where(
        column == cols - 1, pltpu.roll(right, cols - 1, 1), pltpu.roll(mid, total_lanes - 1, 1)
    )
    shifted = []
    for a in range(3):
        for field in (west, mid, east):
            moved = field if a == 0 else pltpu.roll(field, total_lanes - a * cols, 1)
            shifted.append(moved[:, 0:cells])
    src = lax.broadcasted_iota(jnp.int32, (UP * cols, UP * cols), 0)
    dst = lax.broadcasted_iota(jnp.int32, (UP * cols, UP * cols), 1)
    order = jnp.where((dst // UP == src % cols) & (dst % UP == src // cols), 1.0, 0.0).astype(BF16)
    tile = 128
    group = tile // cols
    lane = lax.broadcasted_iota(jnp.int32, (UP, tile), 1)
    bits = []
    span = 1
    while span < group:
        bits.append((span, (lane // (span * cols)) % 2 == 1))
        span *= 2
    for d in range(2):
        lanes_of = [[None] * (UP // group) for _ in range(rows)]
        for t in range(cells // tile):
            flows = [
                jnp.broadcast_to(s[d : d + 1, t * tile : (t + 1) * tile], (UP, tile))
                for s in shifted
            ]
            for u in range(UP // group):
                block = []
                for k in range(group):
                    acc = None
                    for n in range(9):
                        term = mix[n, u * group + k, :, t * tile : (t + 1) * tile] * flows[n]
                        acc = term if acc is None else acc + term
                    block.append(acc)
                for span, high in bits:
                    shift = span * cols
                    done = list(block)
                    for k in range(group):
                        if k & span:
                            continue
                        lo_v, hi_v = block[k], block[k | span]
                        done[k] = jnp.where(high, pltpu.roll(hi_v, shift, 1), lo_v)
                        done[k | span] = jnp.where(
                            high, hi_v, pltpu.roll(lo_v, tile - shift, 1)
                        )
                    block = done
                for k in range(group):
                    lanes_of[t * group + k][u] = block[k]
        value = jnp.concatenate([jnp.concatenate(v, axis=1) for v in lanes_of], axis=0)
        high_part = value.astype(BF16)
        low_part = (value - high_part.astype(F32)).astype(BF16)
        out[d] = jnp.dot(high_part, order, preferred_element_type=F32) + jnp.dot(
            low_part, order, preferred_element_type=F32
        )


def body(frame_one, frame_two, enc_weight, mask_weight):
    rows, cols = frame_one.shape[0], frame_one.shape[1]
    cells = rows * cols
    n2, n1 = rows + 2 * BR + 2, rows + 2
    slots = n2 + -(-n2 // BC) + -(-n1 // BC)
    wide = cols + 2 * BC
    lats, lons = lax.axis_size("lat"), lax.axis_size("lon")
    far_lat = pair_perm(lats, 1, False)
    near_lat = pair_perm(lats, 0, False)
    far_lon = pair_perm(lons, 1, True)
    near_lon = pair_perm(lons, 0, True)

    edge_rows = jax.ShapeDtypeStruct((BR + 2, cols, CH), BF16)
    m_a, m_b = pl.pallas_call(
        functools.partial(edge_kernel, rows),
        out_shape=(edge_rows, edge_rows),
        in_specs=[pl.BlockSpec(memory_space=pl.ANY)] * 2,
        out_specs=(VMEM, VMEM),
        scratch_shapes=[pltpu.SemaphoreType.DMA((4,))],
        compiler_params=params(8),
        name="edge_rows",
    )(frame_one, frame_two)
    row_a = lax.ppermute(m_a, "lat", far_lat)
    row_b = lax.ppermute(m_b, "lat", near_lat)

    msg = jax.ShapeDtypeStruct((slots, BC, CH), BF16)
    n2_pad = -(-n2 // BC) * BC
    m_x, m_in, edges = pl.pallas_call(
        functools.partial(pack_kernel, rows, cols),
        out_shape=(msg, msg, jax.ShapeDtypeStruct((2, n2_pad, CH), F32)),
        in_specs=[VMEM] * 4,
        out_specs=(VMEM,) * 3,
        scratch_shapes=[
            pltpu.VMEM((n2 + n1, cols, CH), BF16),
            pltpu.VMEM((n2_pad, CH), F32),
        ],
        compiler_params=params(16),
        name="pack",
    )(frame_one, frame_two, row_a, row_b)
    col_x = lax.ppermute(m_x, "lon", far_lon)
    col_in = lax.ppermute(m_in, "lon", near_lon)

    tall = rows + 2 * BR
    weight = enc_weight.reshape(9 * CH, CH)
    own_two, own_one, ends_two, ends_one = pl.pallas_call(
        functools.partial(own_kernel, rows, cols),
        out_shape=(
            jax.ShapeDtypeStruct((tall, cols, CH), BF16),
            jax.ShapeDtypeStruct((rows, cols, CH), BF16),
            jax.ShapeDtypeStruct((2, tall, CH), F32),
            jax.ShapeDtypeStruct((2, rows, CH), F32),
        ),
        in_specs=[VMEM] * 5,
        out_specs=(VMEM,) * 4,
        scratch_shapes=[
            pltpu.VMEM((n2, cols + 2 * BR, CH), F32),
            pltpu.VMEM((n1, cols + 2 * BR, CH), F32),
            pltpu.VMEM((3, n2, cols, CH), BF16),
            pltpu.VMEM((3, n1, cols, CH), BF16),
        ],
        compiler_params=params(20),
        cost_estimate=pl.CostEstimate(
            flops=2 * 9 * CH * CH * cols * (tall + rows), bytes_accessed=4 << 20, transcendentals=0
        ),
        name="encode_own",
    )(frame_one, frame_two, row_a, row_b, weight)

    flow, enc_one = pl.pallas_call(
        functools.partial(flow_kernel, rows, cols),
        out_shape=(
            jax.ShapeDtypeStruct((2, cells), F32),
            jax.ShapeDtypeStruct((rows, cols, CH), BF16),
        ),
        in_specs=[VMEM] * 8,
        out_specs=(VMEM, VMEM),
        scratch_shapes=[
            pltpu.VMEM((n2, BC + 2 * BR, CH), F32),
            pltpu.VMEM((3, n2, BC, CH), BF16),
            pltpu.VMEM((tall, wide, CH), BF16),
        ],
        compiler_params=params(20),
        name="flow",
    )(own_two, own_one, ends_two, ends_one, edges, col_x, col_in, weight)

    flow_a = lax.ppermute(flow, "lat", far_lat)
    flow_b = lax.ppermute(flow, "lat", near_lat)

    wt = mask_weight.reshape(CH, 9, UP, UP).transpose(1, 3, 2, 0).reshape(9 * UP * UP, CH)
    mix = pl.pallas_call(
        functools.partial(mix_kernel, cells),
        out_shape=jax.ShapeDtypeStruct((9, UP, UP, cells), F32),
        in_specs=[VMEM] * 2,
        out_specs=VMEM,
        compiler_params=params(16),
        cost_estimate=pl.CostEstimate(
            flops=2 * 576 * CH * cells, bytes_accessed=4 * 576 * cells, transcendentals=576 * cells
        ),
        name="mix",
    )(enc_one, wt)

    trio = jnp.stack([flow, flow_a, flow_b])
    lon_x = lax.ppermute(trio, "lon", far_lon)
    lon_in = lax.ppermute(trio, "lon", near_lon)
    lanes = -(-(cells + 2 * cols) // 128) * 128
    return pl.pallas_call(
        functools.partial(up_kernel, rows, cols),
        out_shape=jax.ShapeDtypeStruct((2, rows * UP, cols * UP), F32),
        in_specs=[VMEM] * 6,
        out_specs=VMEM,
        scratch_shapes=[pltpu.VMEM((3, 2, lanes), F32)],
        compiler_params=params(16),
        name="upsample",
    )(mix, flow, flow_a, flow_b, lon_x, lon_in)


def solution(mesh):
    in_specs = (P("lat", "lon", None), P("lat", "lon", None), P(), P())
    return jax.shard_map(
        body, mesh=mesh, in_specs=in_specs, out_specs=P(None, "lat", "lon"), check_vma=False
    )
```

```python
import functools
import math

import jax
import jax.numpy as jnp
from jax import lax
from jax.experimental import pallas as pl
from jax.experimental.pallas import tpu as pltpu
from jax.sharding import PartitionSpec as P

CH = 256
BR = 8
BC = 16
UP = 8
F32 = jnp.float32
BF16 = jnp.bfloat16
VMEM = pl.BlockSpec(memory_space=pltpu.VMEM)


def params(mib):
    return pltpu.CompilerParams(vmem_limit_bytes=mib * 1024 * 1024)


def pair_perm(size, first, wrap):
    out = []
    for i in range(first, size, 2):
        j = i + 1
        if j >= size:
            if not wrap:
                continue
            j -= size
        out += [(i, j), (j, i)]
    return out


def edge_kernel(rows, cols, f1, f2, m_a, m_b, m_o, g1, g2, col, sems):
    odd = lax.axis_index("lat") % 2
    lon_odd = lax.axis_index("lon") % 2 == 1
    copies = [
        pltpu.make_async_copy(f2, g2, sems.at[4]),
        pltpu.make_async_copy(f1, g1, sems.at[5]),
    ]
    for k, (msg, low) in enumerate(((m_a, odd), (m_b, 1 - odd))):
        copies.append(
            pltpu.make_async_copy(
                f2.at[pl.ds(low * (rows - BR - 1), BR + 1)], msg.at[pl.ds(0, BR + 1)], sems.at[2 * k]
            )
        )
        copies.append(
            pltpu.make_async_copy(
                f1.at[pl.ds(low * (rows - 1), 1)], msg.at[pl.ds(BR + 1, 1)], sems.at[2 * k + 1]
            )
        )
    for copy in copies:
        copy.start()
    for copy in copies:
        copy.wait()

    def column(frame, at):
        lo = at // BC * BC
        slab = frame[:, lo : lo + BC].astype(F32)
        col[0:rows] = slab[:, at - lo, :]
        return col[...].astype(BF16).reshape(-1, BC, CH)

    def send(main, extra, one):
        m_o[0:rows] = g2[:, main : main + BC]
        m_o[rows : rows + col.shape[0] // BC] = column(g2, extra)
        m_o[rows + col.shape[0] // BC :] = column(g1, one)

    @pl.when(lon_odd)
    def _():
        send(cols - BC, cols - BC - 1, cols - 1)

    @pl.when(jnp.logical_not(lon_odd))
    def _():
        send(0, BC, 0)


def pack_kernel(rows, cols, f1, f2, ra, rb, m_c, m_in, ends, ext, col):
    lat_odd = lax.axis_index("lat") % 2 == 1
    lon_odd = lax.axis_index("lon") % 2 == 1
    n2 = rows + 2 * BR + 2
    n1 = rows + 2
    nh = BR + 1
    slots2 = -(-n2 // BC)
    slots1 = -(-n1 // BC)

    def halo(north, south):
        ext[0:nh] = north[0:nh]
        ext[nh : nh + rows] = f2[...]
        ext[nh + rows : n2] = south[0:nh]
        ext[n2] = north[nh]
        ext[n2 + 1 : n2 + 1 + rows] = f1[...]
        ext[n2 + 1 + rows] = south[nh]

    @pl.when(lat_odd)
    def _():
        halo(rb, ra)

    @pl.when(jnp.logical_not(lat_odd))
    def _():
        halo(ra, rb)

    first = ext[0:n2, 0:BC].astype(F32)
    ends[0, 0:n2] = first[:, 0, :]
    final = ext[0:n2, cols - BC : cols].astype(F32)
    ends[1, 0:n2] = final[:, BC - 1, :]

    def column(lo, hi, at):
        base = at // BC * BC
        return ext[lo:hi, base : base + BC].astype(F32)[:, at - base, :]

    def edge(msg, main, extra, one):
        msg[0:n2] = ext[0:n2, main : main + BC]
        col[0:n2] = column(0, n2, extra)
        msg[n2 : n2 + slots2] = col[0 : slots2 * BC].astype(BF16).reshape(slots2, BC, CH)
        col[0:n1] = column(n2, n2 + n1, one)
        msg[n2 + slots2 :] = col[0 : slots1 * BC].astype(BF16).reshape(slots1, BC, CH)

    def corner(msg, main, extra, one):
        msg[0:nh] = ext[0:nh, main : main + BC]
        msg[nh : 2 * nh] = ext[n2 - nh : n2, main : main + BC]
        col[0:nh] = column(0, nh, extra)
        col[nh : 2 * nh] = column(n2 - nh, n2, extra)
        col[2 * nh : 2 * nh + 1] = column(n2, n2 + 1, one)
        col[2 * nh + 1 : 2 * nh + 2] = column(n2 + n1 - 1, n2 + n1, one)
        msg[2 * nh :] = col[0 : 2 * BC].astype(BF16).reshape(2, BC, CH)

    right = (cols - BC, cols - BC - 1, cols - 1)
    left = (0, BC, 0)

    @pl.when(lon_odd)
    def _():
        corner(m_c, *right)
        edge(m_in, *left)

    @pl.when(jnp.logical_not(lon_odd))
    def _():
        corner(m_c, *left)
        edge(m_in, *right)


def conv(x, w, row, count, width):
    lhs = jnp.concatenate(
        [
            x[b, row + a : row + a + count].reshape(count * width, CH)
            for a in range(3)
            for b in range(3)
        ],
        axis=1,
    )
    return jnp.dot(lhs, w[...], preferred_element_type=F32)


def own_kernel(rows, cols, f1, f2, ra, rb, w, e2, e1, ends2, ends1, s2, s1, x2, x1):
    lat_odd = lax.axis_index("lat") % 2 == 1
    n2 = rows + 2 * BR + 2
    n1 = rows + 2

    def put_rows(north, south):
        s2[0 : BR + 1, BR : BR + cols] = north[0 : BR + 1].astype(F32)
        s2[BR + 1 + rows :, BR : BR + cols] = south[0 : BR + 1].astype(F32)
        s1[0, BR : BR + cols] = north[BR + 1].astype(F32)
        s1[n1 - 1, BR : BR + cols] = south[BR + 1].astype(F32)

    s2[BR + 1 : BR + 1 + rows, BR : BR + cols] = f2[...].astype(F32)
    s1[1 : 1 + rows, BR : BR + cols] = f1[...].astype(F32)

    @pl.when(lat_odd)
    def _():
        put_rows(rb, ra)

    @pl.when(jnp.logical_not(lat_odd))
    def _():
        put_rows(ra, rb)

    for s in (s2, s1):
        s[:, 0:BR] = jnp.zeros((s.shape[0], BR, CH), F32)
        s[:, BR + cols :] = jnp.zeros((s.shape[0], BR, CH), F32)
    for b in range(3):
        x2[b] = s2[:, BR - 1 + b : BR - 1 + b + cols].astype(BF16)
        x1[b] = s1[:, BR - 1 + b : BR - 1 + b + cols].astype(BF16)

    def run(x, out, ends, total):
        step = 2 * BR
        for r in range(0, total, step):
            acc = conv(x, w, r, step, cols).reshape(step, cols, CH)
            out[r : r + step] = acc.astype(BF16)
            ends[0, r : r + step] = acc[:, 0, :]
            ends[1, r : r + step] = acc[:, cols - 1, :]

    run(x1, e1, ends1, rows)
    run(x2, e2, ends2, rows + 2 * BR)


def finish_side(rows, cols, side, w, o2, o1, ends2, ends1, edges, ext, xs, one, put):
    n2 = rows + 2 * BR + 2
    tall = rows + 2 * BR
    place = lax.broadcasted_iota(jnp.int32, (1, BC, CH), 1)
    inner = edges[side, 0:n2][:, None, :]
    at = BR - 1 if side else BR + BC
    ext[:, at : at + 1] = inner
    for b in range(3):
        xs[b] = ext[:, BR - 1 + b : BR - 1 + b + BC].astype(BF16)
    strip = conv(xs, w, 0, tall, BC).astype(BF16).reshape(tall, BC, CH)
    near = ext[:, BR : BR + 1] if side else ext[:, BR + BC - 1 : BR + BC]
    near = near[:, 0, :].astype(BF16)
    taps = jnp.concatenate(
        [w[(3 * a + 2 * side) * CH : (3 * a + 2 * side + 1) * CH] for a in range(3)], axis=0
    )
    lhs = jnp.concatenate(
        [jnp.concatenate([near[a : a + tall], one[a : a + rows]], axis=0) for a in range(3)],
        axis=1,
    )
    more = jnp.dot(lhs, taps, preferred_element_type=F32)
    hit = place == (BC - 1 if side else 0)
    lo = cols - BC if side else 0
    full = ends2[side] + more[0:tall]
    two = jnp.where(hit, full[:, None, :], o2[:, lo : lo + BC].astype(F32)).astype(BF16)
    full = ends1[side] + more[tall : tall + rows]
    first = jnp.where(hit, full[:, None, :], o1[:, lo : lo + BC].astype(F32)).astype(BF16)
    put(side, strip, two, first)


def strip_kernel(rows, cols, o2, o1, ends2, ends1, edges, chip, w, strip, two, first, ext, xs):
    lon_odd = lax.axis_index("lon") % 2 == 1
    c_in = chip.at[1 - lax.axis_index("lon") % 2]
    n2 = rows + 2 * BR + 2
    n1 = rows + 2
    slots2 = -(-n2 // BC)
    slots1 = -(-n1 // BC)

    def put(side, *values):
        for ref, value in zip((strip, two, first), values):
            ref[...] = value

    def run(side):
        ext[:, BR : BR + BC] = c_in[0:n2].astype(F32)
        extra = c_in[n2 : n2 + slots2].astype(F32).reshape(slots2 * BC, CH)
        at = BR + BC if side else BR - 1
        ext[:, at : at + 1] = extra[0:n2][:, None, :]
        one = c_in[n2 + slots2 :].astype(F32).reshape(slots1 * BC, CH)[0:n1].astype(BF16)
        finish_side(rows, cols, side, w, o2, o1, ends2, ends1, edges, ext, xs, one, put)

    @pl.when(lon_odd)
    def _():
        run(0)

    @pl.when(jnp.logical_not(lon_odd))
    def _():
        run(1)


def flow_kernel(
    rows, cols, o2, o1, ends2, ends1, edges, strip_in, two_in, first_in, c_o, c_c, w,
    flow, enc_one, ext, xs, col, e2,
):
    lat = lax.axis_index("lat")
    lon_odd = lax.axis_index("lon") % 2 == 1
    n2 = rows + 2 * BR + 2
    n1 = rows + 2
    nh = BR + 1
    wide = cols + 2 * BC
    pads = (c_o.shape[0] - rows) // 2

    def put(side, strip, two, first):
        at = BC + cols if side else 0
        e2[:, at : at + BC] = strip
        lo = cols - BC if side else 0
        e2[:, BC + lo : 2 * BC + lo] = two
        enc_one[:, lo : lo + BC] = first

    def run(side):
        put(1 - side, strip_in[...], two_in[...], first_in[...])
        ext[0:nh, BR : BR + BC] = c_c[0:nh].astype(F32)
        ext[nh : nh + rows, BR : BR + BC] = c_o[0:rows].astype(F32)
        ext[nh + rows :, BR : BR + BC] = c_c[nh : 2 * nh].astype(F32)
        far = c_c[2 * nh :].astype(F32).reshape(2 * BC, CH)
        mine = c_o[rows : rows + pads].astype(F32).reshape(pads * BC, CH)
        at = BR + BC if side else BR - 1
        ext[0:nh, at : at + 1] = far[0:nh][:, None, :]
        ext[nh : nh + rows, at : at + 1] = mine[0:rows][:, None, :]
        ext[nh + rows :, at : at + 1] = far[nh : 2 * nh][:, None, :]
        mine = c_o[rows + pads :].astype(F32).reshape(pads * BC, CH)
        col[0:1] = far[2 * nh : 2 * nh + 1]
        col[1 : 1 + rows] = mine[0:rows]
        col[1 + rows : 2 + rows] = far[2 * nh + 1 : 2 * nh + 2]
        one = col[0:n1].astype(BF16)
        finish_side(rows, cols, side, w, o2, o1, ends2, ends1, edges, ext, xs, one, put)

    @pl.when(lon_odd)
    def _():
        run(1)

    @pl.when(jnp.logical_not(lon_odd))
    def _():
        run(0)

    bands = rows // BR
    queries = BR * cols
    lane = lax.broadcasted_iota(jnp.int32, (BR, queries), 1)
    sub = lax.broadcasted_iota(jnp.int32, (BR, queries), 0).astype(F32)
    q_col = lane % cols
    on_left = q_col < BC
    last = lax.axis_size("lat") - 1
    for g in range(bands):
        query = enc_one[g * BR : g * BR + BR].reshape(queries, CH).astype(F32)
        query = (query * (1.0 / math.sqrt(CH))).astype(BF16)
        sums = None
        for kb in range(3):
            keys = e2[(g + kb) * BR : (g + kb + 1) * BR].reshape(BR * wide, CH)
            score = lax.dot_general(
                keys, query, (((1,), (1,)), ((), ())), preferred_element_type=F32
            ).reshape(BR, wide // BR, BR, queries)
            part = None
            part_y = None
            for kr in range(BR):
                line = score[kr]
                pieces = [jnp.exp(line[2 + i]) for i in range(4)]
                pieces += [jnp.exp(jnp.where(on_left, line[i], line[6 + i])) for i in range(2)]
                total = (pieces[0] + pieces[1]) + (pieces[2] + pieces[3]) + (pieces[4] + pieces[5])
                scaled = total * float((kb - 1) * BR + kr)
                part = pieces if part is None else [p + e for p, e in zip(part, pieces)]
                part_y = scaled if part_y is None else part_y + scaled
            part = part + [part_y]
            if kb == 0 and g == 0:
                part = [jnp.where(lat > 0, p, 0.0) for p in part]
            elif kb == 2 and g == bands - 1:
                part = [jnp.where(lat < last, p, 0.0) for p in part]
            sums = part if sums is None else [s + p for s, p in zip(sums, part)]
        mass = (sums[0] + sums[1]) + (sums[2] + sums[3]) + (sums[4] + sums[5])
        at_four = jnp.where(on_left, -2.0, 4.0)
        at_five = jnp.where(on_left, -1.0, 5.0)
        octs = sums[1] + 2.0 * sums[2] + 3.0 * sums[3] + at_four * sums[4] + at_five * sums[5]
        sum_x = octs * 8.0 + mass * sub
        mass = jnp.sum(mass, axis=0, keepdims=True)
        sum_x = jnp.sum(sum_x, axis=0, keepdims=True)
        sum_y = jnp.sum(sums[6], axis=0, keepdims=True)
        row = (lane // cols)[0:1].astype(F32)
        column = q_col[0:1].astype(F32)
        flow[0:1, g * queries : (g + 1) * queries] = sum_y / mass - row
        flow[1:2, g * queries : (g + 1) * queries] = sum_x / mass - column


def mix_kernel(cells, enc_one, wt, mix):
    feats = enc_one[...].reshape(cells, CH)
    step = 256
    for c0 in range(0, cells, step):
        for k in range(UP):
            wk = jnp.concatenate(
                [wt[n * 64 + k * UP : n * 64 + k * UP + UP] for n in range(9)], axis=0
            )
            logits = lax.dot_general(
                wk, feats[c0 : c0 + step], (((1,), (1,)), ((), ())), preferred_element_type=F32
            )
            expo = jnp.exp(logits).reshape(9, UP, step)
            total = jnp.sum(expo, axis=0)
            mix[:, k, :, c0 : c0 + step] = expo / total[None]


def up_kernel(rows, cols, mix, own, lat_a, lat_b, lon_x, chip, out, pad):
    lat_odd = lax.axis_index("lat") % 2 == 1
    lon_odd = lax.axis_index("lon") % 2 == 1
    lon_in = chip.at[1 - lax.axis_index("lon") % 2]
    cells = rows * cols
    width = cells + 2 * cols

    def place(slot, mine, a, b):
        def at(north, south):
            pad[slot, :, 0:cols] = north[:, cells - cols : cells]
            pad[slot, :, cols + cells : width] = south[:, 0:cols]

        pad[slot, :, cols : cols + cells] = mine[...]

        @pl.when(lat_odd)
        def _():
            at(b, a)

        @pl.when(jnp.logical_not(lat_odd))
        def _():
            at(a, b)

    place(0, own, lat_a, lat_b)

    @pl.when(lon_odd)
    def _():
        place(1, lon_in.at[0], lon_in.at[1], lon_in.at[2])
        place(2, lon_x.at[0], lon_x.at[1], lon_x.at[2])

    @pl.when(jnp.logical_not(lon_odd))
    def _():
        place(1, lon_x.at[0], lon_x.at[1], lon_x.at[2])
        place(2, lon_in.at[0], lon_in.at[1], lon_in.at[2])

    total_lanes = pad.shape[2]
    mid, left, right = pad[0] * UP, pad[1] * UP, pad[2] * UP
    column = lax.broadcasted_iota(jnp.int32, mid.shape, 1) % cols
    west = jnp.where(
        column == 0, pltpu.roll(left, total_lanes - (cols - 1), 1), pltpu.roll(mid, 1, 1)
    )
    east = jnp.where(
        column == cols - 1, pltpu.roll(right, cols - 1, 1), pltpu.roll(mid, total_lanes - 1, 1)
    )
    shifted = []
    for a in range(3):
        for field in (west, mid, east):
            moved = field if a == 0 else pltpu.roll(field, total_lanes - a * cols, 1)
            shifted.append(moved[:, 0:cells])
    src = lax.broadcasted_iota(jnp.int32, (UP * cols, UP * cols), 0)
    dst = lax.broadcasted_iota(jnp.int32, (UP * cols, UP * cols), 1)
    order = jnp.where((dst // UP == src % cols) & (dst % UP == src // cols), 1.0, 0.0).astype(BF16)
    tile = 128
    group = tile // cols
    lane = lax.broadcasted_iota(jnp.int32, (UP, tile), 1)
    bits = []
    span = 1
    while span < group:
        bits.append((span, (lane // (span * cols)) % 2 == 1))
        span *= 2
    for d in range(2):
        lanes_of = [[None] * (UP // group) for _ in range(rows)]
        for t in range(cells // tile):
            flows = [
                jnp.broadcast_to(s[d : d + 1, t * tile : (t + 1) * tile], (UP, tile))
                for s in shifted
            ]
            for u in range(UP // group):
                block = []
                for k in range(group):
                    acc = None
                    for n in range(9):
                        term = mix[n, u * group + k, :, t * tile : (t + 1) * tile] * flows[n]
                        acc = term if acc is None else acc + term
                    block.append(acc)
                for span, high in bits:
                    shift = span * cols
                    done = list(block)
                    for k in range(group):
                        if k & span:
                            continue
                        lo_v, hi_v = block[k], block[k | span]
                        done[k] = jnp.where(high, pltpu.roll(hi_v, shift, 1), lo_v)
                        done[k | span] = jnp.where(
                            high, hi_v, pltpu.roll(lo_v, tile - shift, 1)
                        )
                    block = done
                for k in range(group):
                    lanes_of[t * group + k][u] = block[k]
        value = jnp.concatenate([jnp.concatenate(v, axis=1) for v in lanes_of], axis=0)
        high_part = value.astype(BF16)
        low_part = (value - high_part.astype(F32)).astype(BF16)
        out[d] = jnp.dot(high_part, order, preferred_element_type=F32) + jnp.dot(
            low_part, order, preferred_element_type=F32
        )


def body(frame_one, frame_two, enc_weight, mask_weight):
    rows, cols = frame_one.shape[0], frame_one.shape[1]
    cells = rows * cols
    n2, n1 = rows + 2 * BR + 2, rows + 2
    slots = n2 + -(-n2 // BC) + -(-n1 // BC)
    own_slots = rows + 2 * -(-rows // BC)
    wide = cols + 2 * BC
    lats, lons = lax.axis_size("lat"), lax.axis_size("lon")
    far_lat = pair_perm(lats, 1, False)
    near_lat = pair_perm(lats, 0, False)
    far_lon = pair_perm(lons, 1, True)
    chips = [[i, i + 1] for i in range(0, lons, 2)]

    edge_rows = jax.ShapeDtypeStruct((BR + 2, cols, CH), BF16)
    tile = jax.ShapeDtypeStruct((rows, cols, CH), BF16)
    m_a, m_b, m_o, one, two = pl.pallas_call(
        functools.partial(edge_kernel, rows, cols),
        out_shape=(edge_rows, edge_rows, jax.ShapeDtypeStruct((own_slots, BC, CH), BF16), tile, tile),
        in_specs=[pl.BlockSpec(memory_space=pltpu.MemorySpace.HBM)] * 2,
        out_specs=(VMEM,) * 5,
        scratch_shapes=[
            pltpu.VMEM((-(-rows // BC) * BC, CH), F32),
            pltpu.SemaphoreType.DMA((6,)),
        ],
        compiler_params=params(8),
        name="edges",
    )(
        pltpu.with_memory_space_constraint(frame_one, pltpu.MemorySpace.HBM),
        pltpu.with_memory_space_constraint(frame_two, pltpu.MemorySpace.HBM),
    )
    row_a = lax.ppermute(m_a, "lat", far_lat)
    row_b = lax.ppermute(m_b, "lat", near_lat)
    col_o = lax.ppermute(m_o, "lon", far_lon)

    n2_pad = -(-n2 // BC) * BC
    m_c, m_in, edges = pl.pallas_call(
        functools.partial(pack_kernel, rows, cols),
        out_shape=(
            jax.ShapeDtypeStruct((2 * BR + 4, BC, CH), BF16),
            jax.ShapeDtypeStruct((slots, BC, CH), BF16),
            jax.ShapeDtypeStruct((2, n2_pad, CH), F32),
        ),
        in_specs=[VMEM] * 4,
        out_specs=(VMEM,) * 3,
        scratch_shapes=[
            pltpu.VMEM((n2 + n1, cols, CH), BF16),
            pltpu.VMEM((n2_pad, CH), F32),
        ],
        compiler_params=params(16),
        name="pack",
    )(one, two, row_a, row_b)
    col_c = lax.ppermute(m_c, "lon", far_lon)
    col_in = lax.all_gather(m_in, "lon", axis_index_groups=chips)

    tall = rows + 2 * BR
    weight = enc_weight.reshape(9 * CH, CH)
    own_two, own_one, ends_two, ends_one = pl.pallas_call(
        functools.partial(own_kernel, rows, cols),
        out_shape=(
            jax.ShapeDtypeStruct((tall, cols, CH), BF16),
            jax.ShapeDtypeStruct((rows, cols, CH), BF16),
            jax.ShapeDtypeStruct((2, tall, CH), F32),
            jax.ShapeDtypeStruct((2, rows, CH), F32),
        ),
        in_specs=[VMEM] * 5,
        out_specs=(VMEM,) * 4,
        scratch_shapes=[
            pltpu.VMEM((n2, cols + 2 * BR, CH), F32),
            pltpu.VMEM((n1, cols + 2 * BR, CH), F32),
            pltpu.VMEM((3, n2, cols, CH), BF16),
            pltpu.VMEM((3, n1, cols, CH), BF16),
        ],
        compiler_params=params(20),
        cost_estimate=pl.CostEstimate(
            flops=2 * 9 * CH * CH * cols * (tall + rows), bytes_accessed=4 << 20, transcendentals=0
        ),
        name="encode_own",
    )(one, two, row_a, row_b, weight)

    strip = jax.ShapeDtypeStruct((tall, BC, CH), BF16)
    side_scratch = [pltpu.VMEM((n2, BC + 2 * BR, CH), F32), pltpu.VMEM((3, n2, BC, CH), BF16)]
    strip_in, two_in, first_in = pl.pallas_call(
        functools.partial(strip_kernel, rows, cols),
        out_shape=(strip, strip, jax.ShapeDtypeStruct((rows, BC, CH), BF16)),
        in_specs=[VMEM] * 7,
        out_specs=(VMEM,) * 3,
        scratch_shapes=side_scratch,
        compiler_params=params(16),
        cost_estimate=pl.CostEstimate(
            flops=2 * 9 * CH * CH * BC * tall, bytes_accessed=4 << 20, transcendentals=0
        ),
        name="strip",
    )(own_two, own_one, ends_two, ends_one, edges, col_in, weight)

    flow, enc_one = pl.pallas_call(
        functools.partial(flow_kernel, rows, cols),
        out_shape=(
            jax.ShapeDtypeStruct((2, cells), F32),
            jax.ShapeDtypeStruct((rows, cols, CH), BF16),
        ),
        in_specs=[VMEM] * 11,
        out_specs=(VMEM, VMEM),
        scratch_shapes=side_scratch
        + [pltpu.VMEM((-(-n1 // BR) * BR, CH), F32), pltpu.VMEM((tall, wide, CH), BF16)],
        compiler_params=params(20),
        name="flow",
    )(
        own_two, own_one, ends_two, ends_one, edges, strip_in, two_in, first_in, col_o, col_c, weight
    )

    flow_a = lax.ppermute(flow, "lat", far_lat)
    flow_b = lax.ppermute(flow, "lat", near_lat)

    wt = mask_weight.reshape(CH, 9, UP, UP).transpose(1, 3, 2, 0).reshape(9 * UP * UP, CH)
    mix = pl.pallas_call(
        functools.partial(mix_kernel, cells),
        out_shape=jax.ShapeDtypeStruct((9, UP, UP, cells), F32),
        in_specs=[VMEM] * 2,
        out_specs=VMEM,
        compiler_params=params(16),
        cost_estimate=pl.CostEstimate(
            flops=2 * 576 * CH * cells, bytes_accessed=4 * 576 * cells, transcendentals=576 * cells
        ),
        name="mix",
    )(enc_one, wt)

    trio = jnp.stack([flow, flow_a, flow_b])
    lon_x = lax.ppermute(trio, "lon", far_lon)
    lon_in = lax.all_gather(trio, "lon", axis_index_groups=chips)
    lanes = -(-(cells + 2 * cols) // 128) * 128
    return pl.pallas_call(
        functools.partial(up_kernel, rows, cols),
        out_shape=jax.ShapeDtypeStruct((2, rows * UP, cols * UP), F32),
        in_specs=[VMEM] * 6,
        out_specs=VMEM,
        scratch_shapes=[pltpu.VMEM((3, 2, lanes), F32)],
        compiler_params=params(16),
        name="upsample",
    )(mix, flow, flow_a, flow_b, lon_x, lon_in)


def solution(mesh):
    in_specs = (P("lat", "lon", None), P("lat", "lon", None), P(), P())
    return jax.shard_map(
        body, mesh=mesh, in_specs=in_specs, out_specs=P(None, "lat", "lon"), check_vma=False
    )
```

```python
import functools
import math

import jax
import jax.numpy as jnp
from jax import lax
from jax.experimental import pallas as pl
from jax.experimental.pallas import tpu as pltpu
from jax.sharding import PartitionSpec as P

CH = 256
BR = 8
BC = 16
UP = 8
F32 = jnp.float32
BF16 = jnp.bfloat16
VMEM = pl.BlockSpec(memory_space=pltpu.VMEM)


def params(mib):
    return pltpu.CompilerParams(vmem_limit_bytes=mib * 1024 * 1024)


def pair_perm(size, first, wrap):
    out = []
    for i in range(first, size, 2):
        j = i + 1
        if j >= size:
            if not wrap:
                continue
            j -= size
        out += [(i, j), (j, i)]
    return out


def edge_kernel(rows, cols, f1, f2, m_a, m_b, m_o, g1, g2, col, sems):
    odd = lax.axis_index("lat") % 2
    lon_odd = lax.axis_index("lon") % 2 == 1
    copies = [
        pltpu.make_async_copy(f2, g2, sems.at[4]),
        pltpu.make_async_copy(f1, g1, sems.at[5]),
    ]
    for k, (msg, low) in enumerate(((m_a, odd), (m_b, 1 - odd))):
        copies.append(
            pltpu.make_async_copy(
                f2.at[pl.ds(low * (rows - BR - 1), BR + 1)], msg.at[pl.ds(0, BR + 1)], sems.at[2 * k]
            )
        )
        copies.append(
            pltpu.make_async_copy(
                f1.at[pl.ds(low * (rows - 1), 1)], msg.at[pl.ds(BR + 1, 1)], sems.at[2 * k + 1]
            )
        )
    for copy in copies:
        copy.start()
    for copy in copies:
        copy.wait()

    def column(frame, at):
        lo = at // BC * BC
        slab = frame[:, lo : lo + BC].astype(F32)
        col[0:rows] = slab[:, at - lo, :]
        return col[...].astype(BF16).reshape(-1, BC, CH)

    def send(main, extra, one):
        m_o[0:rows] = g1[:, main : main + BC]
        m_o[rows : rows + col.shape[0] // BC] = column(g1, extra)
        m_o[rows + col.shape[0] // BC :] = column(g2, one)

    @pl.when(lon_odd)
    def _():
        send(cols - BC, cols - BC - 1, cols - 1)

    @pl.when(jnp.logical_not(lon_odd))
    def _():
        send(0, BC, 0)


def pack_kernel(rows, cols, f1, f2, ra, rb, m_c, m_in, ends, ext1, ext2, col):
    lat_odd = lax.axis_index("lat") % 2 == 1
    lon_odd = lax.axis_index("lon") % 2 == 1
    n2 = rows + 2 * BR + 2
    n1 = rows + 2
    nh = BR + 1
    slots2 = -(-n2 // BC)
    slots1 = -(-n1 // BC)

    def halo(north, south):
        ext2[0:nh] = north[0:nh]
        ext2[nh : nh + rows] = f2[...]
        ext2[nh + rows : n2] = south[0:nh]
        ext1[0] = north[nh]
        ext1[1 : 1 + rows] = f1[...]
        ext1[1 + rows] = south[nh]

    @pl.when(lat_odd)
    def _():
        halo(rb, ra)

    @pl.when(jnp.logical_not(lat_odd))
    def _():
        halo(ra, rb)

    def column(frame, lo, hi, at):
        base = at // BC * BC
        return frame[lo:hi, base : base + BC].astype(F32)[:, at - base, :]

    ends[0, 0:n1] = column(ext1, 0, n1, 0)
    ends[1, 0:n1] = column(ext1, 0, n1, cols - 1)

    def edge(msg, main, extra, one):
        msg[0:n1] = ext1[0:n1, main : main + BC]
        col[0:n1] = column(ext1, 0, n1, extra)
        msg[n1 : n1 + slots1] = col[0 : slots1 * BC].astype(BF16).reshape(slots1, BC, CH)
        col[0:n2] = column(ext2, 0, n2, one)
        msg[n1 + slots1 :] = col[0 : slots2 * BC].astype(BF16).reshape(slots2, BC, CH)

    def corner(msg, main, extra, one):
        msg[0] = ext1[0, main : main + BC]
        msg[1] = ext1[n1 - 1, main : main + BC]
        col[0:nh] = column(ext2, 0, nh, one)
        col[nh : 2 * nh] = column(ext2, n2 - nh, n2, one)
        col[2 * nh : 2 * nh + 1] = column(ext1, 0, 1, extra)
        col[2 * nh + 1 : 2 * nh + 2] = column(ext1, n1 - 1, n1, extra)
        msg[2:] = col[0 : 2 * BC].astype(BF16).reshape(2, BC, CH)

    right = (cols - BC, cols - BC - 1, cols - 1)
    left = (0, BC, 0)

    @pl.when(lon_odd)
    def _():
        corner(m_c, *right)
        edge(m_in, *left)

    @pl.when(jnp.logical_not(lon_odd))
    def _():
        corner(m_c, *left)
        edge(m_in, *right)


def conv(x, w, row, count, width):
    lhs = jnp.concatenate(
        [
            x[b, row + a : row + a + count].reshape(count * width, CH)
            for a in range(3)
            for b in range(3)
        ],
        axis=1,
    )
    return jnp.dot(lhs, w[...], preferred_element_type=F32)


def own_kernel(rows, cols, f1, f2, ra, rb, w, e2, e1, ends2, ends1, s2, s1, x2, x1):
    lat_odd = lax.axis_index("lat") % 2 == 1
    n2 = rows + 2 * BR + 2
    n1 = rows + 2

    def put_rows(north, south):
        s2[0 : BR + 1, BR : BR + cols] = north[0 : BR + 1].astype(F32)
        s2[BR + 1 + rows :, BR : BR + cols] = south[0 : BR + 1].astype(F32)
        s1[0, BR : BR + cols] = north[BR + 1].astype(F32)
        s1[n1 - 1, BR : BR + cols] = south[BR + 1].astype(F32)

    s2[BR + 1 : BR + 1 + rows, BR : BR + cols] = f2[...].astype(F32)
    s1[1 : 1 + rows, BR : BR + cols] = f1[...].astype(F32)

    @pl.when(lat_odd)
    def _():
        put_rows(rb, ra)

    @pl.when(jnp.logical_not(lat_odd))
    def _():
        put_rows(ra, rb)

    for s in (s2, s1):
        s[:, 0:BR] = jnp.zeros((s.shape[0], BR, CH), F32)
        s[:, BR + cols :] = jnp.zeros((s.shape[0], BR, CH), F32)
    for b in range(3):
        x2[b] = s2[:, BR - 1 + b : BR - 1 + b + cols].astype(BF16)
        x1[b] = s1[:, BR - 1 + b : BR - 1 + b + cols].astype(BF16)

    def run(x, out, ends, total):
        step = 2 * BR
        for r in range(0, total, step):
            acc = conv(x, w, r, step, cols).reshape(step, cols, CH)
            out[r : r + step] = acc.astype(BF16)
            ends[0, r : r + step] = acc[:, 0, :]
            ends[1, r : r + step] = acc[:, cols - 1, :]

    run(x1, e1, ends1, rows)
    run(x2, e2, ends2, rows + 2 * BR)


def finish_side(rows, cols, side, w, o2, o1, ends2, ends1, edges, ext, xs, rim, put):
    n1 = rows + 2
    tall = rows + 2 * BR
    place = lax.broadcasted_iota(jnp.int32, (1, BC, CH), 1)
    at = BR - 1 if side else BR + BC
    ext[:, at : at + 1] = edges[side, 0:n1][:, None, :]
    for b in range(3):
        xs[b] = ext[:, BR - 1 + b : BR - 1 + b + BC].astype(BF16)
    strip = conv(xs, w, 0, rows, BC).astype(BF16).reshape(rows, BC, CH)
    near = ext[:, BR : BR + 1] if side else ext[:, BR + BC - 1 : BR + BC]
    near = near[:, 0, :].astype(BF16)
    taps = jnp.concatenate(
        [w[(3 * a + 2 * side) * CH : (3 * a + 2 * side + 1) * CH] for a in range(3)], axis=0
    )
    lhs = jnp.concatenate(
        [jnp.concatenate([rim[a : a + tall], near[a : a + rows]], axis=0) for a in range(3)],
        axis=1,
    )
    more = jnp.dot(lhs, taps, preferred_element_type=F32)
    hit = place == (BC - 1 if side else 0)
    lo = cols - BC if side else 0
    full = ends2[side] + more[0:tall]
    two = jnp.where(hit, full[:, None, :], o2[:, lo : lo + BC].astype(F32)).astype(BF16)
    full = ends1[side] + more[tall : tall + rows]
    first = jnp.where(hit, full[:, None, :], o1[:, lo : lo + BC].astype(F32)).astype(BF16)
    put(side, strip, two, first)


def strip_kernel(rows, cols, o2, o1, ends2, ends1, edges, chip, w, strip, two, first, ext, xs):
    lon_odd = lax.axis_index("lon") % 2 == 1
    c_in = chip.at[1 - lax.axis_index("lon") % 2]
    n2 = rows + 2 * BR + 2
    n1 = rows + 2
    slots2 = -(-n2 // BC)
    slots1 = -(-n1 // BC)

    def put(side, *values):
        for ref, value in zip((strip, two, first), values):
            ref[...] = value

    def run(side):
        ext[:, BR : BR + BC] = c_in[0:n1].astype(F32)
        extra = c_in[n1 : n1 + slots1].astype(F32).reshape(slots1 * BC, CH)
        at = BR + BC if side else BR - 1
        ext[:, at : at + 1] = extra[0:n1][:, None, :]
        rim = c_in[n1 + slots1 :].astype(F32).reshape(slots2 * BC, CH)[0:n2].astype(BF16)
        finish_side(rows, cols, side, w, o2, o1, ends2, ends1, edges, ext, xs, rim, put)

    @pl.when(lon_odd)
    def _():
        run(0)

    @pl.when(jnp.logical_not(lon_odd))
    def _():
        run(1)


def score_kernel(
    rows, cols, o2, o1, ends2, ends1, edges, strip_in, two_in, first_in, c_o, c_c, w,
    sums, enc_one, ext, xs, col, e2, beside,
):
    lat = lax.axis_index("lat")
    lon_odd = lax.axis_index("lon") % 2 == 1
    n2 = rows + 2 * BR + 2
    n1 = rows + 2
    nh = BR + 1
    pads = (c_o.shape[0] - rows) // 2

    def put(side, strip, two, first):
        lo = cols - BC if side else 0
        e2[:, lo : lo + BC] = two
        enc_one[:, lo : lo + BC] = first
        lo = 0 if side else cols - BC
        beside[:, lo : lo + BC] = strip

    def run(side):
        put(1 - side, strip_in[...], two_in[...], first_in[...])
        far = c_c[2:].astype(F32).reshape(2 * BC, CH)
        mine = c_o[rows : rows + pads].astype(F32).reshape(pads * BC, CH)
        at = BR + BC if side else BR - 1
        ext[0, BR : BR + BC] = c_c[0].astype(F32)
        ext[1 : 1 + rows, BR : BR + BC] = c_o[0:rows].astype(F32)
        ext[1 + rows, BR : BR + BC] = c_c[1].astype(F32)
        ext[0:1, at : at + 1] = far[2 * nh : 2 * nh + 1][:, None, :]
        ext[1 : 1 + rows, at : at + 1] = mine[0:rows][:, None, :]
        ext[1 + rows : n1, at : at + 1] = far[2 * nh + 1 : 2 * nh + 2][:, None, :]
        mine = c_o[rows + pads :].astype(F32).reshape(pads * BC, CH)
        col[0:nh] = far[0:nh]
        col[nh : nh + rows] = mine[0:rows]
        col[nh + rows : n2] = far[nh : 2 * nh]
        rim = col[0:n2].astype(BF16)
        finish_side(rows, cols, side, w, o2, o1, ends2, ends1, edges, ext, xs, rim, put)

    @pl.when(lon_odd)
    def _():
        run(1)

    @pl.when(jnp.logical_not(lon_odd))
    def _():
        run(0)

    bands = rows // BR
    queries = BR * cols
    shape = (BR, queries)
    sub = lax.broadcasted_iota(jnp.int32, shape, 0).astype(F32)
    of_right = lax.broadcasted_iota(jnp.int32, shape, 1) % cols < BC
    base = jnp.where(of_right, float(BC - cols), float(cols))
    last = lax.axis_size("lat") - 1
    scale = 1.0 / math.sqrt(CH)
    for g in range(bands):
        band = slice(g * BR, g * BR + BR)
        query = [
            (r[band].reshape(queries, CH).astype(F32) * scale).astype(BF16)
            for r in (enc_one, beside)
        ]
        acc = None
        for kb in range(3):
            keys = e2[(g + kb) * BR : (g + kb + 1) * BR].reshape(queries, CH)
            mine, other = (
                lax.dot_general(
                    keys, q, (((1,), (1,)), ((), ())), preferred_element_type=F32
                ).reshape(BR, cols // BR, BR, queries)
                for q in query
            )
            part = None
            for kr in range(BR):
                own = [jnp.exp(mine[kr, i]) for i in range(4)]
                ext_e = [
                    jnp.exp(jnp.where(of_right, other[kr, 2 + i], other[kr, i])) for i in range(2)
                ]
                row = float((kb - 1) * BR + kr)
                now = own + [row * ((own[0] + own[1]) + (own[2] + own[3]))]
                now += ext_e + [row * (ext_e[0] + ext_e[1])]
                part = now if part is None else [p + e for p, e in zip(part, now)]
            if kb == 0 and g == 0:
                part = [jnp.where(lat > 0, p, 0.0) for p in part]
            elif kb == 2 and g == bands - 1:
                part = [jnp.where(lat < last, p, 0.0) for p in part]
            acc = part if acc is None else [s + p for s, p in zip(acc, part)]
        mass = (acc[0] + acc[1]) + (acc[2] + acc[3])
        mass_b = acc[5] + acc[6]
        values = [
            mass,
            acc[4],
            (acc[1] + 2.0 * acc[2] + 3.0 * acc[3]) * 8.0 + mass * sub,
            mass_b,
            acc[7],
            acc[6] * 8.0 + mass_b * (sub + base),
        ]
        values = [jnp.sum(v, axis=0, keepdims=True) for v in values]
        values += [jnp.zeros((2, queries), F32)]
        sums[:, g * queries : (g + 1) * queries] = jnp.concatenate(values, axis=0)


def combine_kernel(rows, cols, mine, far, chip, _, fields):
    lon_odd = lax.axis_index("lon") % 2
    cells = rows * cols
    lane = lax.broadcasted_iota(jnp.int32, (1, cells), 1)
    column = lane % cols
    row = (lane // cols % BR).astype(F32)
    partner = chip[1 - lon_odd]
    is_odd = jnp.broadcast_to(lon_odd == 1, partner.shape)
    left = jnp.where(is_odd, partner, far[...])
    right = jnp.where(is_odd, far[...], partner)
    own = mine[...]

    def flow(total):
        return jnp.concatenate(
            [total[1:2] / total[0:1] - row, total[2:3] / total[0:1] - column.astype(F32)], axis=0
        ) * float(UP)

    mid = flow(own[0:3] + jnp.where(column < BC, left[3:6], right[3:6]))
    west = flow(left[0:3] + own[3:6])
    east = flow(right[0:3] + own[3:6])
    fields[0:2] = jnp.where(
        column == 0, pltpu.roll(west, cells - (cols - 1), 1), pltpu.roll(mid, 1, 1)
    )
    fields[2:4] = mid
    fields[4:6] = jnp.where(
        column == cols - 1, pltpu.roll(east, cols - 1, 1), pltpu.roll(mid, cells - 1, 1)
    )
    fields[6:8] = jnp.zeros((2, cells), F32)


def mix_kernel(cells, enc_one, wt, mix):
    feats = enc_one[...].reshape(cells, CH)
    step = 256
    for c0 in range(0, cells, step):
        for k in range(UP):
            wk = jnp.concatenate(
                [wt[n * 64 + k * UP : n * 64 + k * UP + UP] for n in range(9)], axis=0
            )
            logits = lax.dot_general(
                wk, feats[c0 : c0 + step], (((1,), (1,)), ((), ())), preferred_element_type=F32
            )
            expo = jnp.exp(logits).reshape(9, UP, step)
            total = jnp.sum(expo, axis=0)
            mix[:, k, :, c0 : c0 + step] = expo / total[None]


def lane_order(cols):
    src = lax.broadcasted_iota(jnp.int32, (UP * cols, UP * cols), 0)
    dst = lax.broadcasted_iota(jnp.int32, (UP * cols, UP * cols), 1)
    return jnp.where((dst // UP == src % cols) & (dst % UP == src // cols), 1.0, 0.0).astype(BF16)


def reorder(value, order):
    high = value.astype(BF16)
    low = (value - high.astype(F32)).astype(BF16)
    return jnp.dot(high, order, preferred_element_type=F32) + jnp.dot(
        low, order, preferred_element_type=F32
    )


def up_kernel(rows, cols, mix, fields, out, rim):
    cells = rows * cols
    lane = lax.broadcasted_iota(jnp.int32, (1, cells), 1)
    field = fields[...]
    north = jnp.where(lane < cols, 0.0, pltpu.roll(field, cols, 1))
    south = jnp.where(lane >= cells - cols, 0.0, pltpu.roll(field, cells - cols, 1))
    shifted = [(v, 2 * b) for v in (north, field, south) for b in range(3)]
    order = lane_order(cols)
    tile = 128
    group = tile // cols
    lane = lax.broadcasted_iota(jnp.int32, (UP, tile), 1)
    bits = []
    span = 1
    while span < group:
        bits.append((span, (lane // (span * cols)) % 2 == 1))
        span *= 2
    for d in range(2):
        lanes_of = [[None] * (UP // group) for _ in range(rows)]
        for t in range(cells // tile):
            flows = [
                jnp.broadcast_to(v[k + d : k + d + 1, t * tile : (t + 1) * tile], (UP, tile))
                for v, k in shifted
            ]
            for u in range(UP // group):
                block = []
                for k in range(group):
                    acc = None
                    for n in range(9):
                        term = mix[n, u * group + k, :, t * tile : (t + 1) * tile] * flows[n]
                        acc = term if acc is None else acc + term
                    block.append(acc)
                for span, high in bits:
                    shift = span * cols
                    done = list(block)
                    for k in range(group):
                        if k & span:
                            continue
                        lo_v, hi_v = block[k], block[k | span]
                        done[k] = jnp.where(high, pltpu.roll(hi_v, shift, 1), lo_v)
                        done[k | span] = jnp.where(
                            high, hi_v, pltpu.roll(lo_v, tile - shift, 1)
                        )
                    block = done
                for k in range(group):
                    lanes_of[t * group + k][u] = block[k]
        value = jnp.concatenate([jnp.concatenate(v, axis=1) for v in lanes_of], axis=0)
        value = reorder(value, order)
        out[d] = value
        rim[2 * d] = value[0:UP]
        rim[2 * d + 1] = value[(rows - 1) * UP :]


def rim_kernel(rows, cols, mix, flow_a, flow_b, rim, _, out, done, sems):
    lat_odd = lax.axis_index("lat") % 2 == 1
    cells = rows * cols
    tile = 128
    group = tile // cols
    lane = lax.broadcasted_iota(jnp.int32, (UP, tile), 1) // cols
    a, b = flow_a[...], flow_b[...]
    odd = jnp.broadcast_to(lat_odd, a.shape)
    north = jnp.where(odd, b, a)[:, cells - tile :]
    south = jnp.where(odd, a, b)[:, 0:tile]
    north = pltpu.roll(north, cols, 1)
    south = pltpu.roll(south, tile - cols, 1)
    pieces = []
    for d in range(2):
        for field, first, at, slot in (
            (north, 0, 0, 0),
            (south, 6, cells - tile, group - 1),
        ):
            flows = [
                jnp.broadcast_to(field[2 * k + d : 2 * k + d + 1], (UP, tile)) for k in range(3)
            ]
            halves = []
            for u in range(UP // group):
                whole = None
                for k in range(group):
                    acc = None
                    for n in range(3):
                        term = mix[first + n, u * group + k, :, at : at + tile] * flows[n]
                        acc = term if acc is None else acc + term
                    moved = acc if k == slot else pltpu.roll(acc, (k - slot) * cols % tile, 1)
                    whole = moved if whole is None else jnp.where(lane == k, moved, whole)
                halves.append(whole)
            pieces.append(jnp.concatenate(halves, axis=1))
    value = reorder(jnp.concatenate(pieces, axis=0), lane_order(cols))
    copies = []
    for k in range(4):
        done[k] = rim[k] + value[k * UP : (k + 1) * UP]
        copies.append(
            pltpu.make_async_copy(
                done.at[k],
                out.at[k // 2, pl.ds((k % 2) * (rows - 1) * UP, UP)],
                sems.at[k],
            )
        )
    for copy in copies:
        copy.start()
    for copy in copies:
        copy.wait()


def body(frame_one, frame_two, enc_weight, mask_weight):
    rows, cols = frame_one.shape[0], frame_one.shape[1]
    cells = rows * cols
    n2, n1 = rows + 2 * BR + 2, rows + 2
    slots = n1 + -(-n2 // BC) + -(-n1 // BC)
    own_slots = rows + 2 * -(-rows // BC)
    lats, lons = lax.axis_size("lat"), lax.axis_size("lon")
    far_lat = pair_perm(lats, 1, False)
    near_lat = pair_perm(lats, 0, False)
    far_lon = pair_perm(lons, 1, True)
    chips = [[i, i + 1] for i in range(0, lons, 2)]

    edge_rows = jax.ShapeDtypeStruct((BR + 2, cols, CH), BF16)
    tile = jax.ShapeDtypeStruct((rows, cols, CH), BF16)
    m_a, m_b, m_o, one, two = pl.pallas_call(
        functools.partial(edge_kernel, rows, cols),
        out_shape=(edge_rows, edge_rows, jax.ShapeDtypeStruct((own_slots, BC, CH), BF16), tile, tile),
        in_specs=[pl.BlockSpec(memory_space=pltpu.MemorySpace.HBM)] * 2,
        out_specs=(VMEM,) * 5,
        scratch_shapes=[
            pltpu.VMEM((-(-rows // BC) * BC, CH), F32),
            pltpu.SemaphoreType.DMA((6,)),
        ],
        compiler_params=params(8),
        name="edges",
    )(
        pltpu.with_memory_space_constraint(frame_one, pltpu.MemorySpace.HBM),
        pltpu.with_memory_space_constraint(frame_two, pltpu.MemorySpace.HBM),
    )
    row_a = lax.ppermute(m_a, "lat", far_lat)
    row_b = lax.ppermute(m_b, "lat", near_lat)
    col_o = lax.ppermute(m_o, "lon", far_lon)

    n2_pad = -(-n2 // BC) * BC
    m_c, m_in, edges = pl.pallas_call(
        functools.partial(pack_kernel, rows, cols),
        out_shape=(
            jax.ShapeDtypeStruct((4, BC, CH), BF16),
            jax.ShapeDtypeStruct((slots, BC, CH), BF16),
            jax.ShapeDtypeStruct((2, -(-n1 // BR) * BR, CH), F32),
        ),
        in_specs=[VMEM] * 4,
        out_specs=(VMEM,) * 3,
        scratch_shapes=[
            pltpu.VMEM((n1, cols, CH), BF16),
            pltpu.VMEM((n2, cols, CH), BF16),
            pltpu.VMEM((n2_pad, CH), F32),
        ],
        compiler_params=params(16),
        name="pack",
    )(one, two, row_a, row_b)
    col_c = lax.ppermute(m_c, "lon", far_lon)
    col_in = lax.all_gather(m_in, "lon", axis_index_groups=chips)

    tall = rows + 2 * BR
    weight = enc_weight.reshape(9 * CH, CH)
    own_two, own_one, ends_two, ends_one = pl.pallas_call(
        functools.partial(own_kernel, rows, cols),
        out_shape=(
            jax.ShapeDtypeStruct((tall, cols, CH), BF16),
            jax.ShapeDtypeStruct((rows, cols, CH), BF16),
            jax.ShapeDtypeStruct((2, tall, CH), F32),
            jax.ShapeDtypeStruct((2, rows, CH), F32),
        ),
        in_specs=[VMEM] * 5,
        out_specs=(VMEM,) * 4,
        scratch_shapes=[
            pltpu.VMEM((n2, cols + 2 * BR, CH), F32),
            pltpu.VMEM((n1, cols + 2 * BR, CH), F32),
            pltpu.VMEM((3, n2, cols, CH), BF16),
            pltpu.VMEM((3, n1, cols, CH), BF16),
        ],
        compiler_params=params(20),
        cost_estimate=pl.CostEstimate(
            flops=2 * 9 * CH * CH * cols * (tall + rows), bytes_accessed=4 << 20, transcendentals=0
        ),
        name="encode_own",
    )(one, two, row_a, row_b, weight)

    queries = jax.ShapeDtypeStruct((rows, BC, CH), BF16)
    side_scratch = [
        pltpu.VMEM((n1, BC + 2 * BR, CH), F32),
        pltpu.VMEM((3, n1, BC, CH), BF16),
    ]
    strip_in, two_in, first_in = pl.pallas_call(
        functools.partial(strip_kernel, rows, cols),
        out_shape=(queries, jax.ShapeDtypeStruct((tall, BC, CH), BF16), queries),
        in_specs=[VMEM] * 7,
        out_specs=(VMEM,) * 3,
        scratch_shapes=side_scratch,
        compiler_params=params(16),
        cost_estimate=pl.CostEstimate(
            flops=2 * 9 * CH * CH * BC * tall, bytes_accessed=4 << 20, transcendentals=0
        ),
        name="strip",
    )(own_two, own_one, ends_two, ends_one, edges, col_in, weight)

    lanes = jax.ShapeDtypeStruct((8, cells), F32)
    sums, enc_one = pl.pallas_call(
        functools.partial(score_kernel, rows, cols),
        out_shape=(lanes, tile),
        in_specs=[VMEM] * 11,
        out_specs=(VMEM, VMEM),
        scratch_shapes=side_scratch
        + [
            pltpu.VMEM((n2_pad, CH), F32),
            pltpu.VMEM((tall, cols, CH), BF16),
            pltpu.VMEM((rows, cols, CH), BF16),
        ],
        compiler_params=params(20),
        name="score",
    )(
        own_two, own_one, ends_two, ends_one, edges, strip_in, two_in, first_in, col_o, col_c, weight
    )
    sums_far = lax.ppermute(sums, "lon", far_lon)
    sums_in = lax.all_gather(sums, "lon", axis_index_groups=chips)

    wt = mask_weight.reshape(CH, 9, UP, UP).transpose(1, 3, 2, 0).reshape(9 * UP * UP, CH)
    mix = pl.pallas_call(
        functools.partial(mix_kernel, cells),
        out_shape=jax.ShapeDtypeStruct((9, UP, UP, cells), F32),
        in_specs=[VMEM] * 2,
        out_specs=VMEM,
        compiler_params=params(16),
        cost_estimate=pl.CostEstimate(
            flops=2 * 576 * CH * cells, bytes_accessed=4 * 576 * cells, transcendentals=576 * cells
        ),
        name="mix",
    )(enc_one, wt)

    fields = pl.pallas_call(
        functools.partial(combine_kernel, rows, cols),
        out_shape=lanes,
        in_specs=[VMEM] * 3 + [pl.BlockSpec(memory_space=pl.ANY)],
        out_specs=VMEM,
        compiler_params=params(8),
        name="combine",
    )(sums, sums_far, sums_in, mix)
    flow_a = lax.ppermute(fields, "lat", far_lat)
    flow_b = lax.ppermute(fields, "lat", near_lat)

    fine = jax.ShapeDtypeStruct((2, rows * UP, cols * UP), F32)
    whole, rim = pl.pallas_call(
        functools.partial(up_kernel, rows, cols),
        out_shape=(fine, jax.ShapeDtypeStruct((4, UP, cols * UP), F32)),
        in_specs=[VMEM] * 2,
        out_specs=(VMEM, VMEM),
        compiler_params=params(16),
        cost_estimate=pl.CostEstimate(
            flops=2 * 576 * CH * cells, bytes_accessed=4 * 576 * cells, transcendentals=0
        ),
        name="upsample",
    )(mix, fields)
    return pl.pallas_call(
        functools.partial(rim_kernel, rows, cols),
        out_shape=fine,
        in_specs=[VMEM] * 4 + [pl.BlockSpec(memory_space=pl.ANY)],
        out_specs=pl.BlockSpec(memory_space=pl.ANY),
        scratch_shapes=[
            pltpu.VMEM((4, UP, cols * UP), F32),
            pltpu.SemaphoreType.DMA((4,)),
        ],
        input_output_aliases={4: 0},
        compiler_params=params(8),
        name="rim",
    )(mix, flow_a, flow_b, rim, whole)


def solution(mesh):
    in_specs = (P("lat", "lon", None), P("lat", "lon", None), P(), P())
    return jax.shard_map(
        body, mesh=mesh, in_specs=in_specs, out_specs=P(None, "lat", "lon"), check_vma=False
    )
```

```python
import functools
import math

import jax
import jax.numpy as jnp
from jax import lax
from jax.experimental import pallas as pl
from jax.experimental.pallas import tpu as pltpu
from jax.sharding import PartitionSpec as P

CH = 256
BR = 8
BC = 16
UP = 8
F32 = jnp.float32
BF16 = jnp.bfloat16
VMEM = pl.BlockSpec(memory_space=pltpu.VMEM)


def params(mib):
    return pltpu.CompilerParams(vmem_limit_bytes=mib * 1024 * 1024)


def pair_perm(size, first, wrap, apart=1):
    out = []
    for i in range(size):
        if (i - first) % (2 * apart) >= apart:
            continue
        j = i + apart
        if j >= size:
            if not wrap:
                continue
            j -= size
        out += [(i, j), (j, i)]
    return out


def edge_kernel(rows, cols, f1, f2, m_a, m_b, m_c, m_d, g1, g2, sems):
    band = lax.axis_index("lat")
    odd = band % 2
    upper = band % 4 // 2
    copies = [
        pltpu.make_async_copy(f2, g2, sems.at[0]),
        pltpu.make_async_copy(f1, g1, sems.at[1]),
    ]
    for k, (msg, low) in enumerate(((m_a, odd), (m_b, 1 - odd))):
        copies.append(
            pltpu.make_async_copy(f2, msg.at[pl.ds(0, rows)], sems.at[2 + 2 * k])
        )
        copies.append(
            pltpu.make_async_copy(
                f1.at[pl.ds(low * (rows - 2), 2)], msg.at[pl.ds(rows, 2)], sems.at[3 + 2 * k]
            )
        )
    for k, (msg, low) in enumerate(((m_c, upper), (m_d, 1 - upper))):
        copies.append(
            pltpu.make_async_copy(f2.at[pl.ds(low * (rows - 1), 1)], msg, sems.at[6 + k])
        )
    for copy in copies:
        copy.start()
    for copy in copies:
        copy.wait()


def by_parity(lat_run, ra, rb, rc, rd):
    band = lax.axis_index("lat")
    for odd in (0, 1):
        for upper in (0, 1):

            @pl.when((band % 2 == odd) & (band % 4 // 2 == upper))
            def _():
                pair = (rb, ra) if odd else (ra, rb)
                lat_run(*pair, *((rd, rc) if upper else (rc, rd)))


def edge(msg, main_cols, extra, rim, col):
    n1, n2 = main_cols.shape[0], rim.shape[0]
    slots1, slots2 = -(-n1 // BC), -(-n2 // BC)
    msg[0:n1] = main_cols
    col[0:n1] = extra
    msg[n1 : n1 + slots1] = col[0 : slots1 * BC].astype(BF16).reshape(slots1, BC, CH)
    col[0:n2] = rim
    msg[n1 + slots1 :] = col[0 : slots2 * BC].astype(BF16).reshape(slots2, BC, CH)


def edge_places(cols, right):
    return (cols - BC, cols - BC - 1, cols - 1) if right else (0, BC, 0)


def pack_kernel(rows, cols, f1, f2, ra, rb, rc, rd, m_x, ext1, ext2, col):
    lon_odd = lax.axis_index("lon") % 2
    n2 = 3 * rows + 2
    n1 = rows + 4

    def halo(north, south, north_far, south_far):
        ext2[0:1] = north_far[...]
        ext2[1 : 1 + rows] = north[0:rows]
        ext2[1 + 2 * rows : 1 + 3 * rows] = south[0:rows]
        ext2[n2 - 1 : n2] = south_far[...]
        ext1[0:2] = north[rows : rows + 2]
        ext1[n1 - 2 : n1] = south[rows : rows + 2]

    ext2[1 + rows : 1 + 2 * rows] = f2[...]
    ext1[2 : 2 + rows] = f1[...]
    by_parity(halo, ra, rb, rc, rd)

    def column(frame, at):
        base = at // BC * BC
        return frame[:, base : base + BC].astype(F32)[:, at - base, :]

    for odd in (0, 1):

        @pl.when(lon_odd == odd)
        def _():
            main, extra, one = edge_places(cols, odd == 1)
            edge(m_x, ext1[:, main : main + BC], column(ext1, extra), column(ext2, one), col)


def conv(x, w, row, count, width):
    lhs = jnp.concatenate(
        [
            x[b, row + a : row + a + count].reshape(count * width, CH)
            for a in range(3)
            for b in range(3)
        ],
        axis=1,
    )
    return jnp.dot(lhs, w[...], preferred_element_type=F32)


def own_kernel(
    rows, cols, f1, f2, ra, rb, rc, rd, w, e2, e1, ends2, ends1, m_in, edges, s2, s1, x2, x1, col
):
    lon_odd = lax.axis_index("lon") % 2
    n2 = 3 * rows + 2
    n1 = rows + 4
    own = slice(BR, BR + cols)

    def halo(north, south, north_far, south_far):
        s2[0:1, own] = north_far[...].astype(F32)
        s2[1 : 1 + rows, own] = north[0:rows].astype(F32)
        s2[1 + 2 * rows : 1 + 3 * rows, own] = south[0:rows].astype(F32)
        s2[n2 - 1 : n2, own] = south_far[...].astype(F32)
        s1[0:2, own] = north[rows : rows + 2].astype(F32)
        s1[n1 - 2 : n1, own] = south[rows : rows + 2].astype(F32)

    s2[1 + rows : 1 + 2 * rows, own] = f2[...].astype(F32)
    s1[2 : 2 + rows, own] = f1[...].astype(F32)
    by_parity(halo, ra, rb, rc, rd)
    for s in (s2, s1):
        s[:, 0:BR] = jnp.zeros((s.shape[0], BR, CH), F32)
        s[:, BR + cols :] = jnp.zeros((s.shape[0], BR, CH), F32)
    for b in range(3):
        x2[b] = s2[:, BR - 1 + b : BR - 1 + b + cols].astype(BF16)
        x1[b] = s1[:, BR - 1 + b : BR - 1 + b + cols].astype(BF16)

    def run(x, out, ends, total):
        for r in range(0, total, 2 * BR):
            step = min(2 * BR, total - r)
            acc = conv(x, w, r, step, cols).reshape(step, cols, CH)
            out[r : r + step] = acc.astype(BF16)
            ends[0, r : r + step] = acc[:, 0, :]
            ends[1, r : r + step] = acc[:, cols - 1, :]

    run(x1, e1, ends1, rows + 2)
    run(x2, e2, ends2, 3 * rows)
    edges[0, 0:n1] = s1[:, BR, :]
    edges[1, 0:n1] = s1[:, BR + cols - 1, :]
    for odd in (0, 1):

        @pl.when(lon_odd == odd)
        def _():
            main, extra, one = edge_places(cols, odd == 0)
            edge(m_in, x1[1, :, main : main + BC], s1[:, BR + extra, :], s2[:, BR + one, :], col)


def finish_side(rows, cols, side, msg, w, o2, o1, ends2, ends1, edges, ext, xs, put):
    n2 = 3 * rows + 2
    n1 = rows + 4
    slots2 = -(-n2 // BC)
    slots1 = -(-n1 // BC)
    few, tall = rows + 2, 3 * rows
    extra = msg[n1 : n1 + slots1].astype(F32).reshape(slots1 * BC, CH)[0:n1]
    rim = msg[n1 + slots1 :].astype(F32).reshape(slots2 * BC, CH)[0:n2].astype(BF16)
    inner = edges[side, 0:n1]
    ext[:, BR : BR + BC] = msg[0:n1].astype(F32)
    ext[:, BR - 1 : BR] = (inner if side else extra)[:, None, :]
    ext[:, BR + BC : BR + BC + 1] = (extra if side else inner)[:, None, :]
    for b in range(3):
        xs[b] = ext[:, BR - 1 + b : BR - 1 + b + BC].astype(BF16)
    strip = conv(xs, w, 0, few, BC).astype(BF16).reshape(few, BC, CH)
    near = ext[:, BR : BR + 1] if side else ext[:, BR + BC - 1 : BR + BC]
    near = near[:, 0, :].astype(BF16)
    taps = jnp.concatenate(
        [w[(3 * a + 2 * side) * CH : (3 * a + 2 * side + 1) * CH] for a in range(3)], axis=0
    )
    lhs = jnp.concatenate(
        [jnp.concatenate([rim[a : a + tall], near[a : a + few]], axis=0) for a in range(3)],
        axis=1,
    )
    more = jnp.dot(lhs, taps, preferred_element_type=F32)
    hit = lax.broadcasted_iota(jnp.int32, (1, BC, CH), 1) == (BC - 1 if side else 0)
    lo = cols - BC if side else 0
    full = ends2[side, 0:tall] + more[0:tall]
    two = jnp.where(hit, full[:, None, :], o2[:, lo : lo + BC].astype(F32)).astype(BF16)
    full = ends1[side, 0:few] + more[tall : tall + few]
    first = jnp.where(hit, full[:, None, :], o1[:, lo : lo + BC].astype(F32)).astype(BF16)
    put(side, strip, two, first)


def strip_kernel(rows, cols, o2, o1, ends2, ends1, edges, chip, w, strip, two, first, ext, xs):
    lon_odd = lax.axis_index("lon") % 2
    msg = chip.at[1 - lon_odd]

    def put(side, *values):
        for ref, value in zip((strip, two, first), values):
            ref[...] = value

    for odd in (0, 1):

        @pl.when(lon_odd == odd)
        def _():
            finish_side(rows, cols, 1 - odd, msg, w, o2, o1, ends2, ends1, edges, ext, xs, put)


def score_kernel(
    rows, cols, o2, o1, ends2, ends1, edges, strip_in, two_in, first_in, c_x, w,
    sums, enc_one, ext, xs, e2, beside,
):
    lat = lax.axis_index("lat")
    lon_odd = lax.axis_index("lon") % 2

    def put(side, strip, two, first):
        lo = cols - BC if side else 0
        e2[:, lo : lo + BC] = two
        enc_one[:, lo : lo + BC] = first
        lo = 0 if side else cols - BC
        beside[:, lo : lo + BC] = strip

    for odd in (0, 1):

        @pl.when(lon_odd == odd)
        def _():
            put(1 - odd, strip_in[...], two_in[...], first_in[...])
            finish_side(rows, cols, odd, c_x, w, o2, o1, ends2, ends1, edges, ext, xs, put)

    bands = rows // BR
    last = lax.axis_size("lat") - 1
    scale = 1.0 / math.sqrt(CH)
    groups = cols // BR

    def features(ref, row, count):
        flat = ref[row : row + count].reshape(count * cols, CH).astype(F32)
        return (flat * scale).astype(BF16)

    def scores(block, query):
        keys = e2[block * BR : (block + 1) * BR].reshape(BR * cols, CH)
        return lax.dot_general(
            keys, query, (((1,), (1,)), ((), ())), preferred_element_type=F32
        ).reshape(BR, groups, BR, query.shape[0])

    def add(total, now):
        return now if total is None else [p + e for p, e in zip(total, now)]

    def triple(pieces, by_row, sub, base):
        mass = pieces[0]
        octs = None
        for i, piece in enumerate(pieces[1:], 1):
            mass = mass + piece
            octs = piece * float(i) if octs is None else octs + piece * float(i)
        across = octs * 8.0 + mass * (sub if base is None else sub + base)
        return [jnp.sum(v, axis=0, keepdims=True) for v in (mass, by_row, across)]

    queries = BR * cols
    sub = lax.broadcasted_iota(jnp.int32, (BR, queries), 0).astype(F32)
    of_right = lax.broadcasted_iota(jnp.int32, (BR, queries), 1) % cols < BC
    base = jnp.where(of_right, float(BC - cols), float(cols))
    for g in range(bands):
        query_own = features(enc_one, 1 + g * BR, BR)
        query_side = features(beside, 1 + g * BR, BR)
        acc = None
        for kb in range(3):
            mine = scores(g + kb + 1, query_own)
            other = scores(g + kb + 1, query_side)
            part = None
            for kr in range(BR):
                row = float((kb - 1) * BR + kr)
                own = [jnp.exp(mine[kr, i]) for i in range(4)]
                side = [
                    jnp.exp(jnp.where(of_right, other[kr, 2 + i], other[kr, i])) for i in range(2)
                ]
                now = own + [row * ((own[0] + own[1]) + (own[2] + own[3]))]
                now += side + [row * (side[0] + side[1])]
                part = add(part, now)
            if kb == 0 and g == 0:
                part = [jnp.where(lat > 0, p, 0.0) for p in part]
            elif kb == 2 and g == bands - 1:
                part = [jnp.where(lat < last, p, 0.0) for p in part]
            acc = add(acc, part)
        values = triple(acc[0:4], acc[4], sub, None) + triple(acc[5:7], acc[7], sub, base)
        values += [jnp.zeros((2, queries), F32)]
        sums[:, cols + g * queries : cols + (g + 1) * queries] = jnp.concatenate(values, axis=0)

    lanes = 2 * cols
    sub = lax.broadcasted_iota(jnp.int32, (BR, lanes), 0).astype(F32)
    lane = lax.broadcasted_iota(jnp.int32, (BR, lanes), 1)
    is_own = lane < cols
    of_right = (lane >= cols) & (lane < cols + BC)
    base = jnp.where(is_own, 0.0, jnp.where(of_right, float(BC - cols), float(cols)))
    for row_at, first, at in ((0, 0, 0), (rows + 1, bands + 1, cols + rows * cols)):
        query = jnp.concatenate([features(enc_one, row_at, 1), features(beside, row_at, 1)], axis=0)
        acc = None
        for kb in range(3):
            both = scores(first + kb, query)
            for kr in range(BR):
                row = float((kb - 1) * BR + kr)
                now = [
                    jnp.exp(jnp.where(of_right, both[kr, 2 + i], both[kr, i])) for i in range(2)
                ]
                now += [jnp.where(is_own, jnp.exp(both[kr, i]), 0.0) for i in range(2, 4)]
                now += [row * ((now[0] + now[1]) + (now[2] + now[3]))]
                acc = add(acc, now)
        values = triple(acc[0:4], acc[4], sub, base)
        sums[0:3, at : at + cols] = jnp.concatenate([v[:, 0:cols] for v in values], axis=0)
        sums[3:6, at : at + cols] = jnp.concatenate([v[:, cols:] for v in values], axis=0)
        sums[6:8, at : at + cols] = jnp.zeros((2, cols), F32)


def mix_kernel(rows, cells, enc_one, wt, mix):
    feats = enc_one[1 : 1 + rows].reshape(cells, CH)
    step = 256
    for c0 in range(0, cells, step):
        for k in range(UP):
            wk = jnp.concatenate(
                [wt[n * 64 + k * UP : n * 64 + k * UP + UP] for n in range(9)], axis=0
            )
            logits = lax.dot_general(
                wk, feats[c0 : c0 + step], (((1,), (1,)), ((), ())), preferred_element_type=F32
            )
            expo = jnp.exp(logits).reshape(9, UP, step)
            total = jnp.sum(expo, axis=0)
            mix[:, k, :, c0 : c0 + step] = expo / total[None]


def up_kernel(rows, cols, mine, far, chip, mix, out):
    lat = lax.axis_index("lat")
    last = lax.axis_size("lat") - 1
    lon_odd = lax.axis_index("lon") % 2
    cells = rows * cols
    width = mine.shape[1]
    lane = lax.broadcasted_iota(jnp.int32, (1, width), 1)
    column = lane % cols
    row = ((lane // cols + BR - 1) % BR).astype(F32)
    outside = ((lane < cols) & (lat == 0)) | ((lane >= cols + cells) & (lat == last))
    partner = chip[1 - lon_odd]
    is_odd = jnp.broadcast_to(lon_odd == 1, partner.shape)
    left = jnp.where(is_odd, partner, far[...])
    right = jnp.where(is_odd, far[...], partner)
    own = mine[...]

    def flow(total):
        both = jnp.concatenate(
            [total[1:2] / total[0:1] - row, total[2:3] / total[0:1] - column.astype(F32)], axis=0
        )
        return jnp.where(outside, 0.0, both * float(UP))

    mid = flow(own[0:3] + jnp.where(column < BC, left[3:6], right[3:6]))
    west = flow(left[0:3] + own[3:6])
    east = flow(right[0:3] + own[3:6])
    west = jnp.where(
        column == 0, pltpu.roll(west, width - (cols - 1), 1), pltpu.roll(mid, 1, 1)
    )
    east = jnp.where(
        column == cols - 1, pltpu.roll(east, cols - 1, 1), pltpu.roll(mid, width - 1, 1)
    )
    shifted = []
    for a in range(3):
        for field in (west, mid, east):
            moved = field if a == 0 else pltpu.roll(field, width - a * cols, 1)
            shifted.append(moved[:, 0:cells])
    src = lax.broadcasted_iota(jnp.int32, (UP * cols, UP * cols), 0)
    dst = lax.broadcasted_iota(jnp.int32, (UP * cols, UP * cols), 1)
    order = jnp.where((dst // UP == src % cols) & (dst % UP == src // cols), 1.0, 0.0).astype(BF16)
    tile = 128
    group = tile // cols
    lane = lax.broadcasted_iota(jnp.int32, (UP, tile), 1)
    bits = []
    span = 1
    while span < group:
        bits.append((span, (lane // (span * cols)) % 2 == 1))
        span *= 2
    for d in range(2):
        lanes_of = [[None] * (UP // group) for _ in range(rows)]
        for t in range(cells // tile):
            flows = [
                jnp.broadcast_to(v[d : d + 1, t * tile : (t + 1) * tile], (UP, tile))
                for v in shifted
            ]
            for u in range(UP // group):
                block = []
                for k in range(group):
                    acc = None
                    for n in range(9):
                        term = mix[n, u * group + k, :, t * tile : (t + 1) * tile] * flows[n]
                        acc = term if acc is None else acc + term
                    block.append(acc)
                for span, high in bits:
                    shift = span * cols
                    done = list(block)
                    for k in range(group):
                        if k & span:
                            continue
                        lo_v, hi_v = block[k], block[k | span]
                        done[k] = jnp.where(high, pltpu.roll(hi_v, shift, 1), lo_v)
                        done[k | span] = jnp.where(
                            high, hi_v, pltpu.roll(lo_v, tile - shift, 1)
                        )
                    block = done
                for k in range(group):
                    lanes_of[t * group + k][u] = block[k]
        value = jnp.concatenate([jnp.concatenate(v, axis=1) for v in lanes_of], axis=0)
        high_part = value.astype(BF16)
        low_part = (value - high_part.astype(F32)).astype(BF16)
        out[d] = jnp.dot(high_part, order, preferred_element_type=F32) + jnp.dot(
            low_part, order, preferred_element_type=F32
        )


def body(frame_one, frame_two, enc_weight, mask_weight):
    rows, cols = frame_one.shape[0], frame_one.shape[1]
    cells = rows * cols
    n2, n1, few, tall = 3 * rows + 2, rows + 4, rows + 2, 3 * rows
    n2_pad = -(-n2 // BC) * BC
    slots = n1 + n2_pad // BC + -(-n1 // BC)
    lats, lons = lax.axis_size("lat"), lax.axis_size("lon")
    far_lat = pair_perm(lats, 1, False)
    near_lat = pair_perm(lats, 0, False)
    low_lat = pair_perm(lats, 0, False, 2)
    high_lat = pair_perm(lats, 2, False, 2)
    far_lon = pair_perm(lons, 1, True)
    chips = [[i, i + 1] for i in range(0, lons, 2)]

    def array(*shape, dtype=BF16):
        return jax.ShapeDtypeStruct(shape, dtype)

    tile = array(rows, cols, CH)
    m_a, m_b, m_c, m_d, one, two = pl.pallas_call(
        functools.partial(edge_kernel, rows, cols),
        out_shape=(array(few, cols, CH),) * 2 + (array(1, cols, CH),) * 2 + (tile, tile),
        in_specs=[pl.BlockSpec(memory_space=pltpu.MemorySpace.HBM)] * 2,
        out_specs=(VMEM,) * 6,
        scratch_shapes=[pltpu.SemaphoreType.DMA((8,))],
        compiler_params=params(8),
        name="edges",
    )(
        pltpu.with_memory_space_constraint(frame_one, pltpu.MemorySpace.HBM),
        pltpu.with_memory_space_constraint(frame_two, pltpu.MemorySpace.HBM),
    )
    row_a = lax.ppermute(m_a, "lat", far_lat)
    row_b = lax.ppermute(m_b, "lat", near_lat)
    row_c = lax.ppermute(m_c, "lat", high_lat)
    row_d = lax.ppermute(m_d, "lat", low_lat)

    m_x = pl.pallas_call(
        functools.partial(pack_kernel, rows, cols),
        out_shape=array(slots, BC, CH),
        in_specs=[VMEM] * 6,
        out_specs=VMEM,
        scratch_shapes=[
            pltpu.VMEM((n1, cols, CH), BF16),
            pltpu.VMEM((n2, cols, CH), BF16),
            pltpu.VMEM((n2_pad, CH), F32),
        ],
        compiler_params=params(16),
        name="pack",
    )(one, two, row_a, row_b, row_c, row_d)
    col_x = lax.ppermute(m_x, "lon", far_lon)

    weight = enc_weight.reshape(9 * CH, CH)
    few_pad = -(-few // BR) * BR
    own_two, own_one, ends_two, ends_one, m_in, edges = pl.pallas_call(
        functools.partial(own_kernel, rows, cols),
        out_shape=(
            array(tall, cols, CH),
            array(few, cols, CH),
            array(2, tall, CH, dtype=F32),
            array(2, few_pad, CH, dtype=F32),
            array(slots, BC, CH),
            array(2, -(-n1 // BR) * BR, CH, dtype=F32),
        ),
        in_specs=[VMEM] * 7,
        out_specs=(VMEM,) * 6,
        scratch_shapes=[
            pltpu.VMEM((n2, cols + 2 * BR, CH), F32),
            pltpu.VMEM((n1, cols + 2 * BR, CH), F32),
            pltpu.VMEM((3, n2, cols, CH), BF16),
            pltpu.VMEM((3, n1, cols, CH), BF16),
            pltpu.VMEM((n2_pad, CH), F32),
        ],
        compiler_params=params(24),
        cost_estimate=pl.CostEstimate(
            flops=2 * 9 * CH * CH * cols * (tall + few), bytes_accessed=4 << 20, transcendentals=0
        ),
        name="encode_own",
    )(one, two, row_a, row_b, row_c, row_d, weight)

    col_in = lax.all_gather(m_in, "lon", axis_index_groups=chips)
    side_scratch = [
        pltpu.VMEM((n1, BC + 2 * BR, CH), F32),
        pltpu.VMEM((3, n1, BC, CH), BF16),
    ]
    strip_in, two_in, first_in = pl.pallas_call(
        functools.partial(strip_kernel, rows, cols),
        out_shape=(array(few, BC, CH), array(tall, BC, CH), array(few, BC, CH)),
        in_specs=[VMEM] * 7,
        out_specs=(VMEM,) * 3,
        scratch_shapes=side_scratch,
        compiler_params=params(16),
        cost_estimate=pl.CostEstimate(
            flops=2 * 9 * CH * CH * BC * few, bytes_accessed=4 << 20, transcendentals=0
        ),
        name="strip",
    )(own_two, own_one, ends_two, ends_one, edges, col_in, weight)

    width = -(-few * cols // 128) * 128
    sums, enc_one = pl.pallas_call(
        functools.partial(score_kernel, rows, cols),
        out_shape=(array(8, width, dtype=F32), array(few, cols, CH)),
        in_specs=[VMEM] * 10,
        out_specs=(VMEM, VMEM),
        scratch_shapes=side_scratch
        + [pltpu.VMEM((tall, cols, CH), BF16), pltpu.VMEM((few, cols, CH), BF16)],
        compiler_params=params(20),
        name="score",
    )(own_two, own_one, ends_two, ends_one, edges, strip_in, two_in, first_in, col_x, weight)
    sums_far = lax.ppermute(sums, "lon", far_lon)
    sums_in = lax.all_gather(sums, "lon", axis_index_groups=chips)

    wt = mask_weight.reshape(CH, 9, UP, UP).transpose(1, 3, 2, 0).reshape(9 * UP * UP, CH)
    mix = pl.pallas_call(
        functools.partial(mix_kernel, rows, cells),
        out_shape=array(9, UP, UP, cells, dtype=F32),
        in_specs=[VMEM] * 2,
        out_specs=VMEM,
        compiler_params=params(16),
        cost_estimate=pl.CostEstimate(
            flops=2 * 576 * CH * cells, bytes_accessed=4 * 576 * cells, transcendentals=576 * cells
        ),
        name="mix",
    )(enc_one, wt)
    return pl.pallas_call(
        functools.partial(up_kernel, rows, cols),
        out_shape=array(2, rows * UP, cols * UP, dtype=F32),
        in_specs=[VMEM] * 4,
        out_specs=VMEM,
        compiler_params=params(16),
        name="upsample",
    )(sums, sums_far, sums_in, mix)


def solution(mesh):
    in_specs = (P("lat", "lon", None), P("lat", "lon", None), P(), P())
    return jax.shard_map(
        body, mesh=mesh, in_specs=in_specs, out_specs=P(None, "lat", "lon"), check_vma=False
    )
```

```python
import functools
import math

import jax
import jax.numpy as jnp
from jax import lax
from jax.experimental import pallas as pl
from jax.experimental.pallas import tpu as pltpu
from jax.sharding import PartitionSpec as P

CH = 256
BR = 8
BC = 16
UP = 8
F32 = jnp.float32
BF16 = jnp.bfloat16
VMEM = pl.BlockSpec(memory_space=pltpu.VMEM)


def params(mib):
    return pltpu.CompilerParams(vmem_limit_bytes=mib * 1024 * 1024)


def pair_perm(size, first, wrap, apart=1):
    out = []
    for i in range(size):
        if (i - first) % (2 * apart) >= apart:
            continue
        j = i + apart
        if j >= size:
            if not wrap:
                continue
            j -= size
        out += [(i, j), (j, i)]
    return out


def edge_kernel(rows, cols, f1, f2, m_a, m_b, m_c, m_d, g1, sems):
    band = lax.axis_index("lat")
    odd = band % 2
    upper = band % 4 // 2
    copies = []
    for k, (msg, low) in enumerate(((m_a, odd), (m_b, 1 - odd))):
        copies.append(
            pltpu.make_async_copy(f2, msg.at[pl.ds(0, rows)], sems.at[2 * k])
        )
        copies.append(
            pltpu.make_async_copy(
                f1.at[pl.ds(low * (rows - 2), 2)], msg.at[pl.ds(rows, 2)], sems.at[1 + 2 * k]
            )
        )
    for k, (msg, low) in enumerate(((m_c, upper), (m_d, 1 - upper))):
        copies.append(
            pltpu.make_async_copy(f2.at[pl.ds(low * (rows - 1), 1)], msg, sems.at[4 + k])
        )
    copies.append(pltpu.make_async_copy(f1, g1, sems.at[6]))
    for copy in copies:
        copy.start()
    for copy in copies:
        copy.wait()


def by_parity(lat_run, ra, rb, rc, rd):
    band = lax.axis_index("lat")
    for odd in (0, 1):
        for upper in (0, 1):

            @pl.when((band % 2 == odd) & (band % 4 // 2 == upper))
            def _():
                pair = (rb, ra) if odd else (ra, rb)
                lat_run(*pair, *((rd, rc) if upper else (rc, rd)))


def edge(msg, main_cols, extra, rim, col):
    n1, n2 = main_cols.shape[0], rim.shape[0]
    slots1, slots2 = -(-n1 // BC), -(-n2 // BC)
    msg[0:n1] = main_cols
    col[0:n1] = extra
    msg[n1 : n1 + slots1] = col[0 : slots1 * BC].astype(BF16).reshape(slots1, BC, CH)
    col[0:n2] = rim
    msg[n1 + slots1 :] = col[0 : slots2 * BC].astype(BF16).reshape(slots2, BC, CH)


def edge_places(cols, right):
    return (cols - BC, cols - BC - 1, cols - 1) if right else (0, BC, 0)


def pack_kernel(rows, cols, f1, f2, ra, rb, rc, rd, m_x, ext1, ext2, col):
    lon_odd = lax.axis_index("lon") % 2
    n2 = 3 * rows + 2
    n1 = rows + 4

    def halo(north, south, north_far, south_far):
        ext2[0:1] = north_far[...]
        ext2[1 : 1 + rows] = north[0:rows]
        ext2[1 + 2 * rows : 1 + 3 * rows] = south[0:rows]
        ext2[n2 - 1 : n2] = south_far[...]
        ext1[0:2] = north[rows : rows + 2]
        ext1[n1 - 2 : n1] = south[rows : rows + 2]

    ext2[1 + rows : 1 + 2 * rows] = f2[0:rows]
    ext1[2 : 2 + rows] = f1[...]
    by_parity(halo, ra, rb, rc, rd)

    def column(frame, at):
        base = at // BC * BC
        return frame[:, base : base + BC].astype(F32)[:, at - base, :]

    for odd in (0, 1):

        @pl.when(lon_odd == odd)
        def _():
            main, extra, one = edge_places(cols, odd == 1)
            edge(m_x, ext1[:, main : main + BC], column(ext1, extra), column(ext2, one), col)


def conv(x, w, row, count, width):
    lhs = jnp.concatenate(
        [
            x[b, row + a : row + a + count].reshape(count * width, CH)
            for a in range(3)
            for b in range(3)
        ],
        axis=1,
    )
    return jnp.dot(lhs, w[...], preferred_element_type=F32)


def own_kernel(
    rows, cols, f1, f2, ra, rb, rc, rd, w, e2, e1, ends2, ends1, m_in, edges, s2, s1, x2, x1, col
):
    lon_odd = lax.axis_index("lon") % 2
    n2 = 3 * rows + 2
    n1 = rows + 4
    own = slice(BR, BR + cols)

    def halo(north, south, north_far, south_far):
        s2[0:1, own] = north_far[...].astype(F32)
        s2[1 : 1 + rows, own] = north[0:rows].astype(F32)
        s2[1 + 2 * rows : 1 + 3 * rows, own] = south[0:rows].astype(F32)
        s2[n2 - 1 : n2, own] = south_far[...].astype(F32)
        s1[0:2, own] = north[rows : rows + 2].astype(F32)
        s1[n1 - 2 : n1, own] = south[rows : rows + 2].astype(F32)

    s2[1 + rows : 1 + 2 * rows, own] = f2[0:rows].astype(F32)
    s1[2 : 2 + rows, own] = f1[...].astype(F32)
    by_parity(halo, ra, rb, rc, rd)
    for s in (s2, s1):
        s[:, 0:BR] = jnp.zeros((s.shape[0], BR, CH), F32)
        s[:, BR + cols :] = jnp.zeros((s.shape[0], BR, CH), F32)
    for b in range(3):
        x2[b] = s2[:, BR - 1 + b : BR - 1 + b + cols].astype(BF16)
        x1[b] = s1[:, BR - 1 + b : BR - 1 + b + cols].astype(BF16)

    def run(x, out, ends, total):
        for r in range(0, total, 2 * BR):
            step = min(2 * BR, total - r)
            acc = conv(x, w, r, step, cols).reshape(step, cols, CH)
            out[r : r + step] = acc.astype(BF16)
            ends[0, r : r + step] = acc[:, 0, :]
            ends[1, r : r + step] = acc[:, cols - 1, :]

    run(x1, e1, ends1, rows + 2)
    run(x2, e2, ends2, 3 * rows)
    edges[0, 0:n1] = s1[:, BR, :]
    edges[1, 0:n1] = s1[:, BR + cols - 1, :]
    for odd in (0, 1):

        @pl.when(lon_odd == odd)
        def _():
            main, extra, one = edge_places(cols, odd == 0)
            edge(m_in, x1[1, :, main : main + BC], s1[:, BR + extra, :], s2[:, BR + one, :], col)


def finish_side(rows, cols, side, msg, w, o2, o1, ends2, ends1, edges, ext, xs, put):
    n2 = 3 * rows + 2
    n1 = rows + 4
    slots2 = -(-n2 // BC)
    slots1 = -(-n1 // BC)
    few, tall = rows + 2, 3 * rows
    extra = msg[n1 : n1 + slots1].astype(F32).reshape(slots1 * BC, CH)[0:n1]
    rim = msg[n1 + slots1 :].astype(F32).reshape(slots2 * BC, CH)[0:n2].astype(BF16)
    inner = edges[side, 0:n1]
    ext[:, BR : BR + BC] = msg[0:n1].astype(F32)
    ext[:, BR - 1 : BR] = (inner if side else extra)[:, None, :]
    ext[:, BR + BC : BR + BC + 1] = (extra if side else inner)[:, None, :]
    for b in range(3):
        xs[b] = ext[:, BR - 1 + b : BR - 1 + b + BC].astype(BF16)
    strip = conv(xs, w, 0, few, BC).astype(BF16).reshape(few, BC, CH)
    near = ext[:, BR : BR + 1] if side else ext[:, BR + BC - 1 : BR + BC]
    near = near[:, 0, :].astype(BF16)
    taps = jnp.concatenate(
        [w[(3 * a + 2 * side) * CH : (3 * a + 2 * side + 1) * CH] for a in range(3)], axis=0
    )
    lhs = jnp.concatenate(
        [jnp.concatenate([rim[a : a + tall], near[a : a + few]], axis=0) for a in range(3)],
        axis=1,
    )
    more = jnp.dot(lhs, taps, preferred_element_type=F32)
    hit = lax.broadcasted_iota(jnp.int32, (1, BC, CH), 1) == (BC - 1 if side else 0)
    lo = cols - BC if side else 0
    full = ends2[side, 0:tall] + more[0:tall]
    two = jnp.where(hit, full[:, None, :], o2[:, lo : lo + BC].astype(F32)).astype(BF16)
    full = ends1[side, 0:few] + more[tall : tall + few]
    first = jnp.where(hit, full[:, None, :], o1[:, lo : lo + BC].astype(F32)).astype(BF16)
    put(side, strip, two, first)


def strip_kernel(rows, cols, o2, o1, ends2, ends1, edges, chip, w, strip, two, first, ext, xs):
    lon_odd = lax.axis_index("lon") % 2
    msg = chip.at[1 - lon_odd]

    def put(side, *values):
        for ref, value in zip((strip, two, first), values):
            ref[...] = value

    for odd in (0, 1):

        @pl.when(lon_odd == odd)
        def _():
            finish_side(rows, cols, 1 - odd, msg, w, o2, o1, ends2, ends1, edges, ext, xs, put)


def score_kernel(
    rows, cols, o2, o1, ends2, ends1, edges, strip_in, two_in, first_in, c_x, w,
    sums, enc_one, ext, xs, e2, beside,
):
    lat = lax.axis_index("lat")
    lon_odd = lax.axis_index("lon") % 2

    def put(side, strip, two, first):
        lo = cols - BC if side else 0
        e2[:, lo : lo + BC] = two
        enc_one[:, lo : lo + BC] = first
        lo = 0 if side else cols - BC
        beside[:, lo : lo + BC] = strip

    for odd in (0, 1):

        @pl.when(lon_odd == odd)
        def _():
            put(1 - odd, strip_in[...], two_in[...], first_in[...])
            finish_side(rows, cols, odd, c_x, w, o2, o1, ends2, ends1, edges, ext, xs, put)

    bands = rows // BR
    last = lax.axis_size("lat") - 1
    scale = 1.0 / math.sqrt(CH)
    groups = cols // BR

    def features(ref, row, count):
        flat = ref[row : row + count].reshape(count * cols, CH).astype(F32)
        return (flat * scale).astype(BF16)

    def scores(block, query):
        keys = e2[block * BR : (block + 1) * BR].reshape(BR * cols, CH)
        return lax.dot_general(
            keys, query, (((1,), (1,)), ((), ())), preferred_element_type=F32
        ).reshape(BR, groups, BR, query.shape[0])

    def add(total, now):
        return now if total is None else [p + e for p, e in zip(total, now)]

    def triple(pieces, by_row, sub, base):
        mass = pieces[0]
        octs = None
        for i, piece in enumerate(pieces[1:], 1):
            mass = mass + piece
            octs = piece * float(i) if octs is None else octs + piece * float(i)
        across = octs * 8.0 + mass * (sub if base is None else sub + base)
        return [jnp.sum(v, axis=0, keepdims=True) for v in (mass, by_row, across)]

    queries = BR * cols
    sub = lax.broadcasted_iota(jnp.int32, (BR, queries), 0).astype(F32)
    of_right = lax.broadcasted_iota(jnp.int32, (BR, queries), 1) % cols < BC
    base = jnp.where(of_right, float(BC - cols), float(cols))
    for g in range(bands):
        query_own = features(enc_one, 1 + g * BR, BR)
        query_side = features(beside, 1 + g * BR, BR)
        acc = None
        for kb in range(3):
            mine = scores(g + kb + 1, query_own)
            other = scores(g + kb + 1, query_side)
            part = None
            for kr in range(BR):
                row = float((kb - 1) * BR + kr)
                own = [jnp.exp(mine[kr, i]) for i in range(4)]
                side = [
                    jnp.exp(jnp.where(of_right, other[kr, 2 + i], other[kr, i])) for i in range(2)
                ]
                now = own + [row * ((own[0] + own[1]) + (own[2] + own[3]))]
                now += side + [row * (side[0] + side[1])]
                part = add(part, now)
            if kb == 0 and g == 0:
                part = [jnp.where(lat > 0, p, 0.0) for p in part]
            elif kb == 2 and g == bands - 1:
                part = [jnp.where(lat < last, p, 0.0) for p in part]
            acc = add(acc, part)
        values = triple(acc[0:4], acc[4], sub, None) + triple(acc[5:7], acc[7], sub, base)
        values += [jnp.zeros((2, queries), F32)]
        sums[:, cols + g * queries : cols + (g + 1) * queries] = jnp.concatenate(values, axis=0)

    quarter = cols
    lanes = 4 * quarter
    sub = lax.broadcasted_iota(jnp.int32, (BR, lanes), 0).astype(F32)
    lane = lax.broadcasted_iota(jnp.int32, (BR, lanes), 1)
    below = lane >= 2 * quarter
    spot = lane % (2 * quarter)
    is_own = spot < quarter
    of_right = (spot >= quarter) & (spot < quarter + BC)
    base = jnp.where(is_own, 0.0, jnp.where(of_right, float(BC - cols), float(cols)))
    query = jnp.concatenate(
        [features(r, at, 1) for at in (0, rows + 1) for r in (enc_one, beside)], axis=0
    )
    acc = None
    for kb in range(3):
        over = scores(kb, query)
        under = scores(bands + 1 + kb, query)
        for kr in range(BR):
            row = float((kb - 1) * BR + kr)
            both = [jnp.where(below, under[kr, i], over[kr, i]) for i in range(4)]
            now = [jnp.exp(jnp.where(of_right, both[2 + i], both[i])) for i in range(2)]
            now += [jnp.where(is_own, jnp.exp(both[i]), 0.0) for i in range(2, 4)]
            now += [row * ((now[0] + now[1]) + (now[2] + now[3]))]
            acc = add(acc, now)
    values = triple(acc[0:4], acc[4], sub, base)
    for k, at in enumerate((0, cols + rows * cols)):
        for m in range(2):
            lo = (2 * k + m) * quarter
            sums[3 * m : 3 * m + 3, at : at + cols] = jnp.concatenate(
                [v[:, lo : lo + quarter] for v in values], axis=0
            )
        sums[6:8, at : at + cols] = jnp.zeros((2, cols), F32)


def mix_kernel(rows, cells, enc_one, wt, sums, mix, total, passed):
    passed[...] = sums[...]
    feats = enc_one[1 : 1 + rows].reshape(cells, CH)
    step = 256
    count = UP * UP
    for c0 in range(0, cells, step):
        mass = None
        for n in range(9):
            logits = lax.dot_general(
                wt[n * count : (n + 1) * count],
                feats[c0 : c0 + step],
                (((1,), (1,)), ((), ())),
                preferred_element_type=F32,
            )
            expo = jnp.exp(logits).reshape(UP, UP, step)
            mix[n, :, :, c0 : c0 + step] = expo
            mass = expo if mass is None else mass + expo
        total[:, :, c0 : c0 + step] = 1.0 / mass


def up_kernel(rows, cols, mine, far, chip, mix, total_r, out):
    lat = lax.axis_index("lat")
    last = lax.axis_size("lat") - 1
    lon_odd = lax.axis_index("lon") % 2
    cells = rows * cols
    width = mine.shape[1]
    lane = lax.broadcasted_iota(jnp.int32, (1, width), 1)
    column = lane % cols
    row = ((lane // cols + BR - 1) % BR).astype(F32)
    outside = ((lane < cols) & (lat == 0)) | ((lane >= cols + cells) & (lat == last))
    partner = chip[1 - lon_odd]
    is_odd = jnp.broadcast_to(lon_odd == 1, partner.shape)
    left = jnp.where(is_odd, partner, far[...])
    right = jnp.where(is_odd, far[...], partner)
    own = mine[...]

    def flow(total):
        both = jnp.concatenate(
            [total[1:2] / total[0:1] - row, total[2:3] / total[0:1] - column.astype(F32)], axis=0
        )
        return jnp.where(outside, 0.0, both * float(UP))

    mid = flow(own[0:3] + jnp.where(column < BC, left[3:6], right[3:6]))
    west = flow(left[0:3] + own[3:6])
    east = flow(right[0:3] + own[3:6])
    west = jnp.where(
        column == 0, pltpu.roll(west, width - (cols - 1), 1), pltpu.roll(mid, 1, 1)
    )
    east = jnp.where(
        column == cols - 1, pltpu.roll(east, cols - 1, 1), pltpu.roll(mid, width - 1, 1)
    )
    shifted = []
    for a in range(3):
        for field in (west, mid, east):
            moved = field if a == 0 else pltpu.roll(field, width - a * cols, 1)
            shifted.append(moved[:, 0:cells])
    src = lax.broadcasted_iota(jnp.int32, (UP * cols, UP * cols), 0)
    dst = lax.broadcasted_iota(jnp.int32, (UP * cols, UP * cols), 1)
    order = jnp.where((dst // UP == src % cols) & (dst % UP == src // cols), 1.0, 0.0).astype(BF16)
    tile = 128
    group = tile // cols
    lane = lax.broadcasted_iota(jnp.int32, (UP, tile), 1)
    bits = []
    span = 1
    while span < group:
        bits.append((span, (lane // (span * cols)) % 2 == 1))
        span *= 2
    for d in range(2):
        lanes_of = [[None] * (UP // group) for _ in range(rows)]
        for t in range(cells // tile):
            flows = [
                jnp.broadcast_to(v[d : d + 1, t * tile : (t + 1) * tile], (UP, tile))
                for v in shifted
            ]
            for u in range(UP // group):
                block = []
                for k in range(group):
                    acc = None
                    for n in range(9):
                        term = mix[n, u * group + k, :, t * tile : (t + 1) * tile] * flows[n]
                        acc = term if acc is None else acc + term
                    part = total_r[u * group + k, :, t * tile : (t + 1) * tile]
                    block.append(acc * part)
                for span, high in bits:
                    shift = span * cols
                    done = list(block)
                    for k in range(group):
                        if k & span:
                            continue
                        lo_v, hi_v = block[k], block[k | span]
                        done[k] = jnp.where(high, pltpu.roll(hi_v, shift, 1), lo_v)
                        done[k | span] = jnp.where(
                            high, hi_v, pltpu.roll(lo_v, tile - shift, 1)
                        )
                    block = done
                for k in range(group):
                    lanes_of[t * group + k][u] = block[k]
        value = jnp.concatenate([jnp.concatenate(v, axis=1) for v in lanes_of], axis=0)
        high_part = value.astype(BF16)
        low_part = (value - high_part.astype(F32)).astype(BF16)
        out[d] = jnp.dot(high_part, order, preferred_element_type=F32) + jnp.dot(
            low_part, order, preferred_element_type=F32
        )


def body(frame_one, frame_two, enc_weight, mask_weight):
    rows, cols = frame_one.shape[0], frame_one.shape[1]
    cells = rows * cols
    n2, n1, few, tall = 3 * rows + 2, rows + 4, rows + 2, 3 * rows
    n2_pad = -(-n2 // BC) * BC
    slots = n1 + n2_pad // BC + -(-n1 // BC)
    lats, lons = lax.axis_size("lat"), lax.axis_size("lon")
    far_lat = pair_perm(lats, 1, False)
    near_lat = pair_perm(lats, 0, False)
    low_lat = pair_perm(lats, 0, False, 2)
    high_lat = pair_perm(lats, 2, False, 2)
    far_lon = pair_perm(lons, 1, True)
    chips = [[i, i + 1] for i in range(0, lons, 2)]

    def array(*shape, dtype=BF16):
        return jax.ShapeDtypeStruct(shape, dtype)

    tile = array(rows, cols, CH)
    m_a, m_b, m_c, m_d, one = pl.pallas_call(
        functools.partial(edge_kernel, rows, cols),
        out_shape=(array(few, cols, CH),) * 2 + (array(1, cols, CH),) * 2 + (tile,),
        in_specs=[pl.BlockSpec(memory_space=pltpu.MemorySpace.HBM)] * 2,
        out_specs=(VMEM,) * 5,
        scratch_shapes=[pltpu.SemaphoreType.DMA((7,))],
        compiler_params=params(8),
        name="edges",
    )(
        pltpu.with_memory_space_constraint(frame_one, pltpu.MemorySpace.HBM),
        pltpu.with_memory_space_constraint(frame_two, pltpu.MemorySpace.HBM),
    )
    row_a = lax.ppermute(m_a, "lat", far_lat)
    row_b = lax.ppermute(m_b, "lat", near_lat)
    row_c = lax.ppermute(m_c, "lat", high_lat)
    row_d = lax.ppermute(m_d, "lat", low_lat)

    m_x = pl.pallas_call(
        functools.partial(pack_kernel, rows, cols),
        out_shape=array(slots, BC, CH),
        in_specs=[VMEM] * 6,
        out_specs=VMEM,
        scratch_shapes=[
            pltpu.VMEM((n1, cols, CH), BF16),
            pltpu.VMEM((n2, cols, CH), BF16),
            pltpu.VMEM((n2_pad, CH), F32),
        ],
        compiler_params=params(16),
        name="pack",
    )(one, m_a, row_a, row_b, row_c, row_d)
    col_x = lax.ppermute(m_x, "lon", far_lon)

    weight = enc_weight.reshape(9 * CH, CH)
    few_pad = -(-few // BR) * BR
    own_two, own_one, ends_two, ends_one, m_in, edges = pl.pallas_call(
        functools.partial(own_kernel, rows, cols),
        out_shape=(
            array(tall, cols, CH),
            array(few, cols, CH),
            array(2, tall, CH, dtype=F32),
            array(2, few_pad, CH, dtype=F32),
            array(slots, BC, CH),
            array(2, -(-n1 // BR) * BR, CH, dtype=F32),
        ),
        in_specs=[VMEM] * 7,
        out_specs=(VMEM,) * 6,
        scratch_shapes=[
            pltpu.VMEM((n2, cols + 2 * BR, CH), F32),
            pltpu.VMEM((n1, cols + 2 * BR, CH), F32),
            pltpu.VMEM((3, n2, cols, CH), BF16),
            pltpu.VMEM((3, n1, cols, CH), BF16),
            pltpu.VMEM((n2_pad, CH), F32),
        ],
        compiler_params=params(24),
        cost_estimate=pl.CostEstimate(
            flops=2 * 9 * CH * CH * cols * (tall + few), bytes_accessed=4 << 20, transcendentals=0
        ),
        name="encode_own",
    )(one, m_a, row_a, row_b, row_c, row_d, weight)

    col_in = lax.all_gather(m_in, "lon", axis_index_groups=chips)
    side_scratch = [
        pltpu.VMEM((n1, BC + 2 * BR, CH), F32),
        pltpu.VMEM((3, n1, BC, CH), BF16),
    ]
    strip_in, two_in, first_in = pl.pallas_call(
        functools.partial(strip_kernel, rows, cols),
        out_shape=(array(few, BC, CH), array(tall, BC, CH), array(few, BC, CH)),
        in_specs=[VMEM] * 7,
        out_specs=(VMEM,) * 3,
        scratch_shapes=side_scratch,
        compiler_params=params(16),
        cost_estimate=pl.CostEstimate(
            flops=2 * 9 * CH * CH * BC * few, bytes_accessed=4 << 20, transcendentals=0
        ),
        name="strip",
    )(own_two, own_one, ends_two, ends_one, edges, col_in, weight)

    width = -(-few * cols // 128) * 128
    sums, enc_one = pl.pallas_call(
        functools.partial(score_kernel, rows, cols),
        out_shape=(array(8, width, dtype=F32), array(few, cols, CH)),
        in_specs=[VMEM] * 10,
        out_specs=(VMEM, VMEM),
        scratch_shapes=side_scratch
        + [pltpu.VMEM((tall, cols, CH), BF16), pltpu.VMEM((few, cols, CH), BF16)],
        compiler_params=params(20),
        name="score",
    )(own_two, own_one, ends_two, ends_one, edges, strip_in, two_in, first_in, col_x, weight)
    sums_far = lax.ppermute(sums, "lon", far_lon)

    wt = mask_weight.reshape(CH, 9, UP, UP).transpose(1, 3, 2, 0).reshape(9 * UP * UP, CH)
    mix, inverse, sums_too = pl.pallas_call(
        functools.partial(mix_kernel, rows, cells),
        out_shape=(
            array(9, UP, UP, cells, dtype=F32),
            array(UP, UP, cells, dtype=F32),
            array(8, width, dtype=F32),
        ),
        in_specs=[VMEM] * 3,
        out_specs=(VMEM,) * 3,
        compiler_params=params(16),
        cost_estimate=pl.CostEstimate(
            flops=2 * 576 * CH * cells, bytes_accessed=4 * 576 * cells, transcendentals=576 * cells
        ),
        name="mix",
    )(enc_one, wt, sums)
    sums_in = lax.all_gather(sums_too, "lon", axis_index_groups=chips)
    return pl.pallas_call(
        functools.partial(up_kernel, rows, cols),
        out_shape=array(2, rows * UP, cols * UP, dtype=F32),
        in_specs=[VMEM] * 5,
        out_specs=VMEM,
        compiler_params=params(16),
        name="upsample",
    )(sums, sums_far, sums_in, mix, inverse)


def solution(mesh):
    in_specs = (P("lat", "lon", None), P("lat", "lon", None), P(), P())
    return jax.shard_map(
        body, mesh=mesh, in_specs=in_specs, out_specs=P(None, "lat", "lon"), check_vma=False
    )
```

```python
import functools
import math

import jax
import jax.numpy as jnp
from jax import lax
from jax.experimental import pallas as pl
from jax.experimental.pallas import tpu as pltpu
from jax.sharding import PartitionSpec as P

CH = 256
BR = 8
BC = 16
UP = 8
F32 = jnp.float32
BF16 = jnp.bfloat16
VMEM = pl.BlockSpec(memory_space=pltpu.VMEM)


def params(mib):
    return pltpu.CompilerParams(vmem_limit_bytes=mib * 1024 * 1024)


def pair_perm(size, first, wrap, apart=1):
    out = []
    for i in range(size):
        if (i - first) % (2 * apart) >= apart:
            continue
        j = i + apart
        if j >= size:
            if not wrap:
                continue
            j -= size
        out += [(i, j), (j, i)]
    return out


def edge_kernel(rows, cols, f1, f2, m_a, m_b, m_c, m_d, g1, sems):
    band = lax.axis_index("lat")
    odd = band % 2
    upper = band % 4 // 2
    copies = []
    for k, (msg, low) in enumerate(((m_a, odd), (m_b, 1 - odd))):
        copies.append(
            pltpu.make_async_copy(f2, msg.at[pl.ds(0, rows)], sems.at[2 * k])
        )
        copies.append(
            pltpu.make_async_copy(
                f1.at[pl.ds(low * (rows - 2), 2)], msg.at[pl.ds(rows, 2)], sems.at[1 + 2 * k]
            )
        )
    for k, (msg, low) in enumerate(((m_c, upper), (m_d, 1 - upper))):
        copies.append(
            pltpu.make_async_copy(f2.at[pl.ds(low * (rows - 1), 1)], msg, sems.at[4 + k])
        )
    copies.append(pltpu.make_async_copy(f1, g1, sems.at[6]))
    for copy in copies:
        copy.start()
    for copy in copies:
        copy.wait()


def by_parity(lat_run, ra, rb, rc, rd):
    band = lax.axis_index("lat")
    for odd in (0, 1):
        for upper in (0, 1):

            @pl.when((band % 2 == odd) & (band % 4 // 2 == upper))
            def _():
                pair = (rb, ra) if odd else (ra, rb)
                lat_run(*pair, *((rd, rc) if upper else (rc, rd)))


def edge(msg, main_cols, extra, rim, col):
    n1, n2 = main_cols.shape[0], rim.shape[0]
    slots1, slots2 = -(-n1 // BC), -(-n2 // BC)
    msg[0:n1] = main_cols
    col[0:n1] = extra
    msg[n1 : n1 + slots1] = col[0 : slots1 * BC].astype(BF16).reshape(slots1, BC, CH)
    col[0:n2] = rim
    msg[n1 + slots1 :] = col[0 : slots2 * BC].astype(BF16).reshape(slots2, BC, CH)


def edge_places(cols, right):
    return (cols - BC, cols - BC - 1, cols - 1) if right else (0, BC, 0)


def pack_kernel(rows, cols, f1, f2, ra, rb, rc, rd, m_x, ext1, ext2, col):
    lon_odd = lax.axis_index("lon") % 2
    n2 = 3 * rows + 2
    n1 = rows + 4

    def halo(north, south, north_far, south_far):
        ext2[0:1] = north_far[...]
        ext2[1 : 1 + rows] = north[0:rows]
        ext2[1 + 2 * rows : 1 + 3 * rows] = south[0:rows]
        ext2[n2 - 1 : n2] = south_far[...]
        ext1[0:2] = north[rows : rows + 2]
        ext1[n1 - 2 : n1] = south[rows : rows + 2]

    ext2[1 + rows : 1 + 2 * rows] = f2[0:rows]
    ext1[2 : 2 + rows] = f1[...]
    by_parity(halo, ra, rb, rc, rd)

    def column(frame, at):
        base = at // BC * BC
        return frame[:, base : base + BC].astype(F32)[:, at - base, :]

    for odd in (0, 1):

        @pl.when(lon_odd == odd)
        def _():
            main, extra, one = edge_places(cols, odd == 1)
            edge(m_x, ext1[:, main : main + BC], column(ext1, extra), column(ext2, one), col)


def conv(x, w, row, count, width):
    lhs = jnp.concatenate(
        [
            x[b, row + a : row + a + count].reshape(count * width, CH)
            for a in range(3)
            for b in range(3)
        ],
        axis=1,
    )
    return jnp.dot(lhs, w[...], preferred_element_type=F32)


def own_kernel(
    rows, cols, f1, f2, ra, rb, rc, rd, w, e2, e1, ends2, ends1, m_in, edges, s2, s1, x2, x1, col
):
    lon_odd = lax.axis_index("lon") % 2
    n2 = 3 * rows + 2
    n1 = rows + 4
    own = slice(BR, BR + cols)

    def halo(north, south, north_far, south_far):
        s2[0:1, own] = north_far[...].astype(F32)
        s2[1 : 1 + rows, own] = north[0:rows].astype(F32)
        s2[1 + 2 * rows : 1 + 3 * rows, own] = south[0:rows].astype(F32)
        s2[n2 - 1 : n2, own] = south_far[...].astype(F32)
        s1[0:2, own] = north[rows : rows + 2].astype(F32)
        s1[n1 - 2 : n1, own] = south[rows : rows + 2].astype(F32)

    s2[1 + rows : 1 + 2 * rows, own] = f2[0:rows].astype(F32)
    s1[2 : 2 + rows, own] = f1[...].astype(F32)
    by_parity(halo, ra, rb, rc, rd)
    for s in (s2, s1):
        s[:, 0:BR] = jnp.zeros((s.shape[0], BR, CH), F32)
        s[:, BR + cols :] = jnp.zeros((s.shape[0], BR, CH), F32)
    for b in range(3):
        x2[b] = s2[:, BR - 1 + b : BR - 1 + b + cols].astype(BF16)
        x1[b] = s1[:, BR - 1 + b : BR - 1 + b + cols].astype(BF16)

    def run(x, out, ends, total):
        for r in range(0, total, 2 * BR):
            step = min(2 * BR, total - r)
            acc = conv(x, w, r, step, cols).reshape(step, cols, CH)
            out[r : r + step] = acc.astype(BF16)
            ends[0, r : r + step] = acc[:, 0, :]
            ends[1, r : r + step] = acc[:, cols - 1, :]

    run(x1, e1, ends1, rows + 2)
    run(x2, e2, ends2, 3 * rows)
    edges[0, 0:n1] = s1[:, BR, :]
    edges[1, 0:n1] = s1[:, BR + cols - 1, :]
    for odd in (0, 1):

        @pl.when(lon_odd == odd)
        def _():
            main, extra, one = edge_places(cols, odd == 0)
            edge(m_in, x1[1, :, main : main + BC], s1[:, BR + extra, :], s2[:, BR + one, :], col)


def finish_side(rows, cols, side, msg, w, o2, o1, ends2, ends1, edges, ext, xs, put):
    n2 = 3 * rows + 2
    n1 = rows + 4
    slots2 = -(-n2 // BC)
    slots1 = -(-n1 // BC)
    few, tall = rows + 2, 3 * rows
    extra = msg[n1 : n1 + slots1].astype(F32).reshape(slots1 * BC, CH)[0:n1]
    rim = msg[n1 + slots1 :].astype(F32).reshape(slots2 * BC, CH)[0:n2].astype(BF16)
    inner = edges[side, 0:n1]
    ext[:, BR : BR + BC] = msg[0:n1].astype(F32)
    ext[:, BR - 1 : BR] = (inner if side else extra)[:, None, :]
    ext[:, BR + BC : BR + BC + 1] = (extra if side else inner)[:, None, :]
    for b in range(3):
        xs[b] = ext[:, BR - 1 + b : BR - 1 + b + BC].astype(BF16)
    strip = conv(xs, w, 0, few, BC).astype(BF16).reshape(few, BC, CH)
    near = ext[:, BR : BR + 1] if side else ext[:, BR + BC - 1 : BR + BC]
    near = near[:, 0, :].astype(BF16)
    taps = jnp.concatenate(
        [w[(3 * a + 2 * side) * CH : (3 * a + 2 * side + 1) * CH] for a in range(3)], axis=0
    )
    lhs = jnp.concatenate(
        [jnp.concatenate([rim[a : a + tall], near[a : a + few]], axis=0) for a in range(3)],
        axis=1,
    )
    more = jnp.dot(lhs, taps, preferred_element_type=F32)
    hit = lax.broadcasted_iota(jnp.int32, (1, BC, CH), 1) == (BC - 1 if side else 0)
    lo = cols - BC if side else 0
    full = ends2[side, 0:tall] + more[0:tall]
    two = jnp.where(hit, full[:, None, :], o2[:, lo : lo + BC].astype(F32)).astype(BF16)
    full = ends1[side, 0:few] + more[tall : tall + few]
    first = jnp.where(hit, full[:, None, :], o1[:, lo : lo + BC].astype(F32)).astype(BF16)
    put(side, strip, two, first)


def strip_kernel(
    rows, cols, o2, o1, ends2, ends1, edges, chip, w, strip, two, first, order, ext, xs
):
    src = lax.broadcasted_iota(jnp.int32, order.shape, 0)
    dst = lax.broadcasted_iota(jnp.int32, order.shape, 1)
    to = (src % cols) * UP + src // cols
    order[...] = jnp.where(dst == to, 1.0, 0.0).astype(BF16)
    lon_odd = lax.axis_index("lon") % 2
    msg = chip.at[1 - lon_odd]

    def put(side, *values):
        for ref, value in zip((strip, two, first), values):
            ref[...] = value

    for odd in (0, 1):

        @pl.when(lon_odd == odd)
        def _():
            finish_side(rows, cols, 1 - odd, msg, w, o2, o1, ends2, ends1, edges, ext, xs, put)


def score_kernel(
    rows, cols, o2, o1, ends2, ends1, edges, strip_in, two_in, first_in, c_x, w,
    sums, enc_one, ext, xs, e2, beside,
):
    lat = lax.axis_index("lat")
    lon_odd = lax.axis_index("lon") % 2

    def put(side, strip, two, first):
        lo = cols - BC if side else 0
        e2[:, lo : lo + BC] = two
        enc_one[:, lo : lo + BC] = first
        lo = 0 if side else cols - BC
        beside[:, lo : lo + BC] = strip

    for odd in (0, 1):

        @pl.when(lon_odd == odd)
        def _():
            put(1 - odd, strip_in[...], two_in[...], first_in[...])
            finish_side(rows, cols, odd, c_x, w, o2, o1, ends2, ends1, edges, ext, xs, put)

    bands = rows // BR
    last = lax.axis_size("lat") - 1
    scale = 1.0 / math.sqrt(CH)
    groups = cols // BR

    def features(ref, row, count):
        flat = ref[row : row + count].reshape(count * cols, CH).astype(F32)
        return (flat * scale).astype(BF16)

    def scores(block, query):
        keys = e2[block * BR : (block + 3) * BR].reshape(3 * BR * cols, CH)
        return lax.dot_general(
            keys, query, (((1,), (1,)), ((), ())), preferred_element_type=F32
        ).reshape(3, BR, groups, BR, query.shape[0])

    def add(total, now):
        return now if total is None else [p + e for p, e in zip(total, now)]

    def triple(pieces, by_row, sub, base):
        mass = pieces[0]
        octs = None
        for i, piece in enumerate(pieces[1:], 1):
            mass = mass + piece
            octs = piece * float(i) if octs is None else octs + piece * float(i)
        across = octs * 8.0 + mass * (sub if base is None else sub + base)
        return [jnp.sum(v, axis=0, keepdims=True) for v in (mass, by_row, across)]

    queries = BR * cols
    sub = lax.broadcasted_iota(jnp.int32, (BR, queries), 0).astype(F32)
    of_right = lax.broadcasted_iota(jnp.int32, (BR, queries), 1) % cols < BC
    base = jnp.where(of_right, float(BC - cols), float(cols))
    for g in range(bands):
        query_own = features(enc_one, 1 + g * BR, BR)
        query_side = features(beside, 1 + g * BR, BR)
        acc = None
        of_own = scores(g + 1, query_own)
        of_side = scores(g + 1, query_side)
        for kb in range(3):
            mine, other = of_own[kb], of_side[kb]
            part = None
            for kr in range(BR):
                row = float((kb - 1) * BR + kr)
                own = [jnp.exp(mine[kr, i]) for i in range(4)]
                side = [
                    jnp.exp(jnp.where(of_right, other[kr, 2 + i], other[kr, i])) for i in range(2)
                ]
                now = own + [row * ((own[0] + own[1]) + (own[2] + own[3]))]
                now += side + [row * (side[0] + side[1])]
                part = add(part, now)
            if kb == 0 and g == 0:
                part = [jnp.where(lat > 0, p, 0.0) for p in part]
            elif kb == 2 and g == bands - 1:
                part = [jnp.where(lat < last, p, 0.0) for p in part]
            acc = add(acc, part)
        values = triple(acc[0:4], acc[4], sub, None) + triple(acc[5:7], acc[7], sub, base)
        values += [jnp.zeros((2, queries), F32)]
        sums[:, cols + g * queries : cols + (g + 1) * queries] = jnp.concatenate(values, axis=0)

    quarter = cols
    lanes = 4 * quarter
    sub = lax.broadcasted_iota(jnp.int32, (BR, lanes), 0).astype(F32)
    lane = lax.broadcasted_iota(jnp.int32, (BR, lanes), 1)
    below = lane >= 2 * quarter
    spot = lane % (2 * quarter)
    is_own = spot < quarter
    of_right = (spot >= quarter) & (spot < quarter + BC)
    base = jnp.where(is_own, 0.0, jnp.where(of_right, float(BC - cols), float(cols)))
    query = jnp.concatenate(
        [features(r, at, 1) for at in (0, rows + 1) for r in (enc_one, beside)], axis=0
    )
    acc = None
    all_over = scores(0, query)
    all_under = scores(bands + 1, query)
    for kb in range(3):
        over, under = all_over[kb], all_under[kb]
        for kr in range(BR):
            row = float((kb - 1) * BR + kr)
            both = [jnp.where(below, under[kr, i], over[kr, i]) for i in range(4)]
            now = [jnp.exp(jnp.where(of_right, both[2 + i], both[i])) for i in range(2)]
            now += [jnp.where(is_own, jnp.exp(both[i]), 0.0) for i in range(2, 4)]
            now += [row * ((now[0] + now[1]) + (now[2] + now[3]))]
            acc = add(acc, now)
    values = triple(acc[0:4], acc[4], sub, base)
    for k, at in enumerate((0, cols + rows * cols)):
        for m in range(2):
            lo = (2 * k + m) * quarter
            sums[3 * m : 3 * m + 3, at : at + cols] = jnp.concatenate(
                [v[:, lo : lo + quarter] for v in values], axis=0
            )
        sums[6:8, at : at + cols] = jnp.zeros((2, cols), F32)


def mix_kernel(rows, cells, enc_one, wt, sums, mix, total, passed):
    passed[...] = sums[...]
    feats = enc_one[1 : 1 + rows].reshape(cells, CH)
    step = 256
    count = UP * UP
    for c0 in range(0, cells, step):
        logits = lax.dot_general(
            wt[...], feats[c0 : c0 + step], (((1,), (1,)), ((), ())), preferred_element_type=F32
        )
        mass = None
        for n in range(9):
            expo = jnp.exp(logits[n * count : (n + 1) * count]).reshape(UP, UP, step)
            mix[n, :, :, c0 : c0 + step] = expo
            mass = expo if mass is None else mass + expo
        total[:, :, c0 : c0 + step] = 1.0 / mass


def up_kernel(rows, cols, mine, far, chip, mix, inverse, order_ref, out, fine, sems):
    lat = lax.axis_index("lat")
    last = lax.axis_size("lat") - 1
    lon_odd = lax.axis_index("lon") % 2
    cells = rows * cols
    width = mine.shape[1]
    lane = lax.broadcasted_iota(jnp.int32, (1, width), 1)
    column = lane % cols
    row = ((lane // cols + BR - 1) % BR).astype(F32)
    outside = ((lane < cols) & (lat == 0)) | ((lane >= cols + cells) & (lat == last))
    partner = chip[1 - lon_odd]
    is_odd = jnp.broadcast_to(lon_odd == 1, partner.shape)
    left = jnp.where(is_odd, partner, far[...])
    right = jnp.where(is_odd, far[...], partner)
    own = mine[...]

    def flow(total):
        both = jnp.concatenate(
            [total[1:2] / total[0:1] - row, total[2:3] / total[0:1] - column.astype(F32)], axis=0
        )
        return jnp.where(outside, 0.0, both * float(UP))

    mid = flow(own[0:3] + jnp.where(column < BC, left[3:6], right[3:6]))
    west = flow(left[0:3] + own[3:6])
    east = flow(right[0:3] + own[3:6])
    west = jnp.where(
        column == 0, pltpu.roll(west, width - (cols - 1), 1), pltpu.roll(mid, 1, 1)
    )
    east = jnp.where(
        column == cols - 1, pltpu.roll(east, cols - 1, 1), pltpu.roll(mid, width - 1, 1)
    )
    shifted = []
    for a in range(3):
        for field in (west, mid, east):
            moved = field if a == 0 else pltpu.roll(field, width - a * cols, 1)
            shifted.append(moved[:, 0:cells])
    order = order_ref[...]
    tile = 128
    group = tile // cols
    lane = lax.broadcasted_iota(jnp.int32, (UP, tile), 1)
    bits = []
    span = 1
    while span < group:
        bits.append((span, (lane // (span * cols)) % 2 == 1))
        span *= 2
    count = group * UP
    copies = []
    for t in range(cells // tile):
        here = slice(t * tile, (t + 1) * tile)
        flows = [
            [jnp.broadcast_to(v[d : d + 1, here], (UP, tile)) for v in shifted] for d in range(2)
        ]
        lanes_of = [[[None] * (UP // group) for _ in range(group)] for _ in range(2)]
        for u in range(UP // group):
            blocks = [[], []]
            for k in range(group):
                at = u * group + k
                scale = inverse[at, :, here]
                weights = [mix[n, at, :, here] for n in range(9)]
                for d in range(2):
                    acc = weights[0] * flows[d][0]
                    for n in range(1, 9):
                        acc = acc + weights[n] * flows[d][n]
                    blocks[d].append(acc * scale)
            for d in range(2):
                block = blocks[d]
                for span, high in bits:
                    shift = span * cols
                    done = list(block)
                    for k in range(group):
                        if k & span:
                            continue
                        lo_v, hi_v = block[k], block[k | span]
                        done[k] = jnp.where(high, pltpu.roll(hi_v, shift, 1), lo_v)
                        done[k | span] = jnp.where(
                            high, hi_v, pltpu.roll(lo_v, tile - shift, 1)
                        )
                    block = done
                for k in range(group):
                    lanes_of[d][k][u] = block[k]
        value = jnp.concatenate(
            [jnp.concatenate(v, axis=1) for d in range(2) for v in lanes_of[d]], axis=0
        )
        high_part = value.astype(BF16)
        low_part = (value - high_part.astype(F32)).astype(BF16)
        both = jnp.dot(
            jnp.concatenate([high_part, low_part], axis=0), order, preferred_element_type=F32
        )
        both = both[0 : 2 * count] + both[2 * count :]
        for d in range(2):
            fine[d, t * count : (t + 1) * count] = both[d * count : (d + 1) * count]
            part = pl.ds(t * count, count)
            copy = pltpu.make_async_copy(
                fine.at[d, part], out.at[d, part], sems.at[2 * t + d]
            )
            copy.start()
            copies.append(copy)
    for copy in copies:
        copy.wait()


def body(frame_one, frame_two, enc_weight, mask_weight):
    rows, cols = frame_one.shape[0], frame_one.shape[1]
    cells = rows * cols
    n2, n1, few, tall = 3 * rows + 2, rows + 4, rows + 2, 3 * rows
    n2_pad = -(-n2 // BC) * BC
    slots = n1 + n2_pad // BC + -(-n1 // BC)
    lats, lons = lax.axis_size("lat"), lax.axis_size("lon")
    far_lat = pair_perm(lats, 1, False)
    near_lat = pair_perm(lats, 0, False)
    low_lat = pair_perm(lats, 0, False, 2)
    high_lat = pair_perm(lats, 2, False, 2)
    far_lon = pair_perm(lons, 1, True)
    chips = [[i, i + 1] for i in range(0, lons, 2)]

    def array(*shape, dtype=BF16):
        return jax.ShapeDtypeStruct(shape, dtype)

    tile = array(rows, cols, CH)
    m_a, m_b, m_c, m_d, one = pl.pallas_call(
        functools.partial(edge_kernel, rows, cols),
        out_shape=(array(few, cols, CH),) * 2 + (array(1, cols, CH),) * 2 + (tile,),
        in_specs=[pl.BlockSpec(memory_space=pltpu.MemorySpace.HBM)] * 2,
        out_specs=(VMEM,) * 5,
        scratch_shapes=[pltpu.SemaphoreType.DMA((7,))],
        compiler_params=params(8),
        name="edges",
    )(
        pltpu.with_memory_space_constraint(frame_one, pltpu.MemorySpace.HBM),
        pltpu.with_memory_space_constraint(frame_two, pltpu.MemorySpace.HBM),
    )
    row_a = lax.ppermute(m_a, "lat", far_lat)
    row_b = lax.ppermute(m_b, "lat", near_lat)
    row_c = lax.ppermute(m_c, "lat", high_lat)
    row_d = lax.ppermute(m_d, "lat", low_lat)

    m_x = pl.pallas_call(
        functools.partial(pack_kernel, rows, cols),
        out_shape=array(slots, BC, CH),
        in_specs=[VMEM] * 6,
        out_specs=VMEM,
        scratch_shapes=[
            pltpu.VMEM((n1, cols, CH), BF16),
            pltpu.VMEM((n2, cols, CH), BF16),
            pltpu.VMEM((n2_pad, CH), F32),
        ],
        compiler_params=params(16),
        name="pack",
    )(one, m_b, row_a, row_b, row_c, row_d)
    col_x = lax.ppermute(m_x, "lon", far_lon)

    weight = enc_weight.reshape(9 * CH, CH)
    few_pad = -(-few // BR) * BR
    own_two, own_one, ends_two, ends_one, m_in, edges = pl.pallas_call(
        functools.partial(own_kernel, rows, cols),
        out_shape=(
            array(tall, cols, CH),
            array(few, cols, CH),
            array(2, tall, CH, dtype=F32),
            array(2, few_pad, CH, dtype=F32),
            array(slots, BC, CH),
            array(2, -(-n1 // BR) * BR, CH, dtype=F32),
        ),
        in_specs=[VMEM] * 7,
        out_specs=(VMEM,) * 6,
        scratch_shapes=[
            pltpu.VMEM((n2, cols + 2 * BR, CH), F32),
            pltpu.VMEM((n1, cols + 2 * BR, CH), F32),
            pltpu.VMEM((3, n2, cols, CH), BF16),
            pltpu.VMEM((3, n1, cols, CH), BF16),
            pltpu.VMEM((n2_pad, CH), F32),
        ],
        compiler_params=params(24),
        cost_estimate=pl.CostEstimate(
            flops=2 * 9 * CH * CH * cols * (tall + few), bytes_accessed=4 << 20, transcendentals=0
        ),
        name="encode_own",
    )(one, m_b, row_a, row_b, row_c, row_d, weight)

    col_in = lax.all_gather(m_in, "lon", axis_index_groups=chips)
    side_scratch = [
        pltpu.VMEM((n1, BC + 2 * BR, CH), F32),
        pltpu.VMEM((3, n1, BC, CH), BF16),
    ]
    strip_in, two_in, first_in, order = pl.pallas_call(
        functools.partial(strip_kernel, rows, cols),
        out_shape=(
            array(few, BC, CH),
            array(tall, BC, CH),
            array(few, BC, CH),
            array(UP * cols, UP * cols),
        ),
        in_specs=[VMEM] * 7,
        out_specs=(VMEM,) * 4,
        scratch_shapes=side_scratch,
        compiler_params=params(16),
        cost_estimate=pl.CostEstimate(
            flops=2 * 9 * CH * CH * BC * few, bytes_accessed=4 << 20, transcendentals=0
        ),
        name="strip",
    )(own_two, own_one, ends_two, ends_one, edges, col_in, weight)

    width = -(-few * cols // 128) * 128
    sums, enc_one = pl.pallas_call(
        functools.partial(score_kernel, rows, cols),
        out_shape=(array(8, width, dtype=F32), array(few, cols, CH)),
        in_specs=[VMEM] * 10,
        out_specs=(VMEM, VMEM),
        scratch_shapes=side_scratch
        + [pltpu.VMEM((tall, cols, CH), BF16), pltpu.VMEM((few, cols, CH), BF16)],
        compiler_params=params(20),
        name="score",
    )(own_two, own_one, ends_two, ends_one, edges, strip_in, two_in, first_in, col_x, weight)
    sums_far = lax.ppermute(sums, "lon", far_lon)

    wt = mask_weight.reshape(CH, 9, UP, UP).transpose(1, 3, 2, 0).reshape(9 * UP * UP, CH)
    mix, inverse, sums_too = pl.pallas_call(
        functools.partial(mix_kernel, rows, cells),
        out_shape=(
            array(9, UP, UP, cells, dtype=F32),
            array(UP, UP, cells, dtype=F32),
            array(8, width, dtype=F32),
        ),
        in_specs=[VMEM] * 3,
        out_specs=(VMEM,) * 3,
        compiler_params=params(16),
        cost_estimate=pl.CostEstimate(
            flops=2 * 576 * CH * cells, bytes_accessed=4 * 576 * cells, transcendentals=576 * cells
        ),
        name="mix",
    )(enc_one, wt, sums)
    sums_in = lax.all_gather(sums_too, "lon", axis_index_groups=chips)
    return pl.pallas_call(
        functools.partial(up_kernel, rows, cols),
        out_shape=array(2, rows * UP, cols * UP, dtype=F32),
        in_specs=[VMEM] * 6,
        out_specs=pl.BlockSpec(memory_space=pl.ANY),
        scratch_shapes=[
            pltpu.VMEM((2, rows * UP, cols * UP), F32),
            pltpu.SemaphoreType.DMA((2 * cells // 128,)),
        ],
        compiler_params=params(16),
        name="upsample",
    )(sums, sums_far, sums_in, mix, inverse, order)


def solution(mesh):
    in_specs = (P("lat", "lon", None), P("lat", "lon", None), P(), P())
    return jax.shard_map(
        body, mesh=mesh, in_specs=in_specs, out_specs=P(None, "lat", "lon"), check_vma=False
    )
```

```python
import functools
import math

import jax
import jax.numpy as jnp
from jax import lax
from jax.experimental import pallas as pl
from jax.experimental.pallas import tpu as pltpu
from jax.sharding import PartitionSpec as P

CH = 256
BR = 8
BC = 16
UP = 8
F32 = jnp.float32
BF16 = jnp.bfloat16
VMEM = pl.BlockSpec(memory_space=pltpu.VMEM)


def params(mib):
    return pltpu.CompilerParams(vmem_limit_bytes=mib * 1024 * 1024)


def pair_perm(size, first, wrap, apart=1):
    out = []
    for i in range(size):
        if (i - first) % (2 * apart) >= apart:
            continue
        j = i + apart
        if j >= size:
            if not wrap:
                continue
            j -= size
        out += [(i, j), (j, i)]
    return out


def edge_kernel(rows, cols, f1, f2, m_a, m_b, m_c, m_d, g1, sems):
    band = lax.axis_index("lat")
    odd = band % 2
    upper = band % 4 // 2
    second = pltpu.make_async_copy(f2, m_a.at[pl.ds(0, rows)], sems.at[0])
    first = pltpu.make_async_copy(f1, g1, sems.at[1])
    second.start()
    first.start()
    second.wait()
    m_b[0:rows] = m_a[0:rows]
    for msg, low in ((m_c, upper), (m_d, 1 - upper)):
        msg[...] = m_a[pl.ds(low * (rows - 1), 1)]
    first.wait()
    for msg, low in ((m_a, odd), (m_b, 1 - odd)):
        msg[rows : rows + 2] = g1[pl.ds(low * (rows - 2), 2)]


def by_parity(lat_run, ra, rb, rc, rd):
    band = lax.axis_index("lat")
    for odd in (0, 1):
        for upper in (0, 1):

            @pl.when((band % 2 == odd) & (band % 4 // 2 == upper))
            def _():
                pair = (rb, ra) if odd else (ra, rb)
                lat_run(*pair, *((rd, rc) if upper else (rc, rd)))


def edge(msg, main_cols, extra, rim, col):
    n1, n2 = main_cols.shape[0], rim.shape[0]
    slots1, slots2 = -(-n1 // BC), -(-n2 // BC)
    msg[0:n1] = main_cols
    col[0:n1] = extra
    msg[n1 : n1 + slots1] = col[0 : slots1 * BC].astype(BF16).reshape(slots1, BC, CH)
    col[0:n2] = rim
    msg[n1 + slots1 :] = col[0 : slots2 * BC].astype(BF16).reshape(slots2, BC, CH)


def edge_places(cols, right):
    return (cols - BC, cols - BC - 1, cols - 1) if right else (0, BC, 0)


def pack_kernel(rows, cols, f1, f2, ra, rb, rc, rd, m_x, ext1, ext2, col):
    lon_odd = lax.axis_index("lon") % 2
    n2 = 3 * rows + 2
    n1 = rows + 4

    def halo(north, south, north_far, south_far):
        ext2[0:1] = north_far[...]
        ext2[1 : 1 + rows] = north[0:rows]
        ext2[1 + 2 * rows : 1 + 3 * rows] = south[0:rows]
        ext2[n2 - 1 : n2] = south_far[...]
        ext1[0:2] = north[rows : rows + 2]
        ext1[n1 - 2 : n1] = south[rows : rows + 2]

    ext2[1 + rows : 1 + 2 * rows] = f2[0:rows]
    ext1[2 : 2 + rows] = f1[...]
    by_parity(halo, ra, rb, rc, rd)

    def column(frame, at):
        base = at // BC * BC
        return frame[:, base : base + BC].astype(F32)[:, at - base, :]

    for odd in (0, 1):

        @pl.when(lon_odd == odd)
        def _():
            main, extra, one = edge_places(cols, odd == 1)
            edge(m_x, ext1[:, main : main + BC], column(ext1, extra), column(ext2, one), col)


def conv(x, w, row, count, width):
    lhs = jnp.concatenate(
        [
            x[b, row + a : row + a + count].reshape(count * width, CH)
            for a in range(3)
            for b in range(3)
        ],
        axis=1,
    )
    return jnp.dot(lhs, w[...], preferred_element_type=F32)


def own_kernel(
    rows, cols, f1, f2, ra, rb, rc, rd, w, e2, e1, ends2, ends1, m_in, edges, s2, s1, x2, x1, col
):
    lon_odd = lax.axis_index("lon") % 2
    n2 = 3 * rows + 2
    n1 = rows + 4
    own = slice(BR, BR + cols)

    def halo(north, south, north_far, south_far):
        s2[0:1, own] = north_far[...].astype(F32)
        s2[1 : 1 + rows, own] = north[0:rows].astype(F32)
        s2[1 + 2 * rows : 1 + 3 * rows, own] = south[0:rows].astype(F32)
        s2[n2 - 1 : n2, own] = south_far[...].astype(F32)
        s1[0:2, own] = north[rows : rows + 2].astype(F32)
        s1[n1 - 2 : n1, own] = south[rows : rows + 2].astype(F32)

    s2[1 + rows : 1 + 2 * rows, own] = f2[0:rows].astype(F32)
    s1[2 : 2 + rows, own] = f1[...].astype(F32)
    by_parity(halo, ra, rb, rc, rd)
    for s in (s2, s1):
        s[:, 0:BR] = jnp.zeros((s.shape[0], BR, CH), F32)
        s[:, BR + cols :] = jnp.zeros((s.shape[0], BR, CH), F32)
    for b in range(3):
        x2[b] = s2[:, BR - 1 + b : BR - 1 + b + cols].astype(BF16)
        x1[b] = s1[:, BR - 1 + b : BR - 1 + b + cols].astype(BF16)

    def run(x, out, ends, total):
        for r in range(0, total, 2 * BR):
            step = min(2 * BR, total - r)
            acc = conv(x, w, r, step, cols).reshape(step, cols, CH)
            out[r : r + step] = acc.astype(BF16)
            ends[0, r : r + step] = acc[:, 0, :]
            ends[1, r : r + step] = acc[:, cols - 1, :]

    run(x1, e1, ends1, rows + 2)
    run(x2, e2, ends2, 3 * rows)
    edges[0, 0:n1] = s1[:, BR, :]
    edges[1, 0:n1] = s1[:, BR + cols - 1, :]
    for odd in (0, 1):

        @pl.when(lon_odd == odd)
        def _():
            main, extra, one = edge_places(cols, odd == 0)
            edge(m_in, x1[1, :, main : main + BC], s1[:, BR + extra, :], s2[:, BR + one, :], col)


def finish_side(rows, cols, side, msg, w, o2, o1, ends2, ends1, edges, ext, xs, put):
    n2 = 3 * rows + 2
    n1 = rows + 4
    slots2 = -(-n2 // BC)
    slots1 = -(-n1 // BC)
    few, tall = rows + 2, 3 * rows
    extra = msg[n1 : n1 + slots1].astype(F32).reshape(slots1 * BC, CH)[0:n1]
    rim = msg[n1 + slots1 :].astype(F32).reshape(slots2 * BC, CH)[0:n2].astype(BF16)
    inner = edges[side, 0:n1]
    ext[:, BR : BR + BC] = msg[0:n1].astype(F32)
    ext[:, BR - 1 : BR] = (inner if side else extra)[:, None, :]
    ext[:, BR + BC : BR + BC + 1] = (extra if side else inner)[:, None, :]
    for b in range(3):
        xs[b] = ext[:, BR - 1 + b : BR - 1 + b + BC].astype(BF16)
    strip = conv(xs, w, 0, few, BC).astype(BF16).reshape(few, BC, CH)
    near = ext[:, BR : BR + 1] if side else ext[:, BR + BC - 1 : BR + BC]
    near = near[:, 0, :].astype(BF16)
    taps = jnp.concatenate(
        [w[(3 * a + 2 * side) * CH : (3 * a + 2 * side + 1) * CH] for a in range(3)], axis=0
    )
    lhs = jnp.concatenate(
        [jnp.concatenate([rim[a : a + tall], near[a : a + few]], axis=0) for a in range(3)],
        axis=1,
    )
    more = jnp.dot(lhs, taps, preferred_element_type=F32)
    hit = lax.broadcasted_iota(jnp.int32, (1, BC, CH), 1) == (BC - 1 if side else 0)
    lo = cols - BC if side else 0
    full = ends2[side, 0:tall] + more[0:tall]
    two = jnp.where(hit, full[:, None, :], o2[:, lo : lo + BC].astype(F32)).astype(BF16)
    full = ends1[side, 0:few] + more[tall : tall + few]
    first = jnp.where(hit, full[:, None, :], o1[:, lo : lo + BC].astype(F32)).astype(BF16)
    put(side, strip, two, first)


def strip_kernel(
    rows, cols, o2, o1, ends2, ends1, edges, chip, w, strip, two, first, order, ext, xs
):
    src = lax.broadcasted_iota(jnp.int32, order.shape, 0)
    dst = lax.broadcasted_iota(jnp.int32, order.shape, 1)
    to = (src % cols) * UP + src // cols
    order[...] = jnp.where(dst == to, 1.0, 0.0).astype(BF16)
    lon_odd = lax.axis_index("lon") % 2
    msg = chip.at[1 - lon_odd]

    def put(side, *values):
        for ref, value in zip((strip, two, first), values):
            ref[...] = value

    for odd in (0, 1):

        @pl.when(lon_odd == odd)
        def _():
            finish_side(rows, cols, 1 - odd, msg, w, o2, o1, ends2, ends1, edges, ext, xs, put)


def score_kernel(
    rows, cols, o2, o1, ends2, ends1, edges, strip_in, two_in, first_in, c_x, w,
    sums, enc_one, ext, xs, e2, beside,
):
    lat = lax.axis_index("lat")
    lon_odd = lax.axis_index("lon") % 2

    def put(side, strip, two, first):
        lo = cols - BC if side else 0
        e2[:, lo : lo + BC] = two
        enc_one[:, lo : lo + BC] = first
        lo = 0 if side else cols - BC
        beside[:, lo : lo + BC] = strip

    for odd in (0, 1):

        @pl.when(lon_odd == odd)
        def _():
            put(1 - odd, strip_in[...], two_in[...], first_in[...])
            finish_side(rows, cols, odd, c_x, w, o2, o1, ends2, ends1, edges, ext, xs, put)

    bands = rows // BR
    last = lax.axis_size("lat") - 1
    scale = 1.0 / math.sqrt(CH)
    groups = cols // BR

    def features(ref, row, count):
        flat = ref[row : row + count].reshape(count * cols, CH).astype(F32)
        return (flat * scale).astype(BF16)

    def scores(block, query):
        keys = e2[block * BR : (block + 3) * BR].reshape(3 * BR * cols, CH)
        return lax.dot_general(
            keys, query, (((1,), (1,)), ((), ())), preferred_element_type=F32
        ).reshape(3, BR, groups, BR, query.shape[0])

    def add(total, now):
        return now if total is None else [p + e for p, e in zip(total, now)]

    def triple(pieces, by_row, sub, base):
        mass = pieces[0]
        octs = None
        for i, piece in enumerate(pieces[1:], 1):
            mass = mass + piece
            octs = piece * float(i) if octs is None else octs + piece * float(i)
        across = octs * 8.0 + mass * (sub if base is None else sub + base)
        return [jnp.sum(v, axis=0, keepdims=True) for v in (mass, by_row, across)]

    queries = BR * cols
    sub = lax.broadcasted_iota(jnp.int32, (BR, queries), 0).astype(F32)
    of_right = lax.broadcasted_iota(jnp.int32, (BR, queries), 1) % cols < BC
    base = jnp.where(of_right, float(BC - cols), float(cols))
    for g in range(bands):
        query_own = features(enc_one, 1 + g * BR, BR)
        query_side = features(beside, 1 + g * BR, BR)
        acc = None
        of_own = scores(g + 1, query_own)
        of_side = scores(g + 1, query_side)
        for kb in range(3):
            mine, other = of_own[kb], of_side[kb]
            part = None
            for kr in range(BR):
                row = float((kb - 1) * BR + kr)
                own = [jnp.exp(mine[kr, i]) for i in range(4)]
                side = [
                    jnp.exp(jnp.where(of_right, other[kr, 2 + i], other[kr, i])) for i in range(2)
                ]
                now = own + [row * ((own[0] + own[1]) + (own[2] + own[3]))]
                now += side + [row * (side[0] + side[1])]
                part = add(part, now)
            if kb == 0 and g == 0:
                part = [jnp.where(lat > 0, p, 0.0) for p in part]
            elif kb == 2 and g == bands - 1:
                part = [jnp.where(lat < last, p, 0.0) for p in part]
            acc = add(acc, part)
        values = triple(acc[0:4], acc[4], sub, None) + triple(acc[5:7], acc[7], sub, base)
        values += [jnp.zeros((2, queries), F32)]
        sums[:, cols + g * queries : cols + (g + 1) * queries] = jnp.concatenate(values, axis=0)

    quarter = cols
    lanes = 4 * quarter
    sub = lax.broadcasted_iota(jnp.int32, (BR, lanes), 0).astype(F32)
    lane = lax.broadcasted_iota(jnp.int32, (BR, lanes), 1)
    below = lane >= 2 * quarter
    spot = lane % (2 * quarter)
    is_own = spot < quarter
    of_right = (spot >= quarter) & (spot < quarter + BC)
    base = jnp.where(is_own, 0.0, jnp.where(of_right, float(BC - cols), float(cols)))
    query = jnp.concatenate(
        [features(r, at, 1) for at in (0, rows + 1) for r in (enc_one, beside)], axis=0
    )
    acc = None
    all_over = scores(0, query)
    all_under = scores(bands + 1, query)
    for kb in range(3):
        over, under = all_over[kb], all_under[kb]
        for kr in range(BR):
            row = float((kb - 1) * BR + kr)
            both = [jnp.where(below, under[kr, i], over[kr, i]) for i in range(4)]
            now = [jnp.exp(jnp.where(of_right, both[2 + i], both[i])) for i in range(2)]
            now += [jnp.where(is_own, jnp.exp(both[i]), 0.0) for i in range(2, 4)]
            now += [row * ((now[0] + now[1]) + (now[2] + now[3]))]
            acc = add(acc, now)
    values = triple(acc[0:4], acc[4], sub, base)
    for k, at in enumerate((0, cols + rows * cols)):
        for m in range(2):
            lo = (2 * k + m) * quarter
            sums[3 * m : 3 * m + 3, at : at + cols] = jnp.concatenate(
                [v[:, lo : lo + quarter] for v in values], axis=0
            )
        sums[6:8, at : at + cols] = jnp.zeros((2, cols), F32)


def mix_kernel(rows, cells, enc_one, wt, sums, mix, total, passed):
    passed[...] = sums[...]
    feats = enc_one[1 : 1 + rows].reshape(cells, CH)
    step = 256
    count = UP * UP
    for c0 in range(0, cells, step):
        logits = lax.dot_general(
            wt[...], feats[c0 : c0 + step], (((1,), (1,)), ((), ())), preferred_element_type=F32
        )
        mass = None
        for n in range(9):
            expo = jnp.exp(logits[n * count : (n + 1) * count]).reshape(UP, UP, step)
            mix[n, :, :, c0 : c0 + step] = expo
            mass = expo if mass is None else mass + expo
        total[:, :, c0 : c0 + step] = 1.0 / mass


def up_kernel(rows, cols, mine, far, chip, mix, inverse, order_ref, out, fine, sems):
    lat = lax.axis_index("lat")
    last = lax.axis_size("lat") - 1
    lon_odd = lax.axis_index("lon") % 2
    cells = rows * cols
    width = mine.shape[1]
    lane = lax.broadcasted_iota(jnp.int32, (1, width), 1)
    column = lane % cols
    row = ((lane // cols + BR - 1) % BR).astype(F32)
    outside = ((lane < cols) & (lat == 0)) | ((lane >= cols + cells) & (lat == last))
    partner = chip[1 - lon_odd]
    is_odd = jnp.broadcast_to(lon_odd == 1, partner.shape)
    left = jnp.where(is_odd, partner, far[...])
    right = jnp.where(is_odd, far[...], partner)
    own = mine[...]

    def flow(total):
        both = jnp.concatenate(
            [total[1:2] / total[0:1] - row, total[2:3] / total[0:1] - column.astype(F32)], axis=0
        )
        return jnp.where(outside, 0.0, both * float(UP))

    mid = flow(own[0:3] + jnp.where(column < BC, left[3:6], right[3:6]))
    west = flow(left[0:3] + own[3:6])
    east = flow(right[0:3] + own[3:6])
    west = jnp.where(
        column == 0, pltpu.roll(west, width - (cols - 1), 1), pltpu.roll(mid, 1, 1)
    )
    east = jnp.where(
        column == cols - 1, pltpu.roll(east, cols - 1, 1), pltpu.roll(mid, width - 1, 1)
    )
    shifted = []
    for a in range(3):
        for field in (west, mid, east):
            moved = field if a == 0 else pltpu.roll(field, width - a * cols, 1)
            shifted.append(moved[:, 0:cells])
    order = order_ref[...]
    tile = 128
    group = tile // cols
    lane = lax.broadcasted_iota(jnp.int32, (UP, tile), 1)
    bits = []
    span = 1
    while span < group:
        bits.append((span, (lane // (span * cols)) % 2 == 1))
        span *= 2
    count = group * UP
    copies = []
    for t in range(cells // tile):
        here = slice(t * tile, (t + 1) * tile)
        flows = [
            [jnp.broadcast_to(v[d : d + 1, here], (UP, tile)) for v in shifted] for d in range(2)
        ]
        lanes_of = [[[None] * (UP // group) for _ in range(group)] for _ in range(2)]
        for u in range(UP // group):
            blocks = [[], []]
            for k in range(group):
                at = u * group + k
                scale = inverse[at, :, here]
                weights = [mix[n, at, :, here] for n in range(9)]
                for d in range(2):
                    acc = weights[0] * flows[d][0]
                    for n in range(1, 9):
                        acc = acc + weights[n] * flows[d][n]
                    blocks[d].append(acc * scale)
            for d in range(2):
                block = blocks[d]
                for span, high in bits:
                    shift = span * cols
                    done = list(block)
                    for k in range(group):
                        if k & span:
                            continue
                        lo_v, hi_v = block[k], block[k | span]
                        done[k] = jnp.where(high, pltpu.roll(hi_v, shift, 1), lo_v)
                        done[k | span] = jnp.where(
                            high, hi_v, pltpu.roll(lo_v, tile - shift, 1)
                        )
                    block = done
                for k in range(group):
                    lanes_of[d][k][u] = block[k]
        value = jnp.concatenate(
            [jnp.concatenate(v, axis=1) for d in range(2) for v in lanes_of[d]], axis=0
        )
        high_part = value.astype(BF16)
        low_part = (value - high_part.astype(F32)).astype(BF16)
        both = jnp.dot(
            jnp.concatenate([high_part, low_part], axis=0), order, preferred_element_type=F32
        )
        both = both[0 : 2 * count] + both[2 * count :]
        for d in range(2):
            fine[d, t * count : (t + 1) * count] = both[d * count : (d + 1) * count]
        part = pl.ds(t * count, count)
        copy = pltpu.make_async_copy(fine.at[:, part], out.at[:, part], sems.at[t])
        copy.start()
        copies.append(copy)
    for copy in copies:
        copy.wait()


def body(frame_one, frame_two, enc_weight, mask_weight):
    rows, cols = frame_one.shape[0], frame_one.shape[1]
    cells = rows * cols
    n2, n1, few, tall = 3 * rows + 2, rows + 4, rows + 2, 3 * rows
    n2_pad = -(-n2 // BC) * BC
    slots = n1 + n2_pad // BC + -(-n1 // BC)
    lats, lons = lax.axis_size("lat"), lax.axis_size("lon")
    far_lat = pair_perm(lats, 1, False)
    near_lat = pair_perm(lats, 0, False)
    low_lat = pair_perm(lats, 0, False, 2)
    high_lat = pair_perm(lats, 2, False, 2)
    far_lon = pair_perm(lons, 1, True)
    chips = [[i, i + 1] for i in range(0, lons, 2)]

    def array(*shape, dtype=BF16):
        return jax.ShapeDtypeStruct(shape, dtype)

    tile = array(rows, cols, CH)
    m_a, m_b, m_c, m_d, one = pl.pallas_call(
        functools.partial(edge_kernel, rows, cols),
        out_shape=(array(few, cols, CH),) * 2 + (array(1, cols, CH),) * 2 + (tile,),
        in_specs=[pl.BlockSpec(memory_space=pltpu.MemorySpace.HBM)] * 2,
        out_specs=(VMEM,) * 5,
        scratch_shapes=[pltpu.SemaphoreType.DMA((2,))],
        compiler_params=params(8),
        name="edges",
    )(
        pltpu.with_memory_space_constraint(frame_one, pltpu.MemorySpace.HBM),
        pltpu.with_memory_space_constraint(frame_two, pltpu.MemorySpace.HBM),
    )
    row_a = lax.ppermute(m_a, "lat", far_lat)
    row_b = lax.ppermute(m_b, "lat", near_lat)
    row_c = lax.ppermute(m_c, "lat", high_lat)
    row_d = lax.ppermute(m_d, "lat", low_lat)

    m_x = pl.pallas_call(
        functools.partial(pack_kernel, rows, cols),
        out_shape=array(slots, BC, CH),
        in_specs=[VMEM] * 6,
        out_specs=VMEM,
        scratch_shapes=[
            pltpu.VMEM((n1, cols, CH), BF16),
            pltpu.VMEM((n2, cols, CH), BF16),
            pltpu.VMEM((n2_pad, CH), F32),
        ],
        compiler_params=params(16),
        name="pack",
    )(one, m_b, row_a, row_b, row_c, row_d)
    col_x = lax.ppermute(m_x, "lon", far_lon)

    weight = enc_weight.reshape(9 * CH, CH)
    few_pad = -(-few // BR) * BR
    own_two, own_one, ends_two, ends_one, m_in, edges = pl.pallas_call(
        functools.partial(own_kernel, rows, cols),
        out_shape=(
            array(tall, cols, CH),
            array(few, cols, CH),
            array(2, tall, CH, dtype=F32),
            array(2, few_pad, CH, dtype=F32),
            array(slots, BC, CH),
            array(2, -(-n1 // BR) * BR, CH, dtype=F32),
        ),
        in_specs=[VMEM] * 7,
        out_specs=(VMEM,) * 6,
        scratch_shapes=[
            pltpu.VMEM((n2, cols + 2 * BR, CH), F32),
            pltpu.VMEM((n1, cols + 2 * BR, CH), F32),
            pltpu.VMEM((3, n2, cols, CH), BF16),
            pltpu.VMEM((3, n1, cols, CH), BF16),
            pltpu.VMEM((n2_pad, CH), F32),
        ],
        compiler_params=params(24),
        cost_estimate=pl.CostEstimate(
            flops=2 * 9 * CH * CH * cols * (tall + few), bytes_accessed=4 << 20, transcendentals=0
        ),
        name="encode_own",
    )(one, m_b, row_a, row_b, row_c, row_d, weight)

    col_in = lax.all_gather(m_in, "lon", axis_index_groups=chips)
    side_scratch = [
        pltpu.VMEM((n1, BC + 2 * BR, CH), F32),
        pltpu.VMEM((3, n1, BC, CH), BF16),
    ]
    strip_in, two_in, first_in, order = pl.pallas_call(
        functools.partial(strip_kernel, rows, cols),
        out_shape=(
            array(few, BC, CH),
            array(tall, BC, CH),
            array(few, BC, CH),
            array(UP * cols, UP * cols),
        ),
        in_specs=[VMEM] * 7,
        out_specs=(VMEM,) * 4,
        scratch_shapes=side_scratch,
        compiler_params=params(16),
        cost_estimate=pl.CostEstimate(
            flops=2 * 9 * CH * CH * BC * few, bytes_accessed=4 << 20, transcendentals=0
        ),
        name="strip",
    )(own_two, own_one, ends_two, ends_one, edges, col_in, weight)

    width = -(-few * cols // 128) * 128
    sums, enc_one = pl.pallas_call(
        functools.partial(score_kernel, rows, cols),
        out_shape=(array(8, width, dtype=F32), array(few, cols, CH)),
        in_specs=[VMEM] * 10,
        out_specs=(VMEM, VMEM),
        scratch_shapes=side_scratch
        + [pltpu.VMEM((tall, cols, CH), BF16), pltpu.VMEM((few, cols, CH), BF16)],
        compiler_params=params(20),
        name="score",
    )(own_two, own_one, ends_two, ends_one, edges, strip_in, two_in, first_in, col_x, weight)
    sums_far = lax.ppermute(sums, "lon", far_lon)

    wt = mask_weight.reshape(CH, 9, UP, UP).transpose(1, 3, 2, 0).reshape(9 * UP * UP, CH)
    mix, inverse, sums_too = pl.pallas_call(
        functools.partial(mix_kernel, rows, cells),
        out_shape=(
            array(9, UP, UP, cells, dtype=F32),
            array(UP, UP, cells, dtype=F32),
            array(8, width, dtype=F32),
        ),
        in_specs=[VMEM] * 3,
        out_specs=(VMEM,) * 3,
        compiler_params=params(16),
        cost_estimate=pl.CostEstimate(
            flops=2 * 576 * CH * cells, bytes_accessed=4 * 576 * cells, transcendentals=576 * cells
        ),
        name="mix",
    )(enc_one, wt, sums)
    sums_in = lax.all_gather(sums_too, "lon", axis_index_groups=chips)
    return pl.pallas_call(
        functools.partial(up_kernel, rows, cols),
        out_shape=array(2, rows * UP, cols * UP, dtype=F32),
        in_specs=[VMEM] * 6,
        out_specs=pl.BlockSpec(memory_space=pl.ANY),
        scratch_shapes=[
            pltpu.VMEM((2, rows * UP, cols * UP), F32),
            pltpu.SemaphoreType.DMA((cells // 128,)),
        ],
        compiler_params=params(16),
        name="upsample",
    )(sums, sums_far, sums_in, mix, inverse, order)


def solution(mesh):
    in_specs = (P("lat", "lon", None), P("lat", "lon", None), P(), P())
    return jax.shard_map(
        body, mesh=mesh, in_specs=in_specs, out_specs=P(None, "lat", "lon"), check_vma=False
    )
```

```python
import functools
import math

import jax
import jax.numpy as jnp
from jax import lax
from jax.experimental import pallas as pl
from jax.experimental.pallas import tpu as pltpu
from jax.sharding import PartitionSpec as P

CH = 256
BR = 8
BC = 16
UP = 8
F32 = jnp.float32
BF16 = jnp.bfloat16
VMEM = pl.BlockSpec(memory_space=pltpu.VMEM)


def params(mib):
    return pltpu.CompilerParams(vmem_limit_bytes=mib * 1024 * 1024)


def pair_perm(size, first, wrap, apart=1):
    out = []
    for i in range(size):
        if (i - first) % (2 * apart) >= apart:
            continue
        j = i + apart
        if j >= size:
            if not wrap:
                continue
            j -= size
        out += [(i, j), (j, i)]
    return out


def edge_kernel(rows, cols, f1, f2, m_a, m_b, m_c, m_d, g1, sems):
    band = lax.axis_index("lat")
    odd = band % 2
    upper = band % 4 // 2
    second = pltpu.make_async_copy(f2, m_a.at[pl.ds(0, rows)], sems.at[0])
    first = pltpu.make_async_copy(f1, g1, sems.at[1])
    second.start()
    first.start()
    second.wait()
    m_b[0:rows] = m_a[0:rows]
    for msg, low in ((m_c, upper), (m_d, 1 - upper)):
        msg[...] = m_a[pl.ds(low * (rows - 1), 1)]
    first.wait()
    for msg, low in ((m_a, odd), (m_b, 1 - odd)):
        msg[rows : rows + 2] = g1[pl.ds(low * (rows - 2), 2)]


def by_parity(lat_run, ra, rb, rc, rd):
    band = lax.axis_index("lat")
    for odd in (0, 1):
        for upper in (0, 1):

            @pl.when((band % 2 == odd) & (band % 4 // 2 == upper))
            def _():
                pair = (rb, ra) if odd else (ra, rb)
                lat_run(*pair, *((rd, rc) if upper else (rc, rd)))


def edge(msg, main_cols, extra, rim, col):
    n1, n2 = main_cols.shape[0], rim.shape[0]
    msg[0:n1] = main_cols
    col[0:n1] = extra
    col[n1 : n1 + n2] = rim
    msg[n1:] = col[...].astype(BF16).reshape(-1, BC, CH)


def edge_places(cols, right):
    return (cols - BC, cols - BC - 1, cols - 1) if right else (0, BC, 0)


def pack_kernel(rows, cols, f1, f2, ra, rb, rc, rd, m_x, ext1, ext2, col):
    lon_odd = lax.axis_index("lon") % 2
    n2 = 3 * rows + 2
    n1 = rows + 4

    def halo(north, south, north_far, south_far):
        ext2[0:1] = north_far[...]
        ext2[1 : 1 + rows] = north[0:rows]
        ext2[1 + 2 * rows : 1 + 3 * rows] = south[0:rows]
        ext2[n2 - 1 : n2] = south_far[...]
        ext1[0:2] = north[rows : rows + 2]
        ext1[n1 - 2 : n1] = south[rows : rows + 2]

    ext2[1 + rows : 1 + 2 * rows] = f2[0:rows]
    ext1[2 : 2 + rows] = f1[...]
    by_parity(halo, ra, rb, rc, rd)

    def column(frame, at):
        base = at // BC * BC
        return frame[:, base : base + BC].astype(F32)[:, at - base, :]

    for odd in (0, 1):

        @pl.when(lon_odd == odd)
        def _():
            main, extra, one = edge_places(cols, odd == 1)
            edge(m_x, ext1[:, main : main + BC], column(ext1, extra), column(ext2, one), col)


def conv(x, w, row, count, width):
    lhs = jnp.concatenate(
        [
            x[b, row + a : row + a + count].reshape(count * width, CH)
            for a in range(3)
            for b in range(3)
        ],
        axis=1,
    )
    return jnp.dot(lhs, w[...], preferred_element_type=F32)


def own_kernel(
    rows, cols, f1, f2, ra, rb, rc, rd, w, e2, e1, ends2, ends1, m_in, edges, s2, s1, x2, x1, col
):
    lon_odd = lax.axis_index("lon") % 2
    n2 = 3 * rows + 2
    n1 = rows + 4
    own = slice(BR, BR + cols)

    def halo(north, south, north_far, south_far):
        s2[0:1, own] = north_far[...].astype(F32)
        s2[1 : 1 + rows, own] = north[0:rows].astype(F32)
        s2[1 + 2 * rows : 1 + 3 * rows, own] = south[0:rows].astype(F32)
        s2[n2 - 1 : n2, own] = south_far[...].astype(F32)
        s1[0:2, own] = north[rows : rows + 2].astype(F32)
        s1[n1 - 2 : n1, own] = south[rows : rows + 2].astype(F32)

    s2[1 + rows : 1 + 2 * rows, own] = f2[0:rows].astype(F32)
    s1[2 : 2 + rows, own] = f1[...].astype(F32)
    by_parity(halo, ra, rb, rc, rd)
    for s in (s2, s1):
        s[:, 0:BR] = jnp.zeros((s.shape[0], BR, CH), F32)
        s[:, BR + cols :] = jnp.zeros((s.shape[0], BR, CH), F32)
    for b in range(3):
        x2[b] = s2[:, BR - 1 + b : BR - 1 + b + cols].astype(BF16)
        x1[b] = s1[:, BR - 1 + b : BR - 1 + b + cols].astype(BF16)

    def run(x, out, ends, total):
        for r in range(0, total, 2 * BR):
            step = min(2 * BR, total - r)
            acc = conv(x, w, r, step, cols).reshape(step, cols, CH)
            out[r : r + step] = acc.astype(BF16)
            ends[0, r : r + step] = acc[:, 0, :]
            ends[1, r : r + step] = acc[:, cols - 1, :]

    run(x1, e1, ends1, rows + 2)
    run(x2, e2, ends2, 3 * rows)
    edges[0, 0:n1] = s1[:, BR, :]
    edges[1, 0:n1] = s1[:, BR + cols - 1, :]
    for odd in (0, 1):

        @pl.when(lon_odd == odd)
        def _():
            main, extra, one = edge_places(cols, odd == 0)
            edge(m_in, x1[1, :, main : main + BC], s1[:, BR + extra, :], s2[:, BR + one, :], col)


def finish_side(rows, cols, side, msg, w, o2, o1, ends2, ends1, edges, ext, xs, put):
    n2 = 3 * rows + 2
    n1 = rows + 4
    few, tall = rows + 2, 3 * rows
    singles = msg[n1:].astype(F32).reshape(-1, CH)
    extra = singles[0:n1]
    rim = singles[n1 : n1 + n2].astype(BF16)
    inner = edges[side, 0:n1]
    ext[:, BR : BR + BC] = msg[0:n1].astype(F32)
    ext[:, BR - 1 : BR] = (inner if side else extra)[:, None, :]
    ext[:, BR + BC : BR + BC + 1] = (extra if side else inner)[:, None, :]
    for b in range(3):
        xs[b] = ext[:, BR - 1 + b : BR - 1 + b + BC].astype(BF16)
    strip = conv(xs, w, 0, few, BC).astype(BF16).reshape(few, BC, CH)
    near = ext[:, BR : BR + 1] if side else ext[:, BR + BC - 1 : BR + BC]
    near = near[:, 0, :].astype(BF16)
    taps = jnp.concatenate(
        [w[(3 * a + 2 * side) * CH : (3 * a + 2 * side + 1) * CH] for a in range(3)], axis=0
    )
    lhs = jnp.concatenate(
        [jnp.concatenate([rim[a : a + tall], near[a : a + few]], axis=0) for a in range(3)],
        axis=1,
    )
    more = jnp.dot(lhs, taps, preferred_element_type=F32)
    hit = lax.broadcasted_iota(jnp.int32, (1, BC, CH), 1) == (BC - 1 if side else 0)
    lo = cols - BC if side else 0
    full = ends2[side, 0:tall] + more[0:tall]
    two = jnp.where(hit, full[:, None, :], o2[:, lo : lo + BC].astype(F32)).astype(BF16)
    full = ends1[side, 0:few] + more[tall : tall + few]
    first = jnp.where(hit, full[:, None, :], o1[:, lo : lo + BC].astype(F32)).astype(BF16)
    put(side, strip, two, first)


def strip_kernel(
    rows, cols, o2, o1, ends2, ends1, edges, chip, w, strip, two, first, order, ext, xs
):
    src = lax.broadcasted_iota(jnp.int32, order.shape, 0)
    dst = lax.broadcasted_iota(jnp.int32, order.shape, 1)
    to = (src % cols) * UP + src // cols
    order[...] = jnp.where(dst == to, 1.0, 0.0).astype(BF16)
    lon_odd = lax.axis_index("lon") % 2
    msg = chip.at[1 - lon_odd]

    def put(side, *values):
        for ref, value in zip((strip, two, first), values):
            ref[...] = value

    for odd in (0, 1):

        @pl.when(lon_odd == odd)
        def _():
            finish_side(rows, cols, 1 - odd, msg, w, o2, o1, ends2, ends1, edges, ext, xs, put)


def score_kernel(
    rows, cols, o2, o1, ends2, ends1, edges, strip_in, two_in, first_in, c_x, w,
    sums, enc_one, ext, xs, e2, beside,
):
    lat = lax.axis_index("lat")
    lon_odd = lax.axis_index("lon") % 2

    def put(side, strip, two, first):
        lo = cols - BC if side else 0
        e2[:, lo : lo + BC] = two
        enc_one[:, lo : lo + BC] = first
        lo = 0 if side else cols - BC
        beside[:, lo : lo + BC] = strip

    for odd in (0, 1):

        @pl.when(lon_odd == odd)
        def _():
            put(1 - odd, strip_in[...], two_in[...], first_in[...])
            finish_side(rows, cols, odd, c_x, w, o2, o1, ends2, ends1, edges, ext, xs, put)

    bands = rows // BR
    last = lax.axis_size("lat") - 1
    scale = 1.0 / math.sqrt(CH)
    groups = cols // BR

    def features(ref, row, count):
        flat = ref[row : row + count].reshape(count * cols, CH).astype(F32)
        return (flat * scale).astype(BF16)

    def scores(block, query):
        keys = e2[block * BR : (block + 3) * BR].reshape(3 * BR * cols, CH)
        return lax.dot_general(
            keys, query, (((1,), (1,)), ((), ())), preferred_element_type=F32
        ).reshape(3, BR, groups, BR, query.shape[0])

    def add(total, now):
        return now if total is None else [p + e for p, e in zip(total, now)]

    def triple(pieces, by_row, sub, base):
        mass = pieces[0]
        octs = None
        for i, piece in enumerate(pieces[1:], 1):
            mass = mass + piece
            octs = piece * float(i) if octs is None else octs + piece * float(i)
        across = octs * 8.0 + mass * (sub if base is None else sub + base)
        return [jnp.sum(v, axis=0, keepdims=True) for v in (mass, by_row, across)]

    queries = BR * cols
    sub = lax.broadcasted_iota(jnp.int32, (BR, queries), 0).astype(F32)
    of_right = lax.broadcasted_iota(jnp.int32, (BR, queries), 1) % cols < BC
    base = jnp.where(of_right, float(BC - cols), float(cols))
    for g in range(bands):
        query_own = features(enc_one, 1 + g * BR, BR)
        query_side = features(beside, 1 + g * BR, BR)
        acc = None
        of_own = scores(g + 1, query_own)
        of_side = scores(g + 1, query_side)
        for kb in range(3):
            mine, other = of_own[kb], of_side[kb]
            part = None
            for kr in range(BR):
                row = float((kb - 1) * BR + kr)
                own = [jnp.exp(mine[kr, i]) for i in range(4)]
                side = [
                    jnp.exp(jnp.where(of_right, other[kr, 2 + i], other[kr, i])) for i in range(2)
                ]
                now = own + [row * ((own[0] + own[1]) + (own[2] + own[3]))]
                now += side + [row * (side[0] + side[1])]
                part = add(part, now)
            if kb == 0 and g == 0:
                part = [jnp.where(lat > 0, p, 0.0) for p in part]
            elif kb == 2 and g == bands - 1:
                part = [jnp.where(lat < last, p, 0.0) for p in part]
            acc = add(acc, part)
        values = triple(acc[0:4], acc[4], sub, None) + triple(acc[5:7], acc[7], sub, base)
        values += [jnp.zeros((2, queries), F32)]
        sums[:, cols + g * queries : cols + (g + 1) * queries] = jnp.concatenate(values, axis=0)

    quarter = cols
    lanes = 4 * quarter
    sub = lax.broadcasted_iota(jnp.int32, (BR, lanes), 0).astype(F32)
    lane = lax.broadcasted_iota(jnp.int32, (BR, lanes), 1)
    below = lane >= 2 * quarter
    spot = lane % (2 * quarter)
    is_own = spot < quarter
    of_right = (spot >= quarter) & (spot < quarter + BC)
    base = jnp.where(is_own, 0.0, jnp.where(of_right, float(BC - cols), float(cols)))
    query = jnp.concatenate(
        [features(r, at, 1) for at in (0, rows + 1) for r in (enc_one, beside)], axis=0
    )
    acc = None
    all_over = scores(0, query)
    all_under = scores(bands + 1, query)
    for kb in range(3):
        over, under = all_over[kb], all_under[kb]
        for kr in range(BR):
            row = float((kb - 1) * BR + kr)
            both = [jnp.where(below, under[kr, i], over[kr, i]) for i in range(4)]
            now = [jnp.exp(jnp.where(of_right, both[2 + i], both[i])) for i in range(2)]
            now += [jnp.where(is_own, jnp.exp(both[i]), 0.0) for i in range(2, 4)]
            now += [row * ((now[0] + now[1]) + (now[2] + now[3]))]
            acc = add(acc, now)
    values = triple(acc[0:4], acc[4], sub, base)
    for k, at in enumerate((0, cols + rows * cols)):
        for m in range(2):
            lo = (2 * k + m) * quarter
            sums[3 * m : 3 * m + 3, at : at + cols] = jnp.concatenate(
                [v[:, lo : lo + quarter] for v in values], axis=0
            )
        sums[6:8, at : at + cols] = jnp.zeros((2, cols), F32)


def mix_kernel(rows, cells, enc_one, wt, sums, mix, total, passed):
    passed[...] = sums[...]
    feats = enc_one[1 : 1 + rows].reshape(cells, CH)
    step = 256
    count = UP * UP
    for c0 in range(0, cells, step):
        logits = lax.dot_general(
            wt[...], feats[c0 : c0 + step], (((1,), (1,)), ((), ())), preferred_element_type=F32
        )
        mass = None
        for n in range(9):
            expo = jnp.exp(logits[n * count : (n + 1) * count]).reshape(UP, UP, step)
            mix[n, :, :, c0 : c0 + step] = expo
            mass = expo if mass is None else mass + expo
        total[:, :, c0 : c0 + step] = 1.0 / mass


def up_kernel(rows, cols, mine, far, chip, mix, inverse, order_ref, out, fine, sems):
    lat = lax.axis_index("lat")
    last = lax.axis_size("lat") - 1
    lon_odd = lax.axis_index("lon") % 2
    cells = rows * cols
    width = mine.shape[1]
    lane = lax.broadcasted_iota(jnp.int32, (1, width), 1)
    column = lane % cols
    row = ((lane // cols + BR - 1) % BR).astype(F32)
    outside = ((lane < cols) & (lat == 0)) | ((lane >= cols + cells) & (lat == last))
    partner = chip[1 - lon_odd]
    is_odd = jnp.broadcast_to(lon_odd == 1, partner.shape)
    left = jnp.where(is_odd, partner, far[...])
    right = jnp.where(is_odd, far[...], partner)
    own = mine[...]

    def flow(total):
        both = jnp.concatenate(
            [total[1:2] / total[0:1] - row, total[2:3] / total[0:1] - column.astype(F32)], axis=0
        )
        return jnp.where(outside, 0.0, both * float(UP))

    mid = flow(own[0:3] + jnp.where(column < BC, left[3:6], right[3:6]))
    west = flow(left[0:3] + own[3:6])
    east = flow(right[0:3] + own[3:6])
    west = jnp.where(
        column == 0, pltpu.roll(west, width - (cols - 1), 1), pltpu.roll(mid, 1, 1)
    )
    east = jnp.where(
        column == cols - 1, pltpu.roll(east, cols - 1, 1), pltpu.roll(mid, width - 1, 1)
    )
    shifted = []
    for a in range(3):
        for field in (west, mid, east):
            moved = field if a == 0 else pltpu.roll(field, width - a * cols, 1)
            shifted.append(moved[:, 0:cells])
    order = order_ref[...]
    tile = 128
    group = tile // cols
    lane = lax.broadcasted_iota(jnp.int32, (UP, tile), 1)
    bits = []
    span = 1
    while span < group:
        bits.append((span, (lane // (span * cols)) % 2 == 1))
        span *= 2
    count = group * UP
    copies = []
    for t in range(cells // tile):
        here = slice(t * tile, (t + 1) * tile)
        flows = [
            [jnp.broadcast_to(v[d : d + 1, here], (UP, tile)) for v in shifted] for d in range(2)
        ]
        lanes_of = [[[None] * (UP // group) for _ in range(group)] for _ in range(2)]
        for u in range(UP // group):
            blocks = [[], []]
            for k in range(group):
                at = u * group + k
                scale = inverse[at, :, here]
                weights = [mix[n, at, :, here] for n in range(9)]
                for d in range(2):
                    acc = weights[0] * flows[d][0]
                    for n in range(1, 9):
                        acc = acc + weights[n] * flows[d][n]
                    blocks[d].append(acc * scale)
            for d in range(2):
                block = blocks[d]
                for span, high in bits:
                    shift = span * cols
                    done = list(block)
                    for k in range(group):
                        if k & span:
                            continue
                        lo_v, hi_v = block[k], block[k | span]
                        done[k] = jnp.where(high, pltpu.roll(hi_v, shift, 1), lo_v)
                        done[k | span] = jnp.where(
                            high, hi_v, pltpu.roll(lo_v, tile - shift, 1)
                        )
                    block = done
                for k in range(group):
                    lanes_of[d][k][u] = block[k]
        value = jnp.concatenate(
            [jnp.concatenate(v, axis=1) for d in range(2) for v in lanes_of[d]], axis=0
        )
        high_part = value.astype(BF16)
        low_part = (value - high_part.astype(F32)).astype(BF16)
        both = jnp.dot(
            jnp.concatenate([high_part, low_part], axis=0), order, preferred_element_type=F32
        )
        both = both[0 : 2 * count] + both[2 * count :]
        for d in range(2):
            fine[d, t * count : (t + 1) * count] = both[d * count : (d + 1) * count]
        part = pl.ds(t * count, count)
        copy = pltpu.make_async_copy(fine.at[:, part], out.at[:, part], sems.at[t])
        copy.start()
        copies.append(copy)
    for copy in copies:
        copy.wait()


def body(frame_one, frame_two, enc_weight, mask_weight):
    rows, cols = frame_one.shape[0], frame_one.shape[1]
    cells = rows * cols
    n2, n1, few, tall = 3 * rows + 2, rows + 4, rows + 2, 3 * rows
    singles = -(-(n1 + n2) // BC) * BC
    slots = n1 + singles // BC
    lats, lons = lax.axis_size("lat"), lax.axis_size("lon")
    far_lat = pair_perm(lats, 1, False)
    near_lat = pair_perm(lats, 0, False)
    low_lat = pair_perm(lats, 0, False, 2)
    high_lat = pair_perm(lats, 2, False, 2)
    far_lon = pair_perm(lons, 1, True)
    chips = [[i, i + 1] for i in range(0, lons, 2)]

    def array(*shape, dtype=BF16):
        return jax.ShapeDtypeStruct(shape, dtype)

    tile = array(rows, cols, CH)
    m_a, m_b, m_c, m_d, one = pl.pallas_call(
        functools.partial(edge_kernel, rows, cols),
        out_shape=(array(few, cols, CH),) * 2 + (array(1, cols, CH),) * 2 + (tile,),
        in_specs=[pl.BlockSpec(memory_space=pltpu.MemorySpace.HBM)] * 2,
        out_specs=(VMEM,) * 5,
        scratch_shapes=[pltpu.SemaphoreType.DMA((2,))],
        compiler_params=params(8),
        name="edges",
    )(
        pltpu.with_memory_space_constraint(frame_one, pltpu.MemorySpace.HBM),
        pltpu.with_memory_space_constraint(frame_two, pltpu.MemorySpace.HBM),
    )
    row_a = lax.ppermute(m_a, "lat", far_lat)
    row_b = lax.ppermute(m_b, "lat", near_lat)
    row_c = lax.ppermute(m_c, "lat", high_lat)
    row_d = lax.ppermute(m_d, "lat", low_lat)

    m_x = pl.pallas_call(
        functools.partial(pack_kernel, rows, cols),
        out_shape=array(slots, BC, CH),
        in_specs=[VMEM] * 6,
        out_specs=VMEM,
        scratch_shapes=[
            pltpu.VMEM((n1, cols, CH), BF16),
            pltpu.VMEM((n2, cols, CH), BF16),
            pltpu.VMEM((singles, CH), F32),
        ],
        compiler_params=params(16),
        name="pack",
    )(one, m_b, row_a, row_b, row_c, row_d)
    col_x = lax.ppermute(m_x, "lon", far_lon)

    weight = enc_weight.reshape(9 * CH, CH)
    few_pad = -(-few // BR) * BR
    own_two, own_one, ends_two, ends_one, m_in, edges = pl.pallas_call(
        functools.partial(own_kernel, rows, cols),
        out_shape=(
            array(tall, cols, CH),
            array(few, cols, CH),
            array(2, tall, CH, dtype=F32),
            array(2, few_pad, CH, dtype=F32),
            array(slots, BC, CH),
            array(2, -(-n1 // BR) * BR, CH, dtype=F32),
        ),
        in_specs=[VMEM] * 7,
        out_specs=(VMEM,) * 6,
        scratch_shapes=[
            pltpu.VMEM((n2, cols + 2 * BR, CH), F32),
            pltpu.VMEM((n1, cols + 2 * BR, CH), F32),
            pltpu.VMEM((3, n2, cols, CH), BF16),
            pltpu.VMEM((3, n1, cols, CH), BF16),
            pltpu.VMEM((singles, CH), F32),
        ],
        compiler_params=params(24),
        cost_estimate=pl.CostEstimate(
            flops=2 * 9 * CH * CH * cols * (tall + few), bytes_accessed=4 << 20, transcendentals=0
        ),
        name="encode_own",
    )(one, m_b, row_a, row_b, row_c, row_d, weight)

    col_in = lax.all_gather(m_in, "lon", axis_index_groups=chips)
    side_scratch = [
        pltpu.VMEM((n1, BC + 2 * BR, CH), F32),
        pltpu.VMEM((3, n1, BC, CH), BF16),
    ]
    strip_in, two_in, first_in, order = pl.pallas_call(
        functools.partial(strip_kernel, rows, cols),
        out_shape=(
            array(few, BC, CH),
            array(tall, BC, CH),
            array(few, BC, CH),
            array(UP * cols, UP * cols),
        ),
        in_specs=[VMEM] * 7,
        out_specs=(VMEM,) * 4,
        scratch_shapes=side_scratch,
        compiler_params=params(16),
        cost_estimate=pl.CostEstimate(
            flops=2 * 9 * CH * CH * BC * few, bytes_accessed=4 << 20, transcendentals=0
        ),
        name="strip",
    )(own_two, own_one, ends_two, ends_one, edges, col_in, weight)

    width = -(-few * cols // 128) * 128
    sums, enc_one = pl.pallas_call(
        functools.partial(score_kernel, rows, cols),
        out_shape=(array(8, width, dtype=F32), array(few, cols, CH)),
        in_specs=[VMEM] * 10,
        out_specs=(VMEM, VMEM),
        scratch_shapes=side_scratch
        + [pltpu.VMEM((tall, cols, CH), BF16), pltpu.VMEM((few, cols, CH), BF16)],
        compiler_params=params(20),
        name="score",
    )(own_two, own_one, ends_two, ends_one, edges, strip_in, two_in, first_in, col_x, weight)
    sums_far = lax.ppermute(sums, "lon", far_lon)

    wt = mask_weight.reshape(CH, 9, UP, UP).transpose(1, 3, 2, 0).reshape(9 * UP * UP, CH)
    mix, inverse, sums_too = pl.pallas_call(
        functools.partial(mix_kernel, rows, cells),
        out_shape=(
            array(9, UP, UP, cells, dtype=F32),
            array(UP, UP, cells, dtype=F32),
            array(8, width, dtype=F32),
        ),
        in_specs=[VMEM] * 3,
        out_specs=(VMEM,) * 3,
        compiler_params=params(16),
        cost_estimate=pl.CostEstimate(
            flops=2 * 576 * CH * cells, bytes_accessed=4 * 576 * cells, transcendentals=576 * cells
        ),
        name="mix",
    )(enc_one, wt, sums)
    sums_in = lax.all_gather(sums_too, "lon", axis_index_groups=chips)
    return pl.pallas_call(
        functools.partial(up_kernel, rows, cols),
        out_shape=array(2, rows * UP, cols * UP, dtype=F32),
        in_specs=[VMEM] * 6,
        out_specs=pl.BlockSpec(memory_space=pl.ANY),
        scratch_shapes=[
            pltpu.VMEM((2, rows * UP, cols * UP), F32),
            pltpu.SemaphoreType.DMA((cells // 128,)),
        ],
        compiler_params=params(16),
        name="upsample",
    )(sums, sums_far, sums_in, mix, inverse, order)


def solution(mesh):
    in_specs = (P("lat", "lon", None), P("lat", "lon", None), P(), P())
    return jax.shard_map(
        body, mesh=mesh, in_specs=in_specs, out_specs=P(None, "lat", "lon"), check_vma=False
    )
```

```python
import functools
import math

import jax
import jax.numpy as jnp
from jax import lax
from jax.experimental import pallas as pl
from jax.experimental.pallas import tpu as pltpu
from jax.sharding import PartitionSpec as P

CH = 256
BR = 8
BC = 16
UP = 8
F32 = jnp.float32
BF16 = jnp.bfloat16
VMEM = pl.BlockSpec(memory_space=pltpu.VMEM)


def params(mib):
    return pltpu.CompilerParams(vmem_limit_bytes=mib * 1024 * 1024)


def pair_perm(size, first, wrap, apart=1):
    out = []
    for i in range(size):
        if (i - first) % (2 * apart) >= apart:
            continue
        j = i + apart
        if j >= size:
            if not wrap:
                continue
            j -= size
        out += [(i, j), (j, i)]
    return out


def edge_kernel(rows, cols, f1, f2, m_a, m_b, m_c, m_d, g1, sems):
    band = lax.axis_index("lat")
    odd = band % 2
    upper = band % 4 // 2
    second = pltpu.make_async_copy(f2, m_a.at[pl.ds(0, rows)], sems.at[0])
    first = pltpu.make_async_copy(f1, g1, sems.at[1])
    second.start()
    first.start()
    second.wait()
    m_b[0:rows] = m_a[0:rows]
    for msg, low in ((m_c, upper), (m_d, 1 - upper)):
        msg[...] = m_a[pl.ds(low * (rows - 1), 1)]
    first.wait()
    for msg, low in ((m_a, odd), (m_b, 1 - odd)):
        msg[rows : rows + 2] = g1[pl.ds(low * (rows - 2), 2)]


def by_parity(lat_run, ra, rb, rc, rd):
    band = lax.axis_index("lat")
    for odd in (0, 1):
        for upper in (0, 1):

            @pl.when((band % 2 == odd) & (band % 4 // 2 == upper))
            def _():
                pair = (rb, ra) if odd else (ra, rb)
                lat_run(*pair, *((rd, rc) if upper else (rc, rd)))


def edge(msg, main_cols, extra, rim, col):
    n1, n2 = main_cols.shape[0], rim.shape[0]
    msg[0:n1] = main_cols
    col[0:n1] = extra
    col[n1 : n1 + n2] = rim
    msg[n1:] = col[...].astype(BF16).reshape(-1, BC, CH)


def edge_places(cols, right):
    return (cols - BC, cols - BC - 1, cols - 1) if right else (0, BC, 0)


def pack_kernel(rows, cols, f1, f2, ra, rb, rc, rd, m_x, ext1, ext2, col):
    lon_odd = lax.axis_index("lon") % 2
    n2 = 3 * rows + 2
    n1 = rows + 4

    def halo(north, south, north_far, south_far):
        ext2[0:1] = north_far[...]
        ext2[1 : 1 + rows] = north[0:rows]
        ext2[1 + 2 * rows : 1 + 3 * rows] = south[0:rows]
        ext2[n2 - 1 : n2] = south_far[...]
        ext1[0:2] = north[rows : rows + 2]
        ext1[n1 - 2 : n1] = south[rows : rows + 2]

    ext2[1 + rows : 1 + 2 * rows] = f2[0:rows]
    ext1[2 : 2 + rows] = f1[...]
    by_parity(halo, ra, rb, rc, rd)

    def column(frame, at):
        base = at // BC * BC
        return frame[:, base : base + BC].astype(F32)[:, at - base, :]

    for odd in (0, 1):

        @pl.when(lon_odd == odd)
        def _():
            main, extra, one = edge_places(cols, odd == 1)
            edge(m_x, ext1[:, main : main + BC], column(ext1, extra), column(ext2, one), col)


def conv(x, w, row, count, width):
    lhs = jnp.concatenate(
        [
            x[b, row + a : row + a + count].reshape(count * width, CH)
            for a in range(3)
            for b in range(3)
        ],
        axis=1,
    )
    return jnp.dot(lhs, w[...], preferred_element_type=F32)


def own_kernel(
    rows, cols, f1, f2, ra, rb, rc, rd, w, e2, e1, ends2, ends1, m_in, edges, s2, s1, x2, x1, col
):
    lon_odd = lax.axis_index("lon") % 2
    n2 = 3 * rows + 2
    n1 = rows + 4
    own = slice(BR, BR + cols)

    def halo(north, south, north_far, south_far):
        s2[0:1, own] = north_far[...].astype(F32)
        s2[1 : 1 + rows, own] = north[0:rows].astype(F32)
        s2[1 + 2 * rows : 1 + 3 * rows, own] = south[0:rows].astype(F32)
        s2[n2 - 1 : n2, own] = south_far[...].astype(F32)
        s1[0:2, own] = north[rows : rows + 2].astype(F32)
        s1[n1 - 2 : n1, own] = south[rows : rows + 2].astype(F32)

    s2[1 + rows : 1 + 2 * rows, own] = f2[0:rows].astype(F32)
    s1[2 : 2 + rows, own] = f1[...].astype(F32)
    by_parity(halo, ra, rb, rc, rd)
    for s in (s2, s1):
        s[:, 0:BR] = jnp.zeros((s.shape[0], BR, CH), F32)
        s[:, BR + cols :] = jnp.zeros((s.shape[0], BR, CH), F32)
    for b in range(3):
        x2[b] = s2[:, BR - 1 + b : BR - 1 + b + cols].astype(BF16)
        x1[b] = s1[:, BR - 1 + b : BR - 1 + b + cols].astype(BF16)

    def run(x, out, ends, total):
        for r in range(0, total, 2 * BR):
            step = min(2 * BR, total - r)
            acc = conv(x, w, r, step, cols).reshape(step, cols, CH)
            out[r : r + step] = acc.astype(BF16)
            ends[0, r : r + step] = acc[:, 0, :]
            ends[1, r : r + step] = acc[:, cols - 1, :]

    run(x1, e1, ends1, rows + 2)
    run(x2, e2, ends2, 3 * rows)
    edges[0, 0:n1] = s1[:, BR, :]
    edges[1, 0:n1] = s1[:, BR + cols - 1, :]
    for odd in (0, 1):

        @pl.when(lon_odd == odd)
        def _():
            main, extra, one = edge_places(cols, odd == 0)
            edge(m_in, x1[1, :, main : main + BC], s1[:, BR + extra, :], s2[:, BR + one, :], col)


def finish_side(rows, cols, side, msg, w, o2, o1, ends2, ends1, edges, ext, xs, put):
    n2 = 3 * rows + 2
    n1 = rows + 4
    few, tall = rows + 2, 3 * rows
    singles = msg[n1:].astype(F32).reshape(-1, CH)
    extra = singles[0:n1]
    rim = singles[n1 : n1 + n2].astype(BF16)
    inner = edges[side, 0:n1]
    ext[:, BR : BR + BC] = msg[0:n1].astype(F32)
    ext[:, BR - 1 : BR] = (inner if side else extra)[:, None, :]
    ext[:, BR + BC : BR + BC + 1] = (extra if side else inner)[:, None, :]
    for b in range(3):
        xs[b] = ext[:, BR - 1 + b : BR - 1 + b + BC].astype(BF16)
    strip = conv(xs, w, 0, few, BC).astype(BF16).reshape(few, BC, CH)
    near = ext[:, BR : BR + 1] if side else ext[:, BR + BC - 1 : BR + BC]
    near = near[:, 0, :].astype(BF16)
    taps = jnp.concatenate(
        [w[(3 * a + 2 * side) * CH : (3 * a + 2 * side + 1) * CH] for a in range(3)], axis=0
    )
    lhs = jnp.concatenate(
        [jnp.concatenate([rim[a : a + tall], near[a : a + few]], axis=0) for a in range(3)],
        axis=1,
    )
    more = jnp.dot(lhs, taps, preferred_element_type=F32)
    hit = lax.broadcasted_iota(jnp.int32, (1, BC, CH), 1) == (BC - 1 if side else 0)
    lo = cols - BC if side else 0
    full = ends2[side, 0:tall] + more[0:tall]
    two = jnp.where(hit, full[:, None, :], o2[:, lo : lo + BC].astype(F32)).astype(BF16)
    full = ends1[side, 0:few] + more[tall : tall + few]
    first = jnp.where(hit, full[:, None, :], o1[:, lo : lo + BC].astype(F32)).astype(BF16)
    put(side, strip, two, first)


def strip_kernel(
    rows, cols, o2, o1, ends2, ends1, edges, chip, w, strip, two, first, order, ext, xs
):
    src = lax.broadcasted_iota(jnp.int32, order.shape, 0)
    dst = lax.broadcasted_iota(jnp.int32, order.shape, 1)
    to = (src % cols) * UP + src // cols
    order[...] = jnp.where(dst == to, 1.0, 0.0).astype(BF16)
    lon_odd = lax.axis_index("lon") % 2
    msg = chip.at[1 - lon_odd]

    def put(side, *values):
        for ref, value in zip((strip, two, first), values):
            ref[...] = value

    for odd in (0, 1):

        @pl.when(lon_odd == odd)
        def _():
            finish_side(rows, cols, 1 - odd, msg, w, o2, o1, ends2, ends1, edges, ext, xs, put)


def score_kernel(
    rows, cols, o2, o1, ends2, ends1, edges, strip_in, two_in, first_in, c_x, w,
    sums, enc_one, ext, xs, e2, beside,
):
    lat = lax.axis_index("lat")
    lon_odd = lax.axis_index("lon") % 2

    def put(side, strip, two, first):
        lo = cols - BC if side else 0
        e2[:, lo : lo + BC] = two
        enc_one[:, lo : lo + BC] = first
        lo = 0 if side else cols - BC
        beside[:, lo : lo + BC] = strip

    for odd in (0, 1):

        @pl.when(lon_odd == odd)
        def _():
            put(1 - odd, strip_in[...], two_in[...], first_in[...])
            finish_side(rows, cols, odd, c_x, w, o2, o1, ends2, ends1, edges, ext, xs, put)

    bands = rows // BR
    last = lax.axis_size("lat") - 1
    scale = 1.0 / math.sqrt(CH)
    groups = cols // BR

    def features(ref, row, count):
        flat = ref[row : row + count].reshape(count * cols, CH).astype(F32)
        return (flat * scale).astype(BF16)

    def scores(block, query):
        keys = e2[block * BR : (block + 3) * BR].reshape(3 * BR * cols, CH)
        return lax.dot_general(
            keys, query, (((1,), (1,)), ((), ())), preferred_element_type=F32
        ).reshape(3, BR, groups, BR, query.shape[0])

    def add(total, now):
        return now if total is None else [p + e for p, e in zip(total, now)]

    def triple(pieces, by_row, sub, base):
        mass = pieces[0]
        octs = None
        for i, piece in enumerate(pieces[1:], 1):
            mass = mass + piece
            octs = piece * float(i) if octs is None else octs + piece * float(i)
        across = octs * 8.0 + mass * (sub if base is None else sub + base)
        return [jnp.sum(v, axis=0, keepdims=True) for v in (mass, by_row, across)]

    queries = BR * cols
    sub = lax.broadcasted_iota(jnp.int32, (BR, queries), 0).astype(F32)
    of_right = lax.broadcasted_iota(jnp.int32, (BR, queries), 1) % cols < BC
    base = jnp.where(of_right, float(BC - cols), float(cols))
    for g in range(bands):
        query_own = features(enc_one, 1 + g * BR, BR)
        query_side = features(beside, 1 + g * BR, BR)
        acc = None
        of_own = scores(g + 1, query_own)
        of_side = scores(g + 1, query_side)
        for kb in range(3):
            mine, other = of_own[kb], of_side[kb]
            part = None
            for kr in range(BR):
                row = float((kb - 1) * BR + kr)
                own = [jnp.exp(mine[kr, i]) for i in range(4)]
                side = [
                    jnp.exp(jnp.where(of_right, other[kr, 2 + i], other[kr, i])) for i in range(2)
                ]
                now = own + [row * ((own[0] + own[1]) + (own[2] + own[3]))]
                now += side + [row * (side[0] + side[1])]
                part = add(part, now)
            if kb == 0 and g == 0:
                part = [jnp.where(lat > 0, p, 0.0) for p in part]
            elif kb == 2 and g == bands - 1:
                part = [jnp.where(lat < last, p, 0.0) for p in part]
            acc = add(acc, part)
        values = triple(acc[0:4], acc[4], sub, None) + triple(acc[5:7], acc[7], sub, base)
        values += [jnp.zeros((2, queries), F32)]
        sums[:, cols + g * queries : cols + (g + 1) * queries] = jnp.concatenate(values, axis=0)

    quarter = cols
    lanes = 4 * quarter
    sub = lax.broadcasted_iota(jnp.int32, (BR, lanes), 0).astype(F32)
    lane = lax.broadcasted_iota(jnp.int32, (BR, lanes), 1)
    below = lane >= 2 * quarter
    spot = lane % (2 * quarter)
    is_own = spot < quarter
    of_right = (spot >= quarter) & (spot < quarter + BC)
    base = jnp.where(is_own, 0.0, jnp.where(of_right, float(BC - cols), float(cols)))
    query = jnp.concatenate(
        [features(r, at, 1) for at in (0, rows + 1) for r in (enc_one, beside)], axis=0
    )
    acc = None
    all_over = scores(0, query)
    all_under = scores(bands + 1, query)
    for kb in range(3):
        over, under = all_over[kb], all_under[kb]
        for kr in range(BR):
            row = float((kb - 1) * BR + kr)
            both = [jnp.where(below, under[kr, i], over[kr, i]) for i in range(4)]
            now = [jnp.exp(jnp.where(of_right, both[2 + i], both[i])) for i in range(2)]
            now += [jnp.exp(both[i]) for i in range(2, 4)]
            now += [row * (now[0] + now[1]), row * (now[2] + now[3])]
            acc = add(acc, now)
    acc[2], acc[3], acc[5] = (jnp.where(is_own, acc[i], 0.0) for i in (2, 3, 5))
    values = triple(acc[0:4], acc[4] + acc[5], sub, base)
    for k, at in enumerate((0, cols + rows * cols)):
        for m in range(2):
            lo = (2 * k + m) * quarter
            sums[3 * m : 3 * m + 3, at : at + cols] = jnp.concatenate(
                [v[:, lo : lo + quarter] for v in values], axis=0
            )
        sums[6:8, at : at + cols] = jnp.zeros((2, cols), F32)


def mix_kernel(rows, cells, enc_one, wt, sums, mix, total, passed):
    passed[...] = sums[...]
    feats = enc_one[1 : 1 + rows].reshape(cells, CH)
    step = 256
    count = UP * UP
    for c0 in range(0, cells, step):
        logits = lax.dot_general(
            wt[...], feats[c0 : c0 + step], (((1,), (1,)), ((), ())), preferred_element_type=F32
        )
        mass = None
        for n in range(9):
            expo = jnp.exp(logits[n * count : (n + 1) * count]).reshape(UP, UP, step)
            mix[n, :, :, c0 : c0 + step] = expo
            mass = expo if mass is None else mass + expo
        total[:, :, c0 : c0 + step] = 1.0 / mass


def up_kernel(rows, cols, mine, far, chip, mix, inverse, order_ref, out, fine, sems):
    lat = lax.axis_index("lat")
    last = lax.axis_size("lat") - 1
    lon_odd = lax.axis_index("lon") % 2
    cells = rows * cols
    width = mine.shape[1]
    lane = lax.broadcasted_iota(jnp.int32, (1, width), 1)
    column = lane % cols
    row = ((lane // cols + BR - 1) % BR).astype(F32)
    outside = ((lane < cols) & (lat == 0)) | ((lane >= cols + cells) & (lat == last))
    partner = chip[1 - lon_odd]
    is_odd = jnp.broadcast_to(lon_odd == 1, partner.shape)
    left = jnp.where(is_odd, partner, far[...])
    right = jnp.where(is_odd, far[...], partner)
    own = mine[...]

    def flow(total):
        both = jnp.concatenate(
            [total[1:2] / total[0:1] - row, total[2:3] / total[0:1] - column.astype(F32)], axis=0
        )
        return jnp.where(outside, 0.0, both * float(UP))

    mid = flow(own[0:3] + jnp.where(column < BC, left[3:6], right[3:6]))
    west = flow(left[0:3] + own[3:6])
    east = flow(right[0:3] + own[3:6])
    west = jnp.where(
        column == 0, pltpu.roll(west, width - (cols - 1), 1), pltpu.roll(mid, 1, 1)
    )
    east = jnp.where(
        column == cols - 1, pltpu.roll(east, cols - 1, 1), pltpu.roll(mid, width - 1, 1)
    )
    shifted = []
    for a in range(3):
        for field in (west, mid, east):
            moved = field if a == 0 else pltpu.roll(field, width - a * cols, 1)
            shifted.append(moved[:, 0:cells])
    order = order_ref[...]
    tile = 128
    group = tile // cols
    lane = lax.broadcasted_iota(jnp.int32, (UP, tile), 1)
    bits = []
    span = 1
    while span < group:
        bits.append((span, (lane // (span * cols)) % 2 == 1))
        span *= 2
    count = group * UP
    copies = []
    for t in range(cells // tile):
        here = slice(t * tile, (t + 1) * tile)
        flows = [
            [jnp.broadcast_to(v[d : d + 1, here], (UP, tile)) for v in shifted] for d in range(2)
        ]
        lanes_of = [[[None] * (UP // group) for _ in range(group)] for _ in range(2)]
        for u in range(UP // group):
            blocks = [[], []]
            for k in range(group):
                at = u * group + k
                scale = inverse[at, :, here]
                weights = [mix[n, at, :, here] for n in range(9)]
                for d in range(2):
                    acc = weights[0] * flows[d][0]
                    for n in range(1, 9):
                        acc = acc + weights[n] * flows[d][n]
                    blocks[d].append(acc * scale)
            for d in range(2):
                block = blocks[d]
                for span, high in bits:
                    shift = span * cols
                    done = list(block)
                    for k in range(group):
                        if k & span:
                            continue
                        lo_v, hi_v = block[k], block[k | span]
                        done[k] = jnp.where(high, pltpu.roll(hi_v, shift, 1), lo_v)
                        done[k | span] = jnp.where(
                            high, hi_v, pltpu.roll(lo_v, tile - shift, 1)
                        )
                    block = done
                for k in range(group):
                    lanes_of[d][k][u] = block[k]
        value = jnp.concatenate(
            [jnp.concatenate(v, axis=1) for d in range(2) for v in lanes_of[d]], axis=0
        )
        high_part = value.astype(BF16)
        low_part = (value - high_part.astype(F32)).astype(BF16)
        both = jnp.dot(
            jnp.concatenate([high_part, low_part], axis=0), order, preferred_element_type=F32
        )
        both = both[0 : 2 * count] + both[2 * count :]
        for d in range(2):
            fine[d, t * count : (t + 1) * count] = both[d * count : (d + 1) * count]
        part = pl.ds(t * count, count)
        copy = pltpu.make_async_copy(fine.at[:, part], out.at[:, part], sems.at[t])
        copy.start()
        copies.append(copy)
    for copy in copies:
        copy.wait()


def body(frame_one, frame_two, enc_weight, mask_weight):
    rows, cols = frame_one.shape[0], frame_one.shape[1]
    cells = rows * cols
    n2, n1, few, tall = 3 * rows + 2, rows + 4, rows + 2, 3 * rows
    singles = -(-(n1 + n2) // BC) * BC
    slots = n1 + singles // BC
    lats, lons = lax.axis_size("lat"), lax.axis_size("lon")
    far_lat = pair_perm(lats, 1, False)
    near_lat = pair_perm(lats, 0, False)
    low_lat = pair_perm(lats, 0, False, 2)
    high_lat = pair_perm(lats, 2, False, 2)
    far_lon = pair_perm(lons, 1, True)
    chips = [[i, i + 1] for i in range(0, lons, 2)]

    def array(*shape, dtype=BF16):
        return jax.ShapeDtypeStruct(shape, dtype)

    tile = array(rows, cols, CH)
    m_a, m_b, m_c, m_d, one = pl.pallas_call(
        functools.partial(edge_kernel, rows, cols),
        out_shape=(array(few, cols, CH),) * 2 + (array(1, cols, CH),) * 2 + (tile,),
        in_specs=[pl.BlockSpec(memory_space=pltpu.MemorySpace.HBM)] * 2,
        out_specs=(VMEM,) * 5,
        scratch_shapes=[pltpu.SemaphoreType.DMA((2,))],
        compiler_params=params(8),
        name="edges",
    )(
        pltpu.with_memory_space_constraint(frame_one, pltpu.MemorySpace.HBM),
        pltpu.with_memory_space_constraint(frame_two, pltpu.MemorySpace.HBM),
    )
    row_a = lax.ppermute(m_a, "lat", far_lat)
    row_b = lax.ppermute(m_b, "lat", near_lat)
    row_c = lax.ppermute(m_c, "lat", high_lat)
    row_d = lax.ppermute(m_d, "lat", low_lat)

    m_x = pl.pallas_call(
        functools.partial(pack_kernel, rows, cols),
        out_shape=array(slots, BC, CH),
        in_specs=[VMEM] * 6,
        out_specs=VMEM,
        scratch_shapes=[
            pltpu.VMEM((n1, cols, CH), BF16),
            pltpu.VMEM((n2, cols, CH), BF16),
            pltpu.VMEM((singles, CH), F32),
        ],
        compiler_params=params(16),
        name="pack",
    )(one, m_b, row_a, row_b, row_c, row_d)
    col_x = lax.ppermute(m_x, "lon", far_lon)

    weight = enc_weight.reshape(9 * CH, CH)
    few_pad = -(-few // BR) * BR
    own_two, own_one, ends_two, ends_one, m_in, edges = pl.pallas_call(
        functools.partial(own_kernel, rows, cols),
        out_shape=(
            array(tall, cols, CH),
            array(few, cols, CH),
            array(2, tall, CH, dtype=F32),
            array(2, few_pad, CH, dtype=F32),
            array(slots, BC, CH),
            array(2, -(-n1 // BR) * BR, CH, dtype=F32),
        ),
        in_specs=[VMEM] * 7,
        out_specs=(VMEM,) * 6,
        scratch_shapes=[
            pltpu.VMEM((n2, cols + 2 * BR, CH), F32),
            pltpu.VMEM((n1, cols + 2 * BR, CH), F32),
            pltpu.VMEM((3, n2, cols, CH), BF16),
            pltpu.VMEM((3, n1, cols, CH), BF16),
            pltpu.VMEM((singles, CH), F32),
        ],
        compiler_params=params(24),
        cost_estimate=pl.CostEstimate(
            flops=2 * 9 * CH * CH * cols * (tall + few), bytes_accessed=4 << 20, transcendentals=0
        ),
        name="encode_own",
    )(one, m_b, row_a, row_b, row_c, row_d, weight)

    col_in = lax.all_gather(m_in, "lon", axis_index_groups=chips)
    side_scratch = [
        pltpu.VMEM((n1, BC + 2 * BR, CH), F32),
        pltpu.VMEM((3, n1, BC, CH), BF16),
    ]
    strip_in, two_in, first_in, order = pl.pallas_call(
        functools.partial(strip_kernel, rows, cols),
        out_shape=(
            array(few, BC, CH),
            array(tall, BC, CH),
            array(few, BC, CH),
            array(UP * cols, UP * cols),
        ),
        in_specs=[VMEM] * 7,
        out_specs=(VMEM,) * 4,
        scratch_shapes=side_scratch,
        compiler_params=params(16),
        cost_estimate=pl.CostEstimate(
            flops=2 * 9 * CH * CH * BC * few, bytes_accessed=4 << 20, transcendentals=0
        ),
        name="strip",
    )(own_two, own_one, ends_two, ends_one, edges, col_in, weight)

    width = -(-few * cols // 128) * 128
    sums, enc_one = pl.pallas_call(
        functools.partial(score_kernel, rows, cols),
        out_shape=(array(8, width, dtype=F32), array(few, cols, CH)),
        in_specs=[VMEM] * 10,
        out_specs=(VMEM, VMEM),
        scratch_shapes=side_scratch
        + [pltpu.VMEM((tall, cols, CH), BF16), pltpu.VMEM((few, cols, CH), BF16)],
        compiler_params=params(20),
        name="score",
    )(own_two, own_one, ends_two, ends_one, edges, strip_in, two_in, first_in, col_x, weight)
    sums_far = lax.ppermute(sums, "lon", far_lon)

    wt = mask_weight.reshape(CH, 9, UP, UP).transpose(1, 3, 2, 0).reshape(9 * UP * UP, CH)
    mix, inverse, sums_too = pl.pallas_call(
        functools.partial(mix_kernel, rows, cells),
        out_shape=(
            array(9, UP, UP, cells, dtype=F32),
            array(UP, UP, cells, dtype=F32),
            array(8, width, dtype=F32),
        ),
        in_specs=[VMEM] * 3,
        out_specs=(VMEM,) * 3,
        compiler_params=params(16),
        cost_estimate=pl.CostEstimate(
            flops=2 * 576 * CH * cells, bytes_accessed=4 * 576 * cells, transcendentals=576 * cells
        ),
        name="mix",
    )(enc_one, wt, sums)
    sums_in = lax.all_gather(sums_too, "lon", axis_index_groups=chips)
    return pl.pallas_call(
        functools.partial(up_kernel, rows, cols),
        out_shape=array(2, rows * UP, cols * UP, dtype=F32),
        in_specs=[VMEM] * 6,
        out_specs=pl.BlockSpec(memory_space=pl.ANY),
        scratch_shapes=[
            pltpu.VMEM((2, rows * UP, cols * UP), F32),
            pltpu.SemaphoreType.DMA((cells // 128,)),
        ],
        compiler_params=params(16),
        name="upsample",
    )(sums, sums_far, sums_in, mix, inverse, order)


def solution(mesh):
    in_specs = (P("lat", "lon", None), P("lat", "lon", None), P(), P())
    return jax.shard_map(
        body, mesh=mesh, in_specs=in_specs, out_specs=P(None, "lat", "lon"), check_vma=False
    )
```
